32 devices in a mesh: replica: 4 (over y, x), shard: 8 (over z, core).
Axes of the slice: x: 2, y: 2, z: 4, core: 2. Of those that a mesh axis runs over, the one named last changes fastest.
Arguments:
- queries: bfloat16 [16384, 2048], P(('replica', 'shard')), may hold values from -20 to 20
- keys: bfloat16 [16384, 1024], P(('replica', 'shard')), may hold values from -20 to 20
- values: bfloat16 [16384, 1024], P(('replica', 'shard')), may hold values from -6 to 6
- segments: int32 [32, 512], P(('replica', 'shard')), may hold values from 0 to 7, never falling along the last dimension, each value on 1 to 384 neighbouring positions
- out_weight: bfloat16 [2048, 4608], P('shard'), may hold values from -0.125 to 0.125
- upstream: bfloat16 [16384, 4608], P(('replica', 'shard')), may hold values from -6 to 6
- first_moment: float32 [2048, 4608], P('shard'), may hold values from -0.0034179688 to 0.0034179688
- second_moment: float32 [2048, 4608], P('shard'), may hold values from 1.2207032e-07 to 3.0517579e-06
Outputs:
- grad_queries: bfloat16 [16384, 2048], P(('replica', 'shard'))
- grad_keys: bfloat16 [16384, 1024], P(('replica', 'shard'))
- grad_values: bfloat16 [16384, 1024], P(('replica', 'shard'))
- adam_step: float32 [2048, 4608], P('shard')
The draws below stay inside these ranges and needn't reach their ends.
Inputs may be any that keep to these rules, and one draw needn't show every extreme that they name: `segments`: within each block the document numbers never fall; every document holds 1 to 384 tokens.
All inputs are finite; a program needn't handle non-finite values.
Results may differ from the reference program's by a relative error of at most 0.014.
Values may be sent and summed in bfloat16 or wider, within the bound.
No kernel may reach another device: no remote copies, remote signals or barrier semaphores. Data moves between devices by JAX's collectives and lax.ppermute only.
A program may use at most 192 MiB of HBM per device.

```python
import math
import jax
import jax.numpy as jnp
import numpy as np
from jax import lax

D = 4608
HEADS = 16
KV_HEADS = 8
DH = 128
TOK_DEV = 512
HQ = 2048
KVW = 1024
GROUPS = 32
TOKENS_ALL = 16384


def scaled_rows(key, rows):
    first, second = jax.random.split(key, 2)
    scale = jnp.exp(jax.random.uniform(first, (rows, 1), jnp.float32, math.log(0.3), math.log(3.0)))
    return (second, scale)


def draw_queries(key, part):
    key = jax.random.fold_in(key, 11)
    second, scale = scaled_rows(key, TOKENS_ALL)
    base = jax.random.normal(second, (TOKENS_ALL, HQ), jnp.float32)
    return (scale * base).astype(jnp.bfloat16)


def draw_keys(key, part):
    key = jax.random.fold_in(key, 23)
    second, scale = scaled_rows(key, TOKENS_ALL)
    base = jax.random.normal(second, (TOKENS_ALL, KVW), jnp.float32)
    return (scale * base).astype(jnp.bfloat16)


def with_spikes(entries, own_key, source, target, parts, factor):
    def block_of(dim):
        return (jnp.arange(entries.shape[dim]) // (entries.shape[dim] // parts)).reshape((-1,) + (1,) * (entries.ndim - 1 - dim))

    one_side = jax.random.permutation(own_key, parts)[block_of(target)]
    far = (block_of(target) + parts // 2) % parts
    return jnp.where((block_of(source) == one_side) | (block_of(source) == far), factor * entries, entries)


def block_levels(rng, dims, cuts, smallest, top_value):
    loudness = 1.0
    for axis_at, parts in cuts:
        draws = jax.random.uniform(jax.random.fold_in(jax.random.fold_in(rng, 6), axis_at), (parts,), jnp.float32, smallest / len(cuts), top_value / len(cuts))
        loudness = loudness * jnp.repeat(jnp.exp(draws), dims[axis_at] // parts).reshape((-1,) + (1,) * (len(dims) - 1 - axis_at))
    return loudness


def length_profile(count, total, bound, slope):
    portions = [(1 << 20) // math.isqrt(grade ** slope) + 1 for grade in range(2, count + 1)]
    surplus, holding = total - bound - (count - 1), [1] * (count - 1)
    while surplus > 0:
        candidates = [i for i in range(count - 1) if holding[i] < bound]
        pool, budget = sum([portions[i] for i in candidates]), surplus
        for i in candidates:
            addition = min(bound - holding[i], max(1, budget * portions[i] // pool), surplus)
            holding[i] = holding[i] + addition
            surplus = surplus - addition
    return np.array([bound] + holding)


def uneven(key, count, total, most, slope):
    if count == 2:
        one = jax.random.randint(key, (), max(1, total - most), min(most, total - 1) + 1)
        return jnp.stack([one, total - one])
    lengths = jnp.asarray(length_profile(count, total, most, slope), jnp.int32)
    couples = (count - 1) // 2
    source_of, sink = lengths[1:1 + 2 * couples:2], lengths[2:2 + 2 * couples:2]
    slack = jnp.minimum(source_of - 1, most - sink)
    moved = jax.random.randint(jax.random.fold_in(key, 1), (couples,), 0, 1 << 20) % (slack + 1)
    lengths = lengths.at[1:1 + 2 * couples:2].set(source_of - moved).at[2:2 + 2 * couples:2].set(sink + moved)
    return lengths[jax.random.permutation(jax.random.fold_in(key, 2), count)]


def bell_draw(stream_key, dims, width, most, cuts=(), dtype=jnp.bfloat16):
    factor_of = block_levels(stream_key, dims, cuts, -0.22, 0.18) if cuts else 1.0
    entries = jax.random.normal(stream_key, dims, jnp.float32) * width * factor_of
    return jnp.minimum(jnp.maximum(entries, -most), most).astype(dtype)


def bell_draw_with(own_key, extent, deviation, most, cuts, heavy, dtype=jnp.bfloat16):
    result = deviation * jax.random.normal(own_key, extent, jnp.float32)
    if cuts:
        result = result * block_levels(own_key, extent, cuts, -0.22, 0.18)
    return jnp.clip(with_spikes(result, jax.random.fold_in(own_key, 3), *heavy), -most, most).astype(dtype)


def setup_inputs(seed: int = 0) -> dict:
    key_list = jax.random.split(jax.random.key(seed), 9)
    queries = draw_queries(jax.random.fold_in(key_list[8], 71), 0)
    keys = draw_keys(jax.random.fold_in(key_list[8], 71), 0)
    values = bell_draw_with(key_list[2], (TOKENS_ALL, KVW), 1.0, 6.0, ((0, 32),), (0, 1, 32, 2.75))
    segments = jax.vmap(lambda own: jnp.searchsorted(jnp.cumsum(uneven(own, max(2, TOK_DEV // 64), TOK_DEV, 3 * TOK_DEV // 4, 0)), jnp.arange(TOK_DEV), side="right"))(jax.random.split(key_list[3], GROUPS)).reshape((GROUPS, TOK_DEV)).astype(jnp.int32)
    out_weight = bell_draw(key_list[4], (HQ, D), HQ ** -0.5, 0.125, ((0, 8),))
    upstream = bell_draw(key_list[5], (TOKENS_ALL, D), 1.0, 6.0, ((0, 32),))
    first_moment = bell_draw(key_list[6], (HQ, D), (0.03 * TOKENS_ALL ** -0.5), 0.0034179688, ((0, 8),), jnp.float32)
    second_moment = jnp.clip(jnp.exp(math.log(3.051757857974735e-06) - 3.218876 * jax.random.uniform(key_list[7], (HQ, D), jnp.float32) ** block_levels(key_list[7], (HQ, D), ((0, 8),), -0.2, 0.2)), 1.2207031829802872e-07, 3.051757857974735e-06)
    return dict(queries=queries, keys=keys, values=values, segments=segments, out_weight=out_weight, upstream=upstream, first_moment=first_moment, second_moment=second_moment)


score_scale = 1.0 / 12.0
softcap_limit = 50.0

def recompute(query_heads, key_heads, value_heads, segment_row):
    length = segment_row.shape[0]
    scores = jnp.einsum('igrd,jgd->grij', query_heads.astype(jnp.float32), key_heads.astype(jnp.float32)) * score_scale
    capped = softcap_limit * jnp.tanh(scores / softcap_limit)
    position = jnp.arange(length)
    allowed = (position[None, :] <= position[:, None]) & (segment_row[:, None] == segment_row[None, :])
    weights = jnp.where(allowed, jnp.exp(capped), jnp.zeros_like(capped))
    probs = weights / lax.optimization_barrier(jnp.sum(weights, axis=-1, keepdims=True))
    probs_low = probs.astype(jnp.bfloat16)
    context = jnp.einsum('grij,jgd->igrd', probs_low.astype(jnp.float32), value_heads.astype(jnp.float32)).astype(jnp.bfloat16)
    return (probs, capped, probs_low, context.reshape(length, -1))

def reference(queries, keys, values, segments, out_weight, upstream, first_moment, second_moment):
    groups, length = segments.shape
    repeat = HEADS // KV_HEADS
    query_all = queries.reshape(groups, length, KV_HEADS, repeat, DH)
    key_all = keys.reshape(groups, length, KV_HEADS, DH)
    value_all = values.reshape(groups, length, KV_HEADS, DH)
    upstream_all = upstream.reshape(groups, length, D)

    def step(total, block):
        query_heads, key_heads, value_heads, segment_row, grad_rows = block
        probs, capped, probs_low, context = recompute(query_heads, key_heads, value_heads, segment_row)
        grad_context = lax.dot_general(grad_rows, out_weight, (((1,), (1,)), ((), ())), preferred_element_type=jnp.float32).astype(jnp.bfloat16)
        grad_heads = grad_context.reshape(length, KV_HEADS, repeat, DH).astype(jnp.float32)
        grad_probs = jnp.einsum('igrd,jgd->grij', grad_heads, value_heads.astype(jnp.float32))
        grad_vals = jnp.einsum('grij,igrd->jgd', probs_low.astype(jnp.float32), grad_heads).astype(jnp.bfloat16)
        delta = lax.optimization_barrier(jnp.sum(probs * grad_probs, axis=-1, keepdims=True))
        grad_scores = (probs * (grad_probs - delta) * (1.0 - jnp.square(capped / softcap_limit)) * score_scale).astype(jnp.bfloat16)
        grad_query = jnp.einsum('grij,jgd->igrd', grad_scores.astype(jnp.float32), key_heads.astype(jnp.float32)).astype(jnp.bfloat16)
        grad_key = jnp.einsum('grij,igrd->jgd', grad_scores.astype(jnp.float32), query_heads.astype(jnp.float32)).astype(jnp.bfloat16)
        product = lax.dot_general(context, grad_rows, (((0,), (0,)), ((), ())), preferred_element_type=jnp.float32)
        rounded = lax.optimization_barrier(product.astype(jnp.bfloat16)).astype(jnp.float32)
        return (total + rounded, (grad_query.reshape(length, -1), grad_key.reshape(length, -1), grad_vals.reshape(length, -1)))
    total, results = lax.scan(step, jnp.zeros((HQ, D), jnp.float32), (query_all, key_all, value_all, segments, upstream_all))
    gradient = total / TOKENS_ALL
    moment_one = 0.9 * first_moment + 0.1 * gradient
    moment_two = 0.95 * second_moment + 0.05 * gradient * gradient
    adam_step = moment_one / (jnp.sqrt(moment_two) + 1e-08)
    grad_queries = results[0].reshape(TOKENS_ALL, HQ)
    grad_keys = results[1].reshape(TOKENS_ALL, KVW)
    grad_values = results[2].reshape(TOKENS_ALL, KVW)
    return (grad_queries, grad_keys, grad_values, adam_step)
```

```python
import functools

import jax
import jax.numpy as jnp
import numpy as np
from jax import lax
from jax.experimental import pallas as pl
from jax.experimental.pallas import tpu as pltpu
from jax.sharding import PartitionSpec as P

HEADS = 16
KV_HEADS = 8
DH = 128
REPEAT = HEADS // KV_HEADS

SCALE = 1.0 / 12.0
CAP = 50.0
VMEM = 40 * 1024 * 1024
F32 = jnp.float32
BF16 = jnp.bfloat16

NT = (((1,), (1,)), ((), ()))
NN = (((1,), (0,)), ((), ()))


def dot(a, b, dims):
    return lax.dot_general(a, b, dims, preferred_element_type=F32)


def call(body, grid, in_specs, out_specs, out_shape, scratch=(), aliases=None, cost=None):
    return pl.pallas_call(
        body,
        grid_spec=pltpu.PrefetchScalarGridSpec(
            num_scalar_prefetch=1,
            grid=grid,
            in_specs=in_specs,
            out_specs=out_specs,
            scratch_shapes=list(scratch),
        ),
        out_shape=out_shape,
        input_output_aliases=aliases or {},
        cost_estimate=cost,
        compiler_params=pltpu.CompilerParams(vmem_limit_bytes=VMEM),
    )


def fill_mask(mask_ref, seg_row_ref, seg_col_ref):
    length = mask_ref.shape[0]
    j = lax.broadcasted_iota(jnp.int32, (length, length), 0)
    i = lax.broadcasted_iota(jnp.int32, (length, length), 1)
    allowed = (j <= i) & (seg_col_ref[...] == seg_row_ref[...])
    mask_ref[...] = jnp.where(allowed, 1.0, 0.0).astype(F32)


def tiles_of(length):
    tile = 256
    return [(t * tile, tile, (t + 1) * tile) for t in range(length // tile)]


def softmax_tile(key, query, mask):
    cap_tanh = jnp.tanh(dot(key, query, NT) * (SCALE / CAP))
    weights = jnp.exp(cap_tanh * CAP) * mask
    inverse = 1.0 / jnp.sum(weights, axis=0, keepdims=True)
    return weights * inverse, cap_tanh


def forward_body(heads, sc_ref, q_ref, k_ref, v_ref, seg_row_ref, seg_col_ref, out_ref, mask_ref):
    @pl.when(pl.program_id(0) == 0)
    def _():
        fill_mask(mask_ref, seg_row_ref, seg_col_ref)

    value_t = v_ref[...].T
    for h in range(heads):
        for start, tile, upto in tiles_of(q_ref.shape[0]):
            probs, _ = softmax_tile(
                k_ref[:upto, :],
                q_ref[start : start + tile, h * DH : (h + 1) * DH],
                mask_ref[:upto, start : start + tile],
            )
            context = dot(value_t[:, :upto], probs.astype(BF16), NN)
            out_ref[h * DH : (h + 1) * DH, start : start + tile] = context.astype(BF16)


def forward(sc, flip, queries, keys, values, seg_row, seg_col, lay):
    length = queries.shape[0]
    per = lay.heads_shard

    def shard_of(i, sc):
        return 2 * i + (1 - sc[0] if flip else sc[0])

    def kv_of(i, sc):
        return (shard_of(i, sc) * per) // REPEAT

    pairs = lay.z * per * length * length
    return call(
        functools.partial(forward_body, per),
        (lay.z,),
        [
            pl.BlockSpec((length, per * DH), lambda i, sc: (0, shard_of(i, sc))),
            pl.BlockSpec((length, DH), lambda i, sc: (0, kv_of(i, sc))),
            pl.BlockSpec((length, DH), lambda i, sc: (0, kv_of(i, sc))),
            pl.BlockSpec((1, length), lambda i, sc: (0, 0)),
            pl.BlockSpec((length, 1), lambda i, sc: (0, 0)),
        ],
        pl.BlockSpec((per * DH, length), lambda i, sc: (i, 0)),
        jax.ShapeDtypeStruct((lay.z * per * DH, length), BF16),
        scratch=[pltpu.VMEM((length, length), F32)],
        cost=pl.CostEstimate(
            flops=4 * pairs * DH, transcendentals=2 * pairs, bytes_accessed=4 * length * HEADS * DH
        ),
    )(sc, queries, keys, values, seg_row, seg_col)


def product_body(
    half_tiles, first, last, sc_ref, c0_ref, c1_ref, u0_ref, u1_ref, sa_ref, ka_ref, sb_ref, kb_ref, acc_ref
):
    n = pl.program_id(0)
    half = acc_ref.shape[0] // 2
    acc = dot(c0_ref[...], u0_ref[...], NN) + dot(c1_ref[...], u1_ref[...], NN)
    acc_ref[...] = acc.astype(BF16)

    def split(bit, send_ref, keep_ref):
        keep_ref[...] = acc_ref[pl.ds(pl.multiple_of(bit * half, half), half), :]
        send_ref[...] = acc_ref[pl.ds(pl.multiple_of((1 - bit) * half, half), half), :]

    @pl.when(n < half_tiles)
    def _():
        split(sc_ref[first], sa_ref, ka_ref)

    @pl.when(n >= half_tiles)
    def _():
        split(sc_ref[last], sb_ref, kb_ref)


def product(sc, k, context0, context1, up0, up1, lay):
    length, width = up0.shape
    rows = lay.rows
    tile = width // 4
    at = lay.at_z + k
    left = lambda n, sc: (0, jnp.minimum(n, 1))
    right = lambda n, sc: (0, jnp.maximum(n - 2, 0))
    part = jax.ShapeDtypeStruct((rows // 2, width // 2), BF16)
    return call(
        functools.partial(product_body, 2, lay.at_bit(0), lay.at_bit(lay.bits - 1)),
        (4,),
        [
            pl.BlockSpec((rows, length), lambda n, sc: (sc[at], 0)),
            pl.BlockSpec((rows, length), lambda n, sc: (sc[at], 0)),
            pl.BlockSpec((length, tile), lambda n, sc: (0, n)),
            pl.BlockSpec((length, tile), lambda n, sc: (0, n)),
        ],
        [
            pl.BlockSpec((rows // 2, tile), left),
            pl.BlockSpec((rows // 2, tile), left),
            pl.BlockSpec((rows // 2, tile), right),
            pl.BlockSpec((rows // 2, tile), right),
        ],
        [part] * 4,
        scratch=[pltpu.VMEM((rows, tile), BF16)],
        cost=pl.CostEstimate(
            flops=4 * rows * length * width,
            transcendentals=0,
            bytes_accessed=4 * length * width + 2 * rows * width,
        ),
    )(sc, context0, context1, up0, up1)


def grad_context_body(parts, sc_ref, u0_ref, u1_ref, *refs):
    weights, (g0_ref, g1_ref, a0_ref, a1_ref) = refs[:-4], refs[-4:]
    n = pl.program_id(0)

    def add(weight_ref):
        d0 = dot(u0_ref[...], weight_ref[...], NT)
        d1 = dot(u1_ref[...], weight_ref[...], NT)

        @pl.when(n == 0)
        def _():
            a0_ref[...] = d0
            a1_ref[...] = d1

        @pl.when(n > 0)
        def _():
            a0_ref[...] += d0
            a1_ref[...] += d1

    if len(weights) == 1:
        add(weights[0])
    else:
        for p in range(parts):
            pl.when(n == p)(functools.partial(add, weights[p]))

    @pl.when(n == parts - 1)
    def _():
        g0_ref[...] = a0_ref[...].astype(BF16)
        g1_ref[...] = a1_ref[...].astype(BF16)


def grad_context(sc, up0, up1, weights, lay):
    length, width = up0.shape
    rows = lay.rows
    tile = width // 4
    at = lay.at_piece
    if len(weights) == 1:
        weight_specs = [pl.BlockSpec((rows, tile), lambda n, sc: (0, sc[at + n]))]
    else:
        weight_specs = [pl.BlockSpec((rows, tile), lambda n, sc: (0, 0))] * 4
    return call(
        functools.partial(grad_context_body, 4),
        (4,),
        [pl.BlockSpec((length, tile), lambda n, sc: (0, sc[at + n]))] * 2 + weight_specs,
        [pl.BlockSpec((length, rows), lambda n, sc: (0, 0))] * 2,
        [jax.ShapeDtypeStruct((length, rows), BF16)] * 2,
        scratch=[pltpu.VMEM((length, rows), F32)] * 2,
        cost=pl.CostEstimate(
            flops=4 * rows * length * width,
            transcendentals=0,
            bytes_accessed=4 * length * width + 2 * rows * width,
        ),
    )(sc, up0, up1, *weights)


def backward_body(
    per, sc_ref, q_ref, k_ref, v_ref, seg_row_ref, seg_col_ref, own_ref, other_ref, *refs
):
    gq_ref, gk_ref, gv_ref, mask_ref, ak_ref, av_ref = refs[-6:]
    group = pl.program_id(0)
    parity = sc_ref[0]

    @pl.when(group == 0)
    def _():
        fill_mask(mask_ref, seg_row_ref, seg_col_ref)

    key_t = k_ref[...].T
    ak_ref[...] = jnp.zeros_like(ak_ref)
    av_ref[...] = jnp.zeros_like(av_ref)
    for h in range(REPEAT):
        side = group if per == REPEAT else h
        column = h if per == REPEAT else 0
        cols = slice(column * DH, (column + 1) * DH)
        grad = jnp.where(side == parity, own_ref[:, cols], other_ref[:, cols])
        for start, tile, upto in tiles_of(q_ref.shape[0]):
            query = q_ref[start : start + tile, h * DH : (h + 1) * DH]
            probs, cap_tanh = softmax_tile(
                k_ref[:upto, :], query, mask_ref[:upto, start : start + tile]
            )
            grad_rows = grad[start : start + tile, :]
            grad_probs = dot(v_ref[:upto, :], grad_rows, NT)
            delta = jnp.sum(probs * grad_probs, axis=0, keepdims=True)
            scores = probs * (grad_probs - delta) * (SCALE - SCALE * (cap_tanh * cap_tanh))
            scores = scores.astype(BF16)
            av_ref[:upto, :] += dot(probs.astype(BF16), grad_rows, NN)
            ak_ref[:upto, :] += dot(scores, query, NN)
            grad_query = dot(key_t[:, :upto], scores, NN).T
            gq_ref[start : start + tile, h * DH : (h + 1) * DH] = grad_query.astype(BF16)
    gk_ref[...] = ak_ref[...].astype(BF16)
    gv_ref[...] = av_ref[...].astype(BF16)


def backward(sc, k, queries, keys, values, seg_row, seg_col, own, other, before, lay):
    length = queries.shape[0]
    per = lay.heads_shard
    groups = 2 * per // REPEAT
    at = lay.at_z + k

    def whole(i, sc):
        return (0, sc[at] * groups + i)

    if per == REPEAT:
        gc_spec = pl.BlockSpec((length, lay.rows), lambda i, sc: (0, 0))
    else:
        gc_spec = pl.BlockSpec((length, DH), lambda i, sc: (0, 0))
    in_specs = [
        pl.BlockSpec((length, REPEAT * DH), whole),
        pl.BlockSpec((length, DH), whole),
        pl.BlockSpec((length, DH), whole),
        pl.BlockSpec((1, length), lambda i, sc: (0, 0)),
        pl.BlockSpec((length, 1), lambda i, sc: (0, 0)),
        gc_spec,
        gc_spec,
    ]
    args = [sc, queries, keys, values, seg_row, seg_col, own, other]
    aliases = {}
    if before is not None:
        aliases = {len(args) + n: n for n in range(3)}
        in_specs += [pl.BlockSpec(memory_space=pl.ANY)] * 3
        args += list(before)
    pairs = 2 * per * length * length
    return call(
        functools.partial(backward_body, per),
        (groups,),
        in_specs,
        [
            pl.BlockSpec((length, REPEAT * DH), whole),
            pl.BlockSpec((length, DH), whole),
            pl.BlockSpec((length, DH), whole),
        ],
        [
            jax.ShapeDtypeStruct(queries.shape, BF16),
            jax.ShapeDtypeStruct(keys.shape, BF16),
            jax.ShapeDtypeStruct(values.shape, BF16),
        ],
        scratch=[
            pltpu.VMEM((length, length), F32),
            pltpu.VMEM((length, DH), F32),
            pltpu.VMEM((length, DH), F32),
        ],
        aliases=aliases,
        cost=pl.CostEstimate(
            flops=10 * pairs * DH, transcendentals=2 * pairs, bytes_accessed=20 * length * per * DH
        ),
    )(*args)


def adam_body(pieces, tokens, sc_ref, m1_ref, m2_ref, *refs):
    out_ref = refs[-1]
    n = pl.program_id(0)

    def step(piece_ref):
        gradient = piece_ref[...].astype(F32) * (1.0 / tokens)
        moment_one = 0.9 * m1_ref[...] + 0.1 * gradient
        moment_two = 0.95 * m2_ref[...] + 0.05 * gradient * gradient
        out_ref[...] = moment_one / (jnp.sqrt(moment_two) + 1e-08)

    for p in range(pieces):
        pl.when(n == p)(functools.partial(step, refs[p]))


def adam(places, pieces, first_moment, second_moment, tokens):
    rows, width = pieces[0].shape
    count = len(pieces)
    spec = pl.BlockSpec((rows, width), lambda n, at: (at[2 * n], at[2 * n + 1]))
    return call(
        functools.partial(adam_body, count, tokens),
        (count,),
        [spec, spec] + [pl.BlockSpec((rows, width), lambda n, at: (0, 0))] * count,
        spec,
        jax.ShapeDtypeStruct(first_moment.shape, F32),
        cost=pl.CostEstimate(
            flops=10 * first_moment.size,
            transcendentals=first_moment.size,
            bytes_accessed=14 * first_moment.size,
        ),
    )(places, first_moment, second_moment, *pieces)


class Layout:
    def __init__(self, replicas, shards, rows):
        self.replicas, self.shards, self.rows = replicas, shards, rows
        self.z = shards // 2
        self.bits = replicas.bit_length() - 1
        self.heads_shard = HEADS // shards
        self.order = [0] + list(range(1, self.z, 2)) + list(range(self.z - 2, 0, -2))
        self.place = [self.order.index(z) for z in range(self.z)]
        self.at_z = 1
        self.at_piece = self.at_z + self.z
        table = []
        for r in range(replicas):
            bits = [(r >> b) & 1 for b in range(self.bits)]
            x, y = bits[0], bits[-1]
            for s in range(shards):
                z, core = s // 2, s % 2
                zs = [self.order[(self.place[z] - k) % self.z] for k in range(self.z)]
                table.append([core] + zs + [x, 1 - x, 2 + y, 3 - y] + bits)
        self.table = np.array(table, np.int32)

    def at_bit(self, b):
        return self.at_piece + 4 + b

    def sibling(self, x):
        return lax.ppermute(x, "shard", [(s, s ^ 1) for s in range(self.shards)])

    def onward(self, x):
        perm = []
        for p in range(self.z):
            a, b = self.order[p], self.order[(p + 1) % self.z]
            perm += [(2 * a + core, 2 * b + core) for core in range(2)]
        return lax.ppermute(x, "shard", perm)

    def across(self, x, b):
        return lax.ppermute(x, "replica", [(r, r ^ (1 << b)) for r in range(self.replicas)])


def per_device(queries, keys, values, segments, out_weight, upstream, first_moment, second_moment):
    length, width = upstream.shape
    rows = out_weight.shape[0]
    lay = Layout(lax.axis_size("replica"), lax.axis_size("shard"), rows)
    device = lax.axis_index("replica") * lay.shards + lax.axis_index("shard")
    sc = lax.dynamic_index_in_dim(jnp.asarray(lay.table), device, 0, keepdims=False)
    bit = [sc[lay.at_bit(b)] for b in range(lay.bits)]
    left_bits = list(range(lay.bits))
    right_bits = left_bits[::-1]
    quarter = width // 4

    upstream_other = lay.sibling(upstream)

    ring_x = lax.dynamic_slice_in_dim(out_weight, bit[left_bits[0]] * quarter, quarter, 1)
    ring_y = lax.dynamic_slice_in_dim(
        out_weight, 2 * quarter + bit[right_bits[0]] * quarter, quarter, 1
    )
    weights = [(out_weight,)]
    for k in range(1, lay.z):
        ring_x, ring_y = lay.onward(ring_x), lay.onward(ring_y)
        weights.append(
            (
                ring_x,
                lay.across(ring_x, left_bits[0]),
                ring_y,
                lay.across(ring_y, right_bits[0]),
            )
        )

    seg_row = segments
    seg_col = segments.reshape(length, 1)
    context_send = forward(sc, True, queries, keys, values, seg_row, seg_col, lay)
    context_other = lay.sibling(context_send)
    context_own = forward(sc, False, queries, keys, values, seg_row, seg_col, lay)

    def halved(send, keep, received_before, order):
        total = keep.astype(F32) + lay.across(send, order[0]).astype(F32)
        for b in order[1:]:
            size = total.shape[0] // 2
            away = lax.dynamic_slice_in_dim(total, (1 - bit[b]) * size, size, 0).astype(BF16)
            stay = lax.dynamic_slice_in_dim(total, bit[b] * size, size, 0)
            total = stay + lay.across(away, b).astype(F32)
        if received_before is not None:
            total = total + received_before.astype(F32)
        return total.astype(BF16)

    passed = [None, None]
    for k in list(range(1, lay.z)) + [0]:
        send_l, keep_l, send_r, keep_r = product(
            sc, k, context_own, context_other, upstream, upstream_other, lay
        )
        sums = [
            halved(send_l, keep_l, passed[0], left_bits),
            halved(send_r, keep_r, passed[1], right_bits),
        ]
        if k:
            passed = [lay.onward(x) for x in sums]

    pieces, places = [], []
    for half, order in enumerate([left_bits, right_bits]):
        index = sum(bit[b] << (lay.bits - 1 - n) for n, b in enumerate(order))
        have = [(sums[half], index)]
        for n, b in reversed(list(enumerate(order))):
            weight = 1 << (lay.bits - 1 - n)
            flip = (1 - 2 * bit[b]) * weight
            have += [(lay.across(x, b), at + flip) for x, at in have]
        pieces += [x for x, _ in have]
        for _, at in have:
            places += [at, jnp.int32(half)]
    tokens = length * lay.replicas * lay.shards
    adam_step = adam(
        jnp.stack(places).astype(jnp.int32), pieces, first_moment, second_moment, tokens
    )

    grads = None
    for k in range(lay.z):
        own, send = grad_context(sc, upstream, upstream_other, weights[k], lay)
        grads = backward(
            sc, k, queries, keys, values, seg_row, seg_col, own, lay.sibling(send), grads, lay
        )
    return (*grads, adam_step)


def solution(mesh):
    both = P(("replica", "shard"), None)
    shard = P("shard", None)
    return jax.shard_map(
        per_device,
        mesh=mesh,
        in_specs=(both, both, both, both, shard, both, shard, shard),
        out_specs=(both, both, both, shard),
        check_vma=False,
    )
```

```python
import functools

import jax
import jax.numpy as jnp
import numpy as np
from jax import lax
from jax.experimental import pallas as pl
from jax.experimental.pallas import tpu as pltpu
from jax.sharding import PartitionSpec as P

HEADS = 16
KV_HEADS = 8
DH = 128
REPEAT = HEADS // KV_HEADS

SCALE = 1.0 / 12.0
CAP = 50.0
VMEM = 40 * 1024 * 1024
F32 = jnp.float32
BF16 = jnp.bfloat16

NT = (((1,), (1,)), ((), ()))
NN = (((1,), (0,)), ((), ()))


def dot(a, b, dims):
    return lax.dot_general(a, b, dims, preferred_element_type=F32)


def call(body, sc, grid, ins, outs, scratch=(), through=(), before=()):
    n_in, n_out, n_before, n_through = len(ins), len(outs), len(before), len(through)

    def kernel(sc_ref, *refs):
        at = n_in + n_before + n_through
        body(sc_ref, *refs[:n_in], *refs[at : at + n_out], *refs[at + n_out + n_through :])

    anywhere = pl.BlockSpec(memory_space=pl.ANY)
    aliases = {1 + n_in + n: n for n in range(n_before)}
    aliases.update({1 + n_in + n_before + n: n_out + n for n in range(n_through)})
    results = pl.pallas_call(
        kernel,
        grid_spec=pltpu.PrefetchScalarGridSpec(
            num_scalar_prefetch=1,
            grid=grid,
            in_specs=[pl.BlockSpec(block, index) for _, block, index in ins]
            + [anywhere] * (n_before + n_through),
            out_specs=[pl.BlockSpec(block, index) for _, _, block, index in outs]
            + [anywhere] * n_through,
            scratch_shapes=list(scratch),
        ),
        out_shape=[jax.ShapeDtypeStruct(shape, dtype) for shape, dtype, _, _ in outs]
        + [jax.ShapeDtypeStruct(x.shape, x.dtype) for x in through],
        input_output_aliases=aliases,
        cost_estimate=pl.CostEstimate(flops=1, transcendentals=0, bytes_accessed=1),
        compiler_params=pltpu.CompilerParams(vmem_limit_bytes=VMEM),
    )(sc, *[array for array, _, _ in ins], *before, *through)
    return results[:n_out], results[n_out:]


def first(*_):
    return (0, 0)


def fill_mask(mask_ref, seg_row_ref, seg_col_ref):
    length = mask_ref.shape[0]
    j = lax.broadcasted_iota(jnp.int32, (length, length), 0)
    i = lax.broadcasted_iota(jnp.int32, (length, length), 1)
    allowed = (j <= i) & (seg_col_ref[...] == seg_row_ref[...])
    mask_ref[...] = jnp.where(allowed, 1.0, 0.0).astype(F32)


def tiles_of(length):
    tile = 256
    return [(t * tile, tile, (t + 1) * tile) for t in range(length // tile)]


def softmax_tile(key, query, mask):
    cap_tanh = jnp.tanh(dot(key, query, NT) * (SCALE / CAP))
    weights = jnp.exp(cap_tanh * CAP) * mask
    inverse = 1.0 / jnp.sum(weights, axis=0, keepdims=True)
    return weights * inverse, cap_tanh


def cut_body(sc_ref, a_ref, b_ref, x_ref, y_ref):
    x_ref[...] = a_ref[...]
    y_ref[...] = b_ref[...]


def cut(sc, weight, lay, through):
    rows, width = weight.shape
    block = (rows, width // 4)
    at = lay.at_piece
    return call(
        cut_body,
        sc,
        (1,),
        [
            (weight, block, lambda n, sc: (0, sc[at])),
            (weight, block, lambda n, sc: (0, sc[at + 2])),
        ],
        [(block, BF16, block, first)] * 2,
        through=through,
    )


def forward_body(
    heads, sc_ref, q_ref, k_ref, v_ref, seg_row_ref, seg_col_ref, send_ref, own_ref, mask_ref
):
    @pl.when(pl.program_id(0) == 0)
    def _():
        fill_mask(mask_ref, seg_row_ref, seg_col_ref)

    def run(out_ref):
        value_t = v_ref[...].T
        for h in range(heads):
            for start, tile, upto in tiles_of(q_ref.shape[0]):
                probs, _ = softmax_tile(
                    k_ref[:upto, :],
                    q_ref[start : start + tile, h * DH : (h + 1) * DH],
                    mask_ref[:upto, start : start + tile],
                )
                context = dot(value_t[:, :upto], probs.astype(BF16), NN)
                out_ref[h * DH : (h + 1) * DH, start : start + tile] = context.astype(BF16)

    pl.when(pl.program_id(0) == 0)(functools.partial(run, send_ref))
    pl.when(pl.program_id(0) == 1)(functools.partial(run, own_ref))


def forward(sc, k, block, lay, through):
    queries, keys, values, seg_row, seg_col = block
    length = queries.shape[0]
    per = lay.heads_shard
    at = lay.at_z + k

    def shard_of(i, sc):
        return 2 * sc[at] + jnp.where(i == 0, 1 - sc[0], sc[0])

    def kv_of(i, sc):
        return (0, (shard_of(i, sc) * per) // REPEAT)

    out = ((per * DH, length), BF16, (per * DH, length), first)
    return call(
        functools.partial(forward_body, per),
        sc,
        (2,),
        [
            (queries, (length, per * DH), lambda i, sc: (0, shard_of(i, sc))),
            (keys, (length, DH), kv_of),
            (values, (length, DH), kv_of),
            (seg_row, (1, length), first),
            (seg_col, (length, 1), first),
        ],
        [out, out],
        scratch=[pltpu.VMEM((length, length), F32)],
        through=through,
    )


def product_body(count, at_x, at_y, sc_ref, *refs):
    own, other = refs[:count], refs[count : 2 * count]
    u0_ref, u1_ref = refs[2 * count : 2 * count + 2]
    outs, acc_ref = refs[2 * count + 2 : -1], refs[-1]
    n = pl.program_id(0)
    rows = acc_ref.shape[0] // count
    half = rows // 2

    def stack(parts):
        return parts[0][...] if count == 1 else jnp.concatenate([p[...] for p in parts], axis=0)

    acc = dot(stack(own), u0_ref[...], NN) + dot(stack(other), u1_ref[...], NN)
    acc_ref[...] = acc.astype(BF16)

    def split(bit, side):
        for c in range(count):
            send_ref, keep_ref = outs[4 * c + side], outs[4 * c + side + 1]
            stay = pl.multiple_of(c * rows + bit * half, half)
            away = pl.multiple_of(c * rows + (1 - bit) * half, half)
            keep_ref[...] = acc_ref[pl.ds(stay, half), :]
            send_ref[...] = acc_ref[pl.ds(away, half), :]

    @pl.when(n < 2)
    def _():
        split(sc_ref[at_x], 0)

    @pl.when(n >= 2)
    def _():
        split(sc_ref[at_y], 2)


def product(sc, own, other, up0, up1, lay, through):
    length, width = up0.shape
    rows = lay.rows
    tile = width // 4
    count = len(own)
    half, block = (rows // 2, width // 2), (rows // 2, tile)
    left = (half, BF16, block, lambda n, sc: (0, jnp.minimum(n, 1)))
    right = (half, BF16, block, lambda n, sc: (0, jnp.maximum(n - 2, 0)))
    return call(
        functools.partial(product_body, count, lay.at_bit(0), lay.at_bit(lay.bits - 1)),
        sc,
        (4,),
        [(x, (rows, length), first) for x in (*own, *other)]
        + [(u, (length, tile), lambda n, sc: (0, n)) for u in (up0, up1)],
        [left, left, right, right] * count,
        scratch=[pltpu.VMEM((count * rows, tile), BF16)],
        through=through,
    )


def combine_body(counts, merged, sc_ref, *refs):
    outs = refs[sum(counts) :]
    at = 0
    for side, count in enumerate(counts):
        total = refs[at][...].astype(F32)
        for ref in refs[at + 1 : at + count]:
            total = total + ref[...].astype(F32)
        at += count
        if merged:
            width = total.shape[1]
            outs[0][:, side * width : (side + 1) * width] = total.astype(BF16)
        else:
            outs[side][...] = total.astype(BF16)


def combine(sc, terms, ring, away, merged, lay, through):
    count = len(terms[0])
    deep = count if away else lay.bits
    width = terms[0][0].shape[1]
    size = lay.rows >> deep
    ins, counts = [], []
    for side in range(2):
        order = list(range(lay.bits))
        order = order[::-1] if side else order

        def place(level, order=order):
            def index(n, sc):
                at = 0
                for m in range(level, deep):
                    bit = sc[lay.at_bit(order[m])]
                    bit = 1 - bit if away and m == deep - 1 else bit
                    at = 2 * at + bit
                return (at, 0)

            return index

        for m, x in enumerate(terms[side]):
            ins.append((x, (size, width), place(max(m, 1))))
        if ring is not None:
            ins.append((ring, (size, width), lambda n, sc, side=side: (0, side)))
        counts.append(count + (ring is not None))
    if merged:
        outs = [((size, 2 * width), BF16, (size, 2 * width), first)]
    else:
        outs = [((size, width), BF16, (size, width), first)] * 2
    return call(
        functools.partial(combine_body, counts, merged), sc, (1,), ins, outs, through=through
    )


def grad_context_body(parts, sc_ref, u0_ref, u1_ref, *refs):
    weights, (g0_ref, g1_ref, a0_ref, a1_ref) = refs[:-4], refs[-4:]
    n = pl.program_id(0)

    def add(weight_ref):
        d0 = dot(u0_ref[...], weight_ref[...], NT)
        d1 = dot(u1_ref[...], weight_ref[...], NT)

        @pl.when(n == 0)
        def _():
            a0_ref[...] = d0
            a1_ref[...] = d1

        @pl.when(n > 0)
        def _():
            a0_ref[...] += d0
            a1_ref[...] += d1

    if len(weights) == 1:
        add(weights[0])
    else:
        for p in range(parts):
            pl.when(n == p)(functools.partial(add, weights[p]))

    @pl.when(n == parts - 1)
    def _():
        g0_ref[...] = a0_ref[...].astype(BF16)
        g1_ref[...] = a1_ref[...].astype(BF16)


def grad_context(sc, up0, up1, weights, lay, through):
    length, width = up0.shape
    rows = lay.rows
    tile = width // 4
    at = lay.at_piece
    if len(weights) == 1:
        weight_ins = [(weights[0], (rows, tile), lambda n, sc: (0, sc[at + n]))]
    else:
        weight_ins = [(w, (rows, tile), first) for w in weights]
    return call(
        functools.partial(grad_context_body, 4),
        sc,
        (4,),
        [(u, (length, tile), lambda n, sc: (0, sc[at + n])) for u in (up0, up1)] + weight_ins,
        [((length, rows), BF16, (length, rows), first)] * 2,
        scratch=[pltpu.VMEM((length, rows), F32)] * 2,
        through=through,
    )


def backward_body(
    per, sc_ref, q_ref, k_ref, v_ref, seg_row_ref, seg_col_ref, own_ref, other_ref, *refs
):
    gq_ref, gk_ref, gv_ref, mask_ref, ak_ref, av_ref = refs[-6:]
    group = pl.program_id(0)
    parity = sc_ref[0]

    @pl.when(group == 0)
    def _():
        fill_mask(mask_ref, seg_row_ref, seg_col_ref)

    key_t = k_ref[...].T
    ak_ref[...] = jnp.zeros_like(ak_ref)
    av_ref[...] = jnp.zeros_like(av_ref)
    for h in range(REPEAT):
        side = group if per == REPEAT else h
        column = h if per == REPEAT else 0
        cols = slice(column * DH, (column + 1) * DH)
        grad = jnp.where(side == parity, own_ref[:, cols], other_ref[:, cols])
        for start, tile, upto in tiles_of(q_ref.shape[0]):
            query = q_ref[start : start + tile, h * DH : (h + 1) * DH]
            probs, cap_tanh = softmax_tile(
                k_ref[:upto, :], query, mask_ref[:upto, start : start + tile]
            )
            grad_rows = grad[start : start + tile, :]
            grad_probs = dot(v_ref[:upto, :], grad_rows, NT)
            delta = jnp.sum(probs * grad_probs, axis=0, keepdims=True)
            scores = probs * (grad_probs - delta) * (SCALE - SCALE * (cap_tanh * cap_tanh))
            scores = scores.astype(BF16)
            av_ref[:upto, :] += dot(probs.astype(BF16), grad_rows, NN)
            ak_ref[:upto, :] += dot(scores, query, NN)
            grad_query = dot(key_t[:, :upto], scores, NN).T
            gq_ref[start : start + tile, h * DH : (h + 1) * DH] = grad_query.astype(BF16)
    gk_ref[...] = ak_ref[...].astype(BF16)
    gv_ref[...] = av_ref[...].astype(BF16)


def backward(sc, k, block, own, other, before, lay, through):
    queries, keys, values, seg_row, seg_col = block
    length = queries.shape[0]
    per = lay.heads_shard
    groups = 2 * per // REPEAT
    at = lay.at_z + k

    def whole(i, sc):
        return (0, sc[at] * groups + i)

    heads = (length, REPEAT * DH), whole
    one = (length, DH), whole
    return call(
        functools.partial(backward_body, per),
        sc,
        (groups,),
        [
            (queries, *heads),
            (keys, *one),
            (values, *one),
            (seg_row, (1, length), first),
            (seg_col, (length, 1), first),
            (own, (length, lay.rows), first),
            (other, (length, lay.rows), first),
        ],
        [(queries.shape, BF16, *heads), (keys.shape, BF16, *one), (values.shape, BF16, *one)],
        scratch=[
            pltpu.VMEM((length, length), F32),
            pltpu.VMEM((length, DH), F32),
            pltpu.VMEM((length, DH), F32),
        ],
        before=before,
        through=through,
    )


def adam_body(pieces, tokens, sc_ref, m1_ref, m2_ref, *refs):
    out_ref = refs[-1]
    n = pl.program_id(0)

    def step(piece_ref):
        gradient = piece_ref[...].astype(F32) * (1.0 / tokens)
        moment_one = 0.9 * m1_ref[...] + 0.1 * gradient
        moment_two = 0.95 * m2_ref[...] + 0.05 * gradient * gradient
        out_ref[...] = moment_one / (jnp.sqrt(moment_two) + 1e-08)

    for p in range(pieces):
        pl.when(n == p)(functools.partial(step, refs[p]))


def adam(sc, pieces, first_moment, second_moment, tokens, lay, before, through):
    rows, width = pieces[0][0].shape
    count = len(pieces)
    places = []
    for _, side, flips in pieces:
        order = list(range(lay.bits))
        order = order[::-1] if side else order
        row = 0
        for b, flip in zip(order, flips):
            bit = sc[lay.at_bit(b)]
            row = 2 * row + (1 - bit if flip else bit)
        places += [row, jnp.int32(side)]
    at = lambda n, at: (at[2 * n], at[2 * n + 1])
    block = (rows, width)
    return call(
        functools.partial(adam_body, count, tokens),
        jnp.stack(places).astype(jnp.int32),
        (count,),
        [(first_moment, block, at), (second_moment, block, at)]
        + [(x, block, first) for x, _, _ in pieces],
        [(first_moment.shape, F32, block, at)],
        before=before,
        through=through,
    )


class Layout:
    def __init__(self, replicas, shards, rows):
        self.replicas, self.shards, self.rows = replicas, shards, rows
        self.z = shards // 2
        self.bits = replicas.bit_length() - 1
        self.heads_shard = HEADS // shards
        self.order = [0] + list(range(1, self.z, 2)) + list(range(self.z - 2, 0, -2))
        self.place = [self.order.index(z) for z in range(self.z)]
        self.at_z = 1
        self.at_piece = self.at_z + self.z
        table = []
        for r in range(replicas):
            bits = [(r >> b) & 1 for b in range(self.bits)]
            x, y = bits[0], bits[-1]
            for s in range(shards):
                z, core = s // 2, s % 2
                zs = [self.order[(self.place[z] - k) % self.z] for k in range(self.z)]
                table.append([core] + zs + [x, 1 - x, 2 + y, 3 - y] + bits)
        self.table = np.array(table, np.int32)

    def at_bit(self, b):
        return self.at_piece + 4 + b

    def sibling(self, x):
        return lax.ppermute(x, "shard", [(s, s ^ 1) for s in range(self.shards)])

    def onward(self, x):
        perm = []
        for p in range(self.z):
            a, b = self.order[p], self.order[(p + 1) % self.z]
            perm += [(2 * a + core, 2 * b + core) for core in range(2)]
        return lax.ppermute(x, "shard", perm)

    def across(self, x, b):
        return lax.ppermute(x, "replica", [(r, r ^ (1 << b)) for r in range(self.replicas)])


def per_device(queries, keys, values, segments, out_weight, upstream, first_moment, second_moment):
    length, width = upstream.shape
    lay = Layout(lax.axis_size("replica"), lax.axis_size("shard"), out_weight.shape[0])
    tokens = length * lay.replicas * lay.shards
    device = lax.axis_index("replica") * lay.shards + lax.axis_index("shard")
    sc = lax.dynamic_index_in_dim(jnp.asarray(lay.table), device, 0, keepdims=False)
    orders = [list(range(lay.bits)), list(range(lay.bits))[::-1]]
    block = (queries, keys, values, segments, segments.reshape(length, 1))

    token = jnp.zeros((8, 128), F32)
    arrived = [{}, {}]
    crossed = [{}, {}]
    context_own, context_other = {}, {}
    terms = {}
    ring = {}
    final = []
    grads = ()
    gc_own, gc_other = {}, {}

    def run(function, *args, relays=(), **more):
        nonlocal token
        held = [arrived[side][k] for side, k in relays]
        outs, handed = function(*args, through=[token, *held], **more)
        token = handed[0]
        for (side, k), x in zip(relays, handed[1:]):
            arrived[side][k] = x
            if k + 1 < lay.z:
                arrived[side][k + 1] = lay.onward(x)
            crossed[side][k] = lay.across(x, orders[side][0])
        return outs

    def do_forward(k, relays=()):
        send, context_own[k] = run(forward, sc, k, block, lay, relays=relays)
        context_other[k] = lay.sibling(send)

    def do_product(ks, relays=()):
        outs = run(
            product,
            sc,
            [context_own[k] for k in ks],
            [context_other[k] for k in ks],
            upstream,
            upstream_other,
            lay,
            relays=relays,
        )
        for n, k in enumerate(ks):
            send_l, keep_l, send_r, keep_r = outs[4 * n : 4 * n + 4]
            terms[k] = [
                [keep_l, lay.across(send_l, orders[0][0])],
                [keep_r, lay.across(send_r, orders[1][0])],
            ]

    def do_halve(k, relays=()):
        sends = run(combine, sc, terms[k], None, True, False, lay, relays=relays)
        stage = len(terms[k][0]) - 1
        for side in range(2):
            terms[k][side].append(lay.across(sends[side], orders[side][stage]))

    def do_sum(k, relays=()):
        outs = run(combine, sc, terms[k], ring.get(k), False, k > 0, lay, relays=relays)
        if k:
            ring[(k + 1) % lay.z] = lay.onward(outs[0])
        else:
            final.extend(outs)

    def do_grad_context(k, relays=()):
        weights = [out_weight]
        if k:
            weights = [arrived[0][k], crossed[0][k], arrived[1][k], crossed[1][k]]
        gc_own[k], send = run(
            grad_context, sc, upstream, upstream_other, weights, lay, relays=relays
        )
        gc_other[k] = lay.sibling(send)

    def do_backward(k, relays=()):
        nonlocal grads
        grads = run(
            backward, sc, k, block, gc_own[k], gc_other[k], grads, lay, relays=relays
        )

    upstream_other = lay.sibling(upstream)
    for side, x in enumerate(run(cut, sc, out_weight, lay)):
        arrived[side][1] = lay.onward(x)

    early, rest = list(range(1, lay.z)), list(range(3, lay.z))
    halvings = range(lay.bits - 1)
    do_forward(1)
    do_forward(2)
    do_product([1])
    for k in rest:
        do_forward(k)
    do_forward(0, relays=[(0, 1)])
    do_product(early[1:])
    do_halve(1)
    do_product([0], relays=[(1, 1)])
    do_grad_context(0)
    do_backward(0, relays=[(0, 2)])
    do_halve(2)
    for k in rest:
        do_halve(k, relays=[(1, 2)] if k == 3 else [(0, k - 1), (1, k - 1)])
    do_grad_context(1)
    do_backward(1)
    for n in list(halvings)[1:]:
        do_halve(1)
    do_sum(1)
    do_halve(0)
    for n in list(halvings)[1:]:
        do_halve(2)
    last = lay.z - 1
    do_sum(2, relays=[(0, last), (1, last)])
    do_grad_context(2)
    do_backward(2)
    for n in list(halvings)[1:]:
        for k in [*rest, 0]:
            do_halve(k)
    for k in rest:
        do_sum(k)
    do_sum(0)
    have = [[(final[side], side, (False,) * lay.bits)] for side in range(2)]
    for n in range(lay.bits - 1, -1, -1):
        for side in range(2):
            have[side] += [
                (lay.across(x, orders[side][n]), side, flips[:n] + (True,) + flips[n + 1 :])
                for x, _, flips in have[side]
            ]
    for k in rest:
        do_grad_context(k)
        do_backward(k)
    near = [p for side in range(2) for p in have[side][:-1]]
    far = [have[side][-1] for side in range(2)]
    adam_step = run(adam, sc, near, first_moment, second_moment, tokens, lay, before=())
    adam_step = run(adam, sc, far, first_moment, second_moment, tokens, lay, before=adam_step)
    return (*grads, *adam_step)


def solution(mesh):
    both = P(("replica", "shard"), None)
    shard = P("shard", None)
    return jax.shard_map(
        per_device,
        mesh=mesh,
        in_specs=(both, both, both, both, shard, both, shard, shard),
        out_specs=(both, both, both, shard),
        check_vma=False,
    )
```

```python
import functools

import jax
import jax.numpy as jnp
import numpy as np
from jax import lax
from jax.experimental import pallas as pl
from jax.experimental.pallas import tpu as pltpu
from jax.sharding import PartitionSpec as P

HEADS = 16
KV_HEADS = 8
DH = 128
REPEAT = HEADS // KV_HEADS

SCALE = 1.0 / 12.0
CAP = 50.0
VMEM = 60 * 1024 * 1024
F32 = jnp.float32
BF16 = jnp.bfloat16

NT = (((1,), (1,)), ((), ()))
NN = (((1,), (0,)), ((), ()))


def dot(a, b, dims):
    return lax.dot_general(a, b, dims, preferred_element_type=F32)


def call(body, sc, grid, ins, outs, scratch=(), through=(), before=()):
    n_in, n_out, n_before, n_through = len(ins), len(outs), len(before), len(through)

    def kernel(sc_ref, *refs):
        at = n_in + n_before + n_through
        body(sc_ref, *refs[:n_in], *refs[at : at + n_out], *refs[at + n_out + n_through :])

    anywhere = pl.BlockSpec(memory_space=pl.ANY)
    aliases = {1 + n_in + n: n for n in range(n_before)}
    aliases.update({1 + n_in + n_before + n: n_out + n for n in range(n_through)})
    results = pl.pallas_call(
        kernel,
        grid_spec=pltpu.PrefetchScalarGridSpec(
            num_scalar_prefetch=1,
            grid=grid,
            in_specs=[pl.BlockSpec(block, index) for _, block, index in ins]
            + [anywhere] * (n_before + n_through),
            out_specs=[pl.BlockSpec(block, index) for _, _, block, index in outs]
            + [anywhere] * n_through,
            scratch_shapes=list(scratch),
        ),
        out_shape=[jax.ShapeDtypeStruct(shape, dtype) for shape, dtype, _, _ in outs]
        + [jax.ShapeDtypeStruct(x.shape, x.dtype) for x in through],
        input_output_aliases=aliases,
        cost_estimate=pl.CostEstimate(flops=1, transcendentals=0, bytes_accessed=1),
        compiler_params=pltpu.CompilerParams(vmem_limit_bytes=VMEM),
    )(sc, *[array for array, _, _ in ins], *before, *through)
    return results[:n_out], results[n_out:]


def first(*_):
    return (0, 0)


def fill_mask(mask_ref, seg_row_ref, seg_col_ref):
    length = mask_ref.shape[0]
    j = lax.broadcasted_iota(jnp.int32, (length, length), 0)
    i = lax.broadcasted_iota(jnp.int32, (length, length), 1)
    allowed = (j <= i) & (seg_col_ref[...] == seg_row_ref[...])
    mask_ref[...] = jnp.where(allowed, 1.0, 0.0).astype(F32)


def tiles_of(length):
    tile = 256
    return [(t * tile, tile, (t + 1) * tile) for t in range(length // tile)]


def softmax_tile(key, query, mask):
    cap_tanh = jnp.tanh(dot(key, query, NT) * (SCALE / CAP))
    weights = jnp.exp(cap_tanh * CAP) * mask
    inverse = 1.0 / jnp.sum(weights, axis=0, keepdims=True)
    return weights * inverse, cap_tanh


def cut_body(sc_ref, a_ref, b_ref, x_ref, y_ref):
    x_ref[...] = a_ref[...]
    y_ref[...] = b_ref[...]


def cut(sc, weight, lay, through):
    rows, width = weight.shape
    block = (rows, width // 4)
    at = lay.at_piece
    return call(
        cut_body,
        sc,
        (1,),
        [
            (weight, block, lambda n, sc: (0, sc[at])),
            (weight, block, lambda n, sc: (0, sc[at + 2])),
        ],
        [(block, BF16, block, first)] * 2,
        through=through,
    )


def pick(sc, whole, lay, through):
    rows, width = lay.rows, whole.shape[1]
    block = (rows, width)
    return call(
        pick_body,
        sc,
        (lay.z - 1,),
        [(whole, block, lambda n, sc: (sc[lay.at_z + 1 + n], 0))],
        [(((lay.z - 1) * rows, width), BF16, block, lambda n, sc: (n, 0))],
        through=through,
    )


def pick_body(sc_ref, in_ref, out_ref):
    out_ref[...] = in_ref[...]


def forward_body(heads, sc_ref, q_ref, k_ref, v_ref, seg_row_ref, seg_col_ref, out_ref, mask_ref):
    @pl.when(pl.program_id(0) == 0)
    def _():
        fill_mask(mask_ref, seg_row_ref, seg_col_ref)

    value_t = v_ref[...].T
    for h in range(heads):
        for start, tile, upto in tiles_of(q_ref.shape[0]):
            probs, _ = softmax_tile(
                k_ref[:upto, :],
                q_ref[start : start + tile, h * DH : (h + 1) * DH],
                mask_ref[:upto, start : start + tile],
            )
            context = dot(value_t[:, :upto], probs.astype(BF16), NN)
            out_ref[h * DH : (h + 1) * DH, start : start + tile] = context.astype(BF16)


def forward(sc, ks, sides, block, lay, through):
    queries, keys, values, seg_row, seg_col = block
    length = queries.shape[0]
    per = lay.heads_shard
    count = len(ks)

    def shard_of(i, sc):
        k = lax.rem(ks[0] + lax.rem(i, count), lay.z)
        if len(sides) == 2:
            own = i >= count
        else:
            own = sides[0] == 1
        return 2 * sc[lay.at_z + k] + jnp.where(own, sc[0], 1 - sc[0])

    def kv_of(i, sc):
        return (0, (shard_of(i, sc) * per) // REPEAT)

    rows = per * DH
    steps = count * len(sides)
    return call(
        functools.partial(forward_body, per),
        sc,
        (steps,),
        [
            (queries, (length, rows), lambda i, sc: (0, shard_of(i, sc))),
            (keys, (length, DH), kv_of),
            (values, (length, DH), kv_of),
            (seg_row, (1, length), first),
            (seg_col, (length, 1), first),
        ],
        [((steps * rows, length), BF16, (rows, length), lambda i, sc: (i, 0))],
        scratch=[pltpu.VMEM((length, length), F32)],
        through=through,
    )


def product_body(count, at_x, at_y, sc_ref, *refs):
    own, other = refs[:count], refs[count : 2 * count]
    u0_ref, u1_ref = refs[2 * count : 2 * count + 2]
    outs, acc_ref = refs[2 * count + 2 : -1], refs[-1]
    n = pl.program_id(0)
    rows = acc_ref.shape[0] // count
    half = rows // 2

    def stack(parts):
        return parts[0][...] if count == 1 else jnp.concatenate([p[...] for p in parts], axis=0)

    acc = dot(stack(own), u0_ref[...], NN) + dot(stack(other), u1_ref[...], NN)
    acc_ref[...] = acc.astype(BF16)

    def split(bit, side):
        for c in range(count):
            send_ref, keep_ref = outs[4 * c + side], outs[4 * c + side + 1]
            stay = pl.multiple_of(c * rows + bit * half, half)
            away = pl.multiple_of(c * rows + (1 - bit) * half, half)
            keep_ref[...] = acc_ref[pl.ds(stay, half), :]
            send_ref[...] = acc_ref[pl.ds(away, half), :]

    @pl.when(n < 2)
    def _():
        split(sc_ref[at_x], 0)

    @pl.when(n >= 2)
    def _():
        split(sc_ref[at_y], 2)


def product(sc, own, other, up0, up1, lay, through):
    length, width = up0.shape
    rows = lay.rows
    tile = width // 4
    count = len(own)
    half, block = (rows // 2, width // 2), (rows // 2, tile)
    left = (half, BF16, block, lambda n, sc: (0, jnp.minimum(n, 1)))
    right = (half, BF16, block, lambda n, sc: (0, jnp.maximum(n - 2, 0)))
    return call(
        functools.partial(product_body, count, lay.at_bit(0), lay.at_bit(lay.bits - 1)),
        sc,
        (4,),
        [(x, (rows, length), lambda n, sc, at=at: (at, 0)) for x, at in (*own, *other)]
        + [(u, (length, tile), lambda n, sc: (0, n)) for u in (up0, up1)],
        [left, left, right, right] * count,
        scratch=[pltpu.VMEM((count * rows, tile), BF16)],
        through=through,
    )


def combine_body(counts, merged, sc_ref, *refs):
    outs = refs[sum(counts) :]
    at = 0
    for side, count in enumerate(counts):
        total = refs[at][...].astype(F32)
        for ref in refs[at + 1 : at + count]:
            total = total + ref[...].astype(F32)
        at += count
        if merged:
            width = total.shape[1]
            outs[0][:, side * width : (side + 1) * width] = total.astype(BF16)
        else:
            outs[side][...] = total.astype(BF16)


def combine(sc, terms, ring, away, merged, lay, through):
    count = len(terms[0])
    deep = count if away else lay.bits
    width = terms[0][0].shape[1]
    size = lay.rows >> deep
    ins, counts = [], []
    for side in range(2):
        order = list(range(lay.bits))
        order = order[::-1] if side else order

        def place(level, order=order):
            def index(n, sc):
                at = 0
                for m in range(level, deep):
                    bit = sc[lay.at_bit(order[m])]
                    bit = 1 - bit if away and m == deep - 1 else bit
                    at = 2 * at + bit
                return (at, 0)

            return index

        for m, x in enumerate(terms[side]):
            ins.append((x, (size, width), place(max(m, 1))))
        if ring is not None:
            ins.append((ring, (size, width), lambda n, sc, side=side: (0, side)))
        counts.append(count + (ring is not None))
    if merged:
        outs = [((size, 2 * width), BF16, (size, 2 * width), first)]
    else:
        outs = [((size, width), BF16, (size, width), first)] * 2
    return call(
        functools.partial(combine_body, counts, merged), sc, (1,), ins, outs, through=through
    )


def grad_context_body(parts, sc_ref, u0_ref, u1_ref, *refs):
    weights, (g0_ref, g1_ref, a0_ref, a1_ref) = refs[:-4], refs[-4:]
    n = pl.program_id(0)

    def add(weight_ref):
        d0 = dot(u0_ref[...], weight_ref[...], NT)
        d1 = dot(u1_ref[...], weight_ref[...], NT)

        @pl.when(n == 0)
        def _():
            a0_ref[...] = d0
            a1_ref[...] = d1

        @pl.when(n > 0)
        def _():
            a0_ref[...] += d0
            a1_ref[...] += d1

    if len(weights) == 1:
        add(weights[0])
    else:
        for p in range(parts):
            pl.when(n == p)(functools.partial(add, weights[p]))

    @pl.when(n == parts - 1)
    def _():
        g0_ref[...] = a0_ref[...].astype(BF16)
        g1_ref[...] = a1_ref[...].astype(BF16)


def grad_context(sc, up0, up1, weights, lay, through):
    length, width = up0.shape
    rows = weights[0].shape[0]
    tile = width // 4
    at = lay.at_piece
    if len(weights) == 1:
        weight_ins = [(weights[0], (rows, tile), lambda n, sc: (0, sc[at + n]))]
    else:
        weight_ins = [(w, (rows, tile), first) for w in weights]
    return call(
        functools.partial(grad_context_body, 4),
        sc,
        (4,),
        [(u, (length, tile), lambda n, sc: (0, sc[at + n])) for u in (up0, up1)] + weight_ins,
        [((length, rows), BF16, (length, rows), first)] * 2,
        scratch=[pltpu.VMEM((length, rows), F32)] * 2,
        through=through,
    )


def backward_body(
    per, sc_ref, q_ref, k_ref, v_ref, seg_row_ref, seg_col_ref, own_ref, other_ref, *refs
):
    gq_ref, gk_ref, gv_ref, mask_ref, ak_ref, av_ref = refs[-6:]
    group = pl.program_id(0)
    parity = sc_ref[0]

    @pl.when(group == 0)
    def _():
        fill_mask(mask_ref, seg_row_ref, seg_col_ref)

    key_t = k_ref[...].T
    ak_ref[...] = jnp.zeros_like(ak_ref)
    av_ref[...] = jnp.zeros_like(av_ref)
    for h in range(REPEAT):
        side = group if per == REPEAT else h
        column = h if per == REPEAT else 0
        cols = slice(column * DH, (column + 1) * DH)
        grad = jnp.where(side == parity, own_ref[:, cols], other_ref[:, cols])
        for start, tile, upto in tiles_of(q_ref.shape[0]):
            query = q_ref[start : start + tile, h * DH : (h + 1) * DH]
            probs, cap_tanh = softmax_tile(
                k_ref[:upto, :], query, mask_ref[:upto, start : start + tile]
            )
            grad_rows = grad[start : start + tile, :]
            grad_probs = dot(v_ref[:upto, :], grad_rows, NT)
            delta = jnp.sum(probs * grad_probs, axis=0, keepdims=True)
            scores = probs * (grad_probs - delta) * (SCALE - SCALE * (cap_tanh * cap_tanh))
            scores = scores.astype(BF16)
            av_ref[:upto, :] += dot(probs.astype(BF16), grad_rows, NN)
            ak_ref[:upto, :] += dot(scores, query, NN)
            grad_query = dot(key_t[:, :upto], scores, NN).T
            gq_ref[start : start + tile, h * DH : (h + 1) * DH] = grad_query.astype(BF16)
    gk_ref[...] = ak_ref[...].astype(BF16)
    gv_ref[...] = av_ref[...].astype(BF16)


def backward(sc, k, block, own, other, column, before, lay, through):
    queries, keys, values, seg_row, seg_col = block
    length = queries.shape[0]
    per = lay.heads_shard
    groups = 2 * per // REPEAT
    at = lay.at_z + k

    def whole(i, sc):
        return (0, sc[at] * groups + i)

    heads = (length, REPEAT * DH), whole
    one = (length, DH), whole
    return call(
        functools.partial(backward_body, per),
        sc,
        (groups,),
        [
            (queries, *heads),
            (keys, *one),
            (values, *one),
            (seg_row, (1, length), first),
            (seg_col, (length, 1), first),
            (own, (length, lay.rows), lambda i, sc: (0, column)),
            (other, (length, lay.rows), lambda i, sc: (0, column)),
        ],
        [(queries.shape, BF16, *heads), (keys.shape, BF16, *one), (values.shape, BF16, *one)],
        scratch=[
            pltpu.VMEM((length, length), F32),
            pltpu.VMEM((length, DH), F32),
            pltpu.VMEM((length, DH), F32),
        ],
        before=before,
        through=through,
    )


def adam_body(pieces, tokens, sc_ref, m1_ref, m2_ref, *refs):
    out_ref = refs[-1]
    n = pl.program_id(0)

    def step(piece_ref):
        gradient = piece_ref[...].astype(F32) * (1.0 / tokens)
        moment_one = 0.9 * m1_ref[...] + 0.1 * gradient
        moment_two = 0.95 * m2_ref[...] + 0.05 * gradient * gradient
        out_ref[...] = moment_one / (jnp.sqrt(moment_two) + 1e-08)

    for p in range(pieces):
        pl.when(n == p)(functools.partial(step, refs[p]))


def adam(sc, pieces, first_moment, second_moment, tokens, lay, before, through):
    rows, width = pieces[0][0].shape
    count = len(pieces)
    places = []
    for _, side, flips in pieces:
        order = list(range(lay.bits))
        order = order[::-1] if side else order
        row = 0
        for b, flip in zip(order, flips):
            bit = sc[lay.at_bit(b)]
            row = 2 * row + (1 - bit if flip else bit)
        places += [row, jnp.int32(side)]
    at = lambda n, at: (at[2 * n], at[2 * n + 1])
    block = (rows, width)
    return call(
        functools.partial(adam_body, count, tokens),
        jnp.stack(places).astype(jnp.int32),
        (count,),
        [(first_moment, block, at), (second_moment, block, at)]
        + [(x, block, first) for x, _, _ in pieces],
        [(first_moment.shape, F32, block, at)],
        before=before,
        through=through,
    )


class Layout:
    def __init__(self, replicas, shards, rows):
        self.replicas, self.shards, self.rows = replicas, shards, rows
        self.z = shards // 2
        self.bits = replicas.bit_length() - 1
        self.heads_shard = HEADS // shards
        self.order = [0] + list(range(1, self.z, 2)) + list(range(self.z - 2, 0, -2))
        self.place = [self.order.index(z) for z in range(self.z)]
        self.at_z = 1
        self.at_piece = self.at_z + self.z
        table = []
        for r in range(replicas):
            bits = [(r >> b) & 1 for b in range(self.bits)]
            x, y = bits[0], bits[-1]
            for s in range(shards):
                z, core = s // 2, s % 2
                zs = [self.order[(self.place[z] - k) % self.z] for k in range(self.z)]
                table.append([core] + zs + [x, 1 - x, 2 + y, 3 - y] + bits)
        self.table = np.array(table, np.int32)

    def at_bit(self, b):
        return self.at_piece + 4 + b

    def sibling(self, x):
        return lax.ppermute(x, "shard", [(s, s ^ 1) for s in range(self.shards)])

    def gather_z(self, x):
        groups = [list(range(core, self.shards, 2)) for core in range(2)]
        return lax.all_gather(x, "shard", axis_index_groups=groups, axis=0, tiled=True)

    def onward(self, x):
        perm = []
        for p in range(self.z):
            a, b = self.order[p], self.order[(p + 1) % self.z]
            perm += [(2 * a + core, 2 * b + core) for core in range(2)]
        return lax.ppermute(x, "shard", perm)

    def across(self, x, b):
        return lax.ppermute(x, "replica", [(r, r ^ (1 << b)) for r in range(self.replicas)])


def per_device(queries, keys, values, segments, out_weight, upstream, first_moment, second_moment):
    length, width = upstream.shape
    lay = Layout(lax.axis_size("replica"), lax.axis_size("shard"), out_weight.shape[0])
    tokens = length * lay.replicas * lay.shards
    device = lax.axis_index("replica") * lay.shards + lax.axis_index("shard")
    sc = lax.dynamic_index_in_dim(jnp.asarray(lay.table), device, 0, keepdims=False)
    orders = [list(range(lay.bits)), list(range(lay.bits))[::-1]]
    block = (queries, keys, values, segments, segments.reshape(length, 1))

    box = {"token": jnp.zeros((8, 128), F32)}
    terms = {}
    ring = {}
    final = []
    grads = ()

    def run(function, *args, held=(), **more):
        names = ["token", *held]
        outs, handed = function(*args, through=[box[n] for n in names], **more)
        box.update(zip(names, handed))
        return outs

    def do_product(k, held=()):
        own, other = contexts[k]
        outs = run(product, sc, [own], [other], upstream, upstream_other, lay, held=held)
        box["send", k, 0], keep_l, box["send", k, 1], keep_r = outs
        terms[k] = [[keep_l], [keep_r]]

    def send(k):
        for side in range(2):
            stage = len(terms[k][side]) - 1
            got = lay.across(box["send", k, side], orders[side][stage])
            terms[k][side].append(got)

    def do_halve(k, held=()):
        for stage in range(1, lay.bits):
            outs = run(combine, sc, terms[k], None, True, False, lay, held=held)
            box["send", k, 0], box["send", k, 1] = outs
            held = ()
            if stage < lay.bits - 1:
                send(k)

    def do_sum(k, held=()):
        outs = run(combine, sc, terms[k], ring.get(k), False, k > 0, lay, held=held)
        if k:
            ring[(k + 1) % lay.z] = lay.onward(outs[0])
        else:
            final.extend(outs)

    def sends(k):
        return [("send", k, 0), ("send", k, 1)]

    def do_backward(k, gc, column, held=()):
        nonlocal grads
        grads = run(backward, sc, k, block, *gc, column, grads, lay, held=held)

    upstream_other = lay.sibling(upstream)
    gathered = [lay.gather_z(x) for x in run(cut, sc, out_weight, lay)]

    late = [*range(2, lay.z), 0]
    contexts = {}
    (both_sides,) = run(forward, sc, [1], [0, 1], block, lay)
    rows = lay.rows
    contexts[1] = (both_sides, 1), (lay.sibling(both_sides[:rows]), 0)
    (away,) = run(forward, sc, late, [0], block, lay)
    away = lay.sibling(away)
    do_product(1)
    send(1)
    (stay,) = run(forward, sc, late, [1], block, lay)
    for n, k in enumerate(late):
        contexts[k] = (stay, n), (away, n)
    do_product(2)
    send(2)
    do_halve(1)
    send(1)
    own, away = run(grad_context, sc, upstream, upstream_other, [out_weight], lay)
    gc = own, lay.sibling(away)
    do_product(3)
    do_halve(2, held=sends(3))
    send(3)
    do_backward(0, gc, 0)
    do_sum(1, held=sends(2))
    send(2)
    do_product(0)
    for k in range(4, lay.z):
        do_product(k)
        send(k)
    for k in range(3, lay.z):
        do_halve(k)
        send(k)
    do_sum(2)
    mine = [run(pick, sc, whole, lay)[0] for whole in gathered]
    weights = [mine[0], lay.across(mine[0], orders[0][0]), mine[1], lay.across(mine[1], orders[1][0])]
    for k in range(3, lay.z):
        do_sum(k, held=sends(0) if k == lay.z - 1 else ())
    send(0)
    own, away = run(grad_context, sc, upstream, upstream_other, weights, lay)
    gc = own, lay.sibling(away)
    do_halve(0)
    send(0)
    for k in range(1, lay.z - 2):
        do_backward(k, gc, k - 1)
    do_sum(0)

    have = [[(final[side], side, (False,) * lay.bits)] for side in range(2)]

    def spread(n, side, piece):
        x, _, flips = piece
        flips = flips[:n] + (True,) + flips[n + 1 :]
        return lay.across(x, orders[side][n]), side, flips

    moments = first_moment, second_moment, tokens, lay
    near, far = [], []
    for n in range(lay.bits - 1, -1, -1):
        for side in range(2):
            have[side].append(spread(n, side, have[side][0]))
    do_backward(lay.z - 2, gc, lay.z - 3)
    for side in range(2):
        box["got", side] = have[side][1][0]
    step = run(
        adam,
        sc,
        [have[0][0], have[1][0]],
        *moments,
        before=(),
        held=[("got", 0), ("got", 1)],
    )
    for side in range(2):
        have[side][1] = (box["got", side], *have[side][1][1:])
        pieces = [have[side][1]]
        done = {p[2] for p in have[side]}
        near += have[side][1:]
        for n in range(lay.bits - 2, -1, -1):
            base = [have[side][m] for m in range(1, lay.bits) if m <= lay.bits - 1 - n]
            base += [p for s, p in far if s == side]
            for p in base:
                flips = p[2][:n] + (True,) + p[2][n + 1 :]
                if flips not in done:
                    done.add(flips)
                    far.append((side, spread(n, side, p)))
    do_backward(lay.z - 1, gc, lay.z - 2)
    step = run(adam, sc, near, *moments, before=step)
    step = run(adam, sc, [p for _, p in far], *moments, before=step)
    return (*grads, *step)


def solution(mesh):
    both = P(("replica", "shard"), None)
    shard = P("shard", None)
    return jax.shard_map(
        per_device,
        mesh=mesh,
        in_specs=(both, both, both, both, shard, both, shard, shard),
        out_specs=(both, both, both, shard),
        check_vma=False,
    )
```

```python
import functools

import jax
import jax.numpy as jnp
import numpy as np
from jax import lax
from jax.experimental import pallas as pl
from jax.experimental.pallas import tpu as pltpu
from jax.sharding import PartitionSpec as P

HEADS = 16
KV_HEADS = 8
DH = 128
REPEAT = HEADS // KV_HEADS

SCALE = 1.0 / 12.0
CAP = 50.0
MIB = 1024 * 1024
F32 = jnp.float32
BF16 = jnp.bfloat16

NT = (((1,), (1,)), ((), ()))
NN = (((1,), (0,)), ((), ()))


def dot(a, b, dims):
    return lax.dot_general(a, b, dims, preferred_element_type=F32)


def call(body, sc, grid, ins, outs, scratch=(), through=(), before=(), mib=20):
    n_in, n_out, n_before, n_through = len(ins), len(outs), len(before), len(through)

    def kernel(sc_ref, *refs):
        at = n_in + n_before + n_through
        body(sc_ref, *refs[:n_in], *refs[at : at + n_out], *refs[at + n_out + n_through :])

    anywhere = pl.BlockSpec(memory_space=pl.ANY)
    stay = pl.BlockSpec(memory_space=pltpu.HBM)
    aliases = {1 + n_in + n: n for n in range(n_before)}
    aliases.update({1 + n_in + n_before + n: n_out + n for n in range(n_through)})
    results = pl.pallas_call(
        kernel,
        grid_spec=pltpu.PrefetchScalarGridSpec(
            num_scalar_prefetch=1,
            grid=grid,
            in_specs=[pl.BlockSpec(block, index) for _, block, index in ins]
            + [anywhere] * n_before
            + [stay] * n_through,
            out_specs=[pl.BlockSpec(block, index) for _, _, block, index in outs]
            + [stay] * n_through,
            scratch_shapes=list(scratch),
        ),
        out_shape=[jax.ShapeDtypeStruct(shape, dtype) for shape, dtype, _, _ in outs]
        + [jax.ShapeDtypeStruct(x.shape, x.dtype) for x in through],
        input_output_aliases=aliases,
        cost_estimate=pl.CostEstimate(flops=1, transcendentals=0, bytes_accessed=1),
        compiler_params=pltpu.CompilerParams(vmem_limit_bytes=mib * MIB),
    )(sc, *[array for array, _, _ in ins], *before, *through)
    return results[:n_out], results[n_out:]


def first(*_):
    return (0, 0)


def fill_mask(mask_ref, seg_row_ref, seg_col_ref):
    length = mask_ref.shape[0]
    j = lax.broadcasted_iota(jnp.int32, (length, length), 0)
    i = lax.broadcasted_iota(jnp.int32, (length, length), 1)
    allowed = (j <= i) & (seg_col_ref[...] == seg_row_ref[...])
    mask_ref[...] = jnp.where(allowed, 1.0, 0.0).astype(F32)


def tiles_of(length):
    tile = 256
    return [(t * tile, tile, (t + 1) * tile) for t in range(length // tile)]


def softmax_tile(key, query, mask):
    cap_tanh = jnp.tanh(dot(key, query, NT) * (SCALE / CAP))
    weights = jnp.exp(cap_tanh * CAP) * mask
    inverse = 1.0 / jnp.sum(weights, axis=0, keepdims=True)
    return weights * inverse, cap_tanh


def cut_body(sc_ref, a_ref, b_ref, x_ref, y_ref, token_ref):
    x_ref[...] = a_ref[...]
    y_ref[...] = b_ref[...]
    token_ref[...] = jnp.zeros_like(token_ref)


def cut(sc, weight, lay):
    rows, width = weight.shape
    block = (rows, width // 4)
    at = lay.at_piece
    return call(
        cut_body,
        sc,
        (1,),
        [
            (weight, block, lambda n, sc: (0, sc[at])),
            (weight, block, lambda n, sc: (0, sc[at + 2])),
        ],
        [(block, BF16, block, first)] * 2 + [((8, 128), F32, (8, 128), first)],
    )


def pack(sc, parts, lay, through):
    rows, width = parts[0].shape
    block = (rows, width)
    return call(
        functools.partial(pack_body, len(parts)),
        sc,
        (len(parts),),
        [(x, block, first) for x in parts],
        [((len(parts) * rows, width), BF16, block, lambda n, sc: (n, 0))],
        through=through,
    )


def pack_body(count, sc_ref, *refs):
    def copy(p):
        refs[-1][...] = refs[p][...]

    for p in range(count):
        pl.when(pl.program_id(0) == p)(functools.partial(copy, p))


def pick(sc, whole, lay, through):
    rows, width = lay.rows, whole.shape[1]
    block = (rows, width)
    return call(
        pick_body,
        sc,
        (lay.z - 1,),
        [(whole, block, lambda n, sc: (sc[lay.at_z + 1 + n], 0))],
        [(((lay.z - 1) * rows, width), BF16, block, lambda n, sc: (n, 0))],
        through=through,
    )


def pick_body(sc_ref, in_ref, out_ref):
    out_ref[...] = in_ref[...]


def forward_body(heads, sc_ref, q_ref, k_ref, v_ref, seg_row_ref, seg_col_ref, out_ref, mask_ref):
    @pl.when(pl.program_id(0) == 0)
    def _():
        fill_mask(mask_ref, seg_row_ref, seg_col_ref)

    value_t = v_ref[...].T
    for h in range(heads):
        for start, tile, upto in tiles_of(q_ref.shape[0]):
            probs, _ = softmax_tile(
                k_ref[:upto, :],
                q_ref[start : start + tile, h * DH : (h + 1) * DH],
                mask_ref[:upto, start : start + tile],
            )
            context = dot(value_t[:, :upto], probs.astype(BF16), NN)
            out_ref[h * DH : (h + 1) * DH, start : start + tile] = context.astype(BF16)


def forward(sc, ks, sides, block, lay, through):
    queries, keys, values, seg_row, seg_col = block
    length = queries.shape[0]
    per = lay.heads_shard
    count = len(ks)

    def shard_of(i, sc):
        k = lax.rem(ks[0] + lax.rem(i, count), lay.z)
        if len(sides) == 2:
            own = i >= count
        else:
            own = sides[0] == 1
        return 2 * sc[lay.at_z + k] + jnp.where(own, sc[0], 1 - sc[0])

    def kv_of(i, sc):
        return (0, (shard_of(i, sc) * per) // REPEAT)

    rows = per * DH
    steps = count * len(sides)
    return call(
        functools.partial(forward_body, per),
        sc,
        (steps,),
        [
            (queries, (length, rows), lambda i, sc: (0, shard_of(i, sc))),
            (keys, (length, DH), kv_of),
            (values, (length, DH), kv_of),
            (seg_row, (1, length), first),
            (seg_col, (length, 1), first),
        ],
        [((steps * rows, length), BF16, (rows, length), lambda i, sc: (i, 0))],
        scratch=[pltpu.VMEM((length, length), F32)],
        through=through,
    )


def product_body(count, at_x, at_y, sc_ref, *refs):
    own, other = refs[:count], refs[count : 2 * count]
    u0_ref, u1_ref = refs[2 * count : 2 * count + 2]
    outs, acc_ref = refs[2 * count + 2 : -1], refs[-1]
    n = pl.program_id(0)
    rows = acc_ref.shape[0] // count
    half = rows // 2

    def stack(parts):
        return parts[0][...] if count == 1 else jnp.concatenate([p[...] for p in parts], axis=0)

    acc = dot(stack(own), u0_ref[...], NN) + dot(stack(other), u1_ref[...], NN)
    acc_ref[...] = acc.astype(BF16)

    def split(bit, side):
        for c in range(count):
            send_ref, keep_ref = outs[4 * c + side], outs[4 * c + side + 1]
            stay = pl.multiple_of(c * rows + bit * half, half)
            away = pl.multiple_of(c * rows + (1 - bit) * half, half)
            keep_ref[...] = acc_ref[pl.ds(stay, half), :]
            send_ref[...] = acc_ref[pl.ds(away, half), :]

    @pl.when(n < 2)
    def _():
        split(sc_ref[at_x], 0)

    @pl.when(n >= 2)
    def _():
        split(sc_ref[at_y], 2)


def product(sc, own, other, up0, up1, lay, through):
    length, width = up0.shape
    rows = lay.rows
    tile = width // 4
    count = len(own)
    half, block = (rows // 2, width // 2), (rows // 2, tile)
    left = (half, BF16, block, lambda n, sc: (0, jnp.minimum(n, 1)))
    right = (half, BF16, block, lambda n, sc: (0, jnp.maximum(n - 2, 0)))
    return call(
        functools.partial(product_body, count, lay.at_bit(0), lay.at_bit(lay.bits - 1)),
        sc,
        (4,),
        [(x, (rows, length), lambda n, sc, at=at: (at, 0)) for x, at in (*own, *other)]
        + [(u, (length, tile), lambda n, sc: (0, n)) for u in (up0, up1)],
        [left, left, right, right] * count,
        scratch=[pltpu.VMEM((count * rows, tile), BF16)],
        through=through,
    )


def combine_body(counts, merged, sc_ref, *refs):
    outs = refs[sum(counts) :]
    at = 0
    for side, count in enumerate(counts):
        total = refs[at][...].astype(F32)
        for ref in refs[at + 1 : at + count]:
            total = total + ref[...].astype(F32)
        at += count
        if merged:
            width = total.shape[1]
            outs[0][:, side * width : (side + 1) * width] = total.astype(BF16)
        else:
            outs[side][...] = total.astype(BF16)


def combine(sc, terms, ring, away, merged, lay, through):
    count = len(terms[0])
    deep = count if away else lay.bits
    width = terms[0][0].shape[1]
    size = lay.rows >> deep
    ins, counts = [], []
    for side in range(2):
        order = list(range(lay.bits))
        order = order[::-1] if side else order

        def place(level, order=order):
            def index(n, sc):
                at = 0
                for m in range(level, deep):
                    bit = sc[lay.at_bit(order[m])]
                    bit = 1 - bit if away and m == deep - 1 else bit
                    at = 2 * at + bit
                return (at, 0)

            return index

        for m, x in enumerate(terms[side]):
            ins.append((x, (size, width), place(max(m, 1))))
        if ring is not None:
            ins.append((ring, (size, width), lambda n, sc, side=side: (0, side)))
        counts.append(count + (ring is not None))
    if merged:
        outs = [((size, 2 * width), BF16, (size, 2 * width), first)]
    else:
        outs = [((size, width), BF16, (size, width), first)] * 2
    return call(
        functools.partial(combine_body, counts, merged), sc, (1,), ins, outs, through=through
    )


def grad_context_body(parts, sc_ref, u0_ref, u1_ref, *refs):
    weights, (g0_ref, g1_ref, a0_ref, a1_ref) = refs[:-4], refs[-4:]
    n = pl.program_id(0)

    def add(weight_ref):
        d0 = dot(u0_ref[...], weight_ref[...], NT)
        d1 = dot(u1_ref[...], weight_ref[...], NT)

        @pl.when(n == 0)
        def _():
            a0_ref[...] = d0
            a1_ref[...] = d1

        @pl.when(n > 0)
        def _():
            a0_ref[...] += d0
            a1_ref[...] += d1

    if len(weights) == 1:
        add(weights[0])
    else:
        for p in range(parts):
            pl.when(n == p)(functools.partial(add, weights[p]))

    @pl.when(n == parts - 1)
    def _():
        g0_ref[...] = a0_ref[...].astype(BF16)
        g1_ref[...] = a1_ref[...].astype(BF16)


def grad_context(sc, up0, up1, weights, lay, through):
    length, width = up0.shape
    rows = weights[0].shape[0]
    tile = width // 4
    at = lay.at_piece
    if len(weights) == 1:
        weight_ins = [(weights[0], (rows, tile), lambda n, sc: (0, sc[at + n]))]
    else:
        weight_ins = [(w, (rows, tile), first) for w in weights]
    return call(
        functools.partial(grad_context_body, 4),
        sc,
        (4,),
        [(u, (length, tile), lambda n, sc: (0, sc[at + n])) for u in (up0, up1)] + weight_ins,
        [((length, rows), BF16, (length, rows), first)] * 2,
        scratch=[pltpu.VMEM((length, rows), F32)] * 2,
        through=through,
        mib=20 if len(weights) == 1 else 36,
    )


def backward_body(
    per, sc_ref, q_ref, k_ref, v_ref, seg_row_ref, seg_col_ref, own_ref, other_ref, *refs
):
    gq_ref, gk_ref, gv_ref, mask_ref, ak_ref, av_ref = refs[-6:]
    group = pl.program_id(0)
    parity = sc_ref[0]

    @pl.when(group == 0)
    def _():
        fill_mask(mask_ref, seg_row_ref, seg_col_ref)

    key_t = k_ref[...].T
    ak_ref[...] = jnp.zeros_like(ak_ref)
    av_ref[...] = jnp.zeros_like(av_ref)
    for h in range(REPEAT):
        side = group if per == REPEAT else h
        column = h if per == REPEAT else 0
        cols = slice(column * DH, (column + 1) * DH)
        grad = jnp.where(side == parity, own_ref[:, cols], other_ref[:, cols])
        for start, tile, upto in tiles_of(q_ref.shape[0]):
            query = q_ref[start : start + tile, h * DH : (h + 1) * DH]
            probs, cap_tanh = softmax_tile(
                k_ref[:upto, :], query, mask_ref[:upto, start : start + tile]
            )
            grad_rows = grad[start : start + tile, :]
            grad_probs = dot(v_ref[:upto, :], grad_rows, NT)
            delta = jnp.sum(probs * grad_probs, axis=0, keepdims=True)
            scores = probs * (grad_probs - delta) * (SCALE - SCALE * (cap_tanh * cap_tanh))
            scores = scores.astype(BF16)
            av_ref[:upto, :] += dot(probs.astype(BF16), grad_rows, NN)
            ak_ref[:upto, :] += dot(scores, query, NN)
            grad_query = dot(key_t[:, :upto], scores, NN).T
            gq_ref[start : start + tile, h * DH : (h + 1) * DH] = grad_query.astype(BF16)
    gk_ref[...] = ak_ref[...].astype(BF16)
    gv_ref[...] = av_ref[...].astype(BF16)


def backward(sc, k, block, own, other, column, before, lay, through):
    queries, keys, values, seg_row, seg_col = block
    length = queries.shape[0]
    per = lay.heads_shard
    groups = 2 * per // REPEAT
    at = lay.at_z + k

    def whole(i, sc):
        return (0, sc[at] * groups + i)

    heads = (length, REPEAT * DH), whole
    one = (length, DH), whole
    return call(
        functools.partial(backward_body, per),
        sc,
        (groups,),
        [
            (queries, *heads),
            (keys, *one),
            (values, *one),
            (seg_row, (1, length), first),
            (seg_col, (length, 1), first),
            (own, (length, lay.rows), lambda i, sc: (0, column)),
            (other, (length, lay.rows), lambda i, sc: (0, column)),
        ],
        [(queries.shape, BF16, *heads), (keys.shape, BF16, *one), (values.shape, BF16, *one)],
        scratch=[
            pltpu.VMEM((length, length), F32),
            pltpu.VMEM((length, DH), F32),
            pltpu.VMEM((length, DH), F32),
        ],
        before=before,
        through=through,
    )


def adam_body(pieces, tokens, sc_ref, m1_ref, m2_ref, *refs):
    out_ref = refs[-1]
    n = pl.program_id(0)

    def step(piece_ref):
        gradient = piece_ref[...].astype(F32) * (1.0 / tokens)
        moment_one = 0.9 * m1_ref[...] + 0.1 * gradient
        moment_two = 0.95 * m2_ref[...] + 0.05 * gradient * gradient
        out_ref[...] = moment_one / (jnp.sqrt(moment_two) + 1e-08)

    for p in range(pieces):
        pl.when(n == p)(functools.partial(step, refs[p]))


def adam(sc, pieces, first_moment, second_moment, tokens, lay, before, through):
    rows, width = pieces[0][0].shape
    count = len(pieces)
    columns = [lay.at_place(side, flips) for _, side, flips in pieces]

    def at(n, sc):
        row, side = sc[columns[0]], pieces[0][1]
        for p in range(1, count):
            row = jnp.where(n == p, sc[columns[p]], row)
            side = jnp.where(n == p, pieces[p][1], side)
        return (row, side)

    block = (rows, width)
    return call(
        functools.partial(adam_body, count, tokens),
        sc,
        (count,),
        [(first_moment, block, at), (second_moment, block, at)]
        + [(x, block, first) for x, _, _ in pieces],
        [(first_moment.shape, F32, block, at)],
        before=before,
        through=through,
        mib=60,
    )


class Layout:
    def __init__(self, replicas, shards, rows):
        self.replicas, self.shards, self.rows = replicas, shards, rows
        self.z = shards // 2
        self.bits = replicas.bit_length() - 1
        self.heads_shard = HEADS // shards
        self.order = [0] + list(range(1, self.z, 2)) + list(range(self.z - 2, 0, -2))
        self.place = [self.order.index(z) for z in range(self.z)]
        self.at_z = 1
        self.at_piece = self.at_z + self.z
        table = []
        for r in range(replicas):
            bits = [(r >> b) & 1 for b in range(self.bits)]
            x, y = bits[0], bits[-1]
            for s in range(shards):
                z, core = s // 2, s % 2
                zs = [self.order[(self.place[z] - k) % self.z] for k in range(self.z)]
                row = [core] + zs + [x, 1 - x, 2 + y, 3 - y] + bits
                for order in (bits, bits[::-1]):
                    here = sum(b << n for n, b in enumerate(order[::-1]))
                    row += [here ^ flips for flips in range(replicas)]
                table.append(row)
        self.table = np.array(table, np.int32)

    def at_bit(self, b):
        return self.at_piece + 4 + b

    def sibling(self, x):
        return lax.ppermute(x, "shard", [(s, s ^ 1) for s in range(self.shards)])

    def at_place(self, side, flips):
        code = sum(int(f) << n for n, f in enumerate(flips[::-1]))
        return self.at_piece + 4 + self.bits + side * self.replicas + code

    def gather_z(self, x):
        groups = [list(range(core, self.shards, 2)) for core in range(2)]
        return lax.all_gather(x, "shard", axis_index_groups=groups, axis=0, tiled=True)

    def onward(self, x):
        perm = []
        for p in range(self.z):
            a, b = self.order[p], self.order[(p + 1) % self.z]
            perm += [(2 * a + core, 2 * b + core) for core in range(2)]
        return lax.ppermute(x, "shard", perm)

    def across(self, x, b):
        return lax.ppermute(x, "replica", [(r, r ^ (1 << b)) for r in range(self.replicas)])


def per_device(queries, keys, values, segments, out_weight, upstream, first_moment, second_moment):
    length, width = upstream.shape
    lay = Layout(lax.axis_size("replica"), lax.axis_size("shard"), out_weight.shape[0])
    tokens = length * lay.replicas * lay.shards
    device = lax.axis_index("replica") * lay.shards + lax.axis_index("shard")
    sc = lax.dynamic_index_in_dim(jnp.asarray(lay.table), device, 0, keepdims=False)
    orders = [list(range(lay.bits)), list(range(lay.bits))[::-1]]
    block = (queries, keys, values, segments, segments.reshape(length, 1))

    box = {}
    terms = {}
    ring = {}
    final = []
    grads = ()

    def run(function, *args, held=(), **more):
        names = ["token", *held]
        outs, handed = function(*args, through=[box[n] for n in names], **more)
        box.update(zip(names, handed))
        return outs

    def do_product(k, held=()):
        own, other = contexts[k]
        outs = run(product, sc, [own], [other], upstream, upstream_other, lay, held=held)
        box["send", k, 0], keep_l, box["send", k, 1], keep_r = outs
        terms[k] = [[keep_l], [keep_r]]

    def send(k):
        for side in range(2):
            stage = len(terms[k][side]) - 1
            got = lay.across(box["send", k, side], orders[side][stage])
            terms[k][side].append(got)

    def do_halve(k, held=()):
        for stage in range(1, lay.bits):
            outs = run(combine, sc, terms[k], None, True, False, lay, held=held)
            box["send", k, 0], box["send", k, 1] = outs
            held = ()
            if stage < lay.bits - 1:
                send(k)

    def do_sum(k, held=()):
        outs = run(combine, sc, terms[k], ring.get(k), False, k > 0, lay, held=held)
        if k:
            ring[(k + 1) % lay.z] = lay.onward(outs[0])
        else:
            final.extend(outs)

    def sends(k):
        return [("send", k, 0), ("send", k, 1)]

    def do_backward(k, gc, column, held=()):
        nonlocal grads
        grads = run(backward, sc, k, block, *gc, column, grads, lay, held=held)

    upstream_other = lay.sibling(upstream)
    part_x, part_y, box["token"] = cut(sc, out_weight, lay)[0]
    gathered = lay.gather_z(part_x)
    box["ring", 1] = lay.onward(part_y)

    def relay(k):
        if k + 1 < lay.z:
            box["ring", k + 1] = lay.onward(box["ring", k])

    late = [*range(2, lay.z), 0]
    contexts = {}
    (both_sides,) = run(forward, sc, [1], [0, 1], block, lay)
    rows = lay.rows
    contexts[1] = (both_sides, 1), (lay.sibling(both_sides[:rows]), 0)
    (away,) = run(forward, sc, late, [0], block, lay)
    away = lay.sibling(away)
    do_product(1)
    send(1)
    (stay,) = run(forward, sc, late, [1], block, lay, held=[("ring", 1)])
    relay(1)
    for n, k in enumerate(late):
        contexts[k] = (stay, n), (away, n)
    do_product(2)
    send(2)
    do_halve(1, held=[("ring", 2)])
    relay(2)
    send(1)
    do_product(3)
    do_halve(2, held=sends(3))
    send(3)
    own, away = run(
        grad_context, sc, upstream, upstream_other, [out_weight], lay, held=[("ring", 3)]
    )
    relay(3)
    box["gc"] = lay.sibling(away)
    do_sum(1, held=[*sends(2), "gc"])
    send(2)
    do_backward(0, (own, box["gc"]), 0)
    do_product(0)
    for k in range(4, lay.z):
        do_product(k, held=[("ring", k)])
        relay(k)
        send(k)
    for k in range(3, lay.z):
        do_halve(k)
        send(k)
    (mine_y,) = run(pack, sc, [box["ring", k] for k in range(1, lay.z)], lay)
    do_sum(2)
    (mine_x,) = run(pick, sc, gathered, lay)
    weights = [
        mine_x,
        lay.across(mine_x, orders[0][0]),
        mine_y,
        lay.across(mine_y, orders[1][0]),
    ]
    for k in range(3, lay.z):
        do_sum(k, held=sends(0) if k == lay.z - 1 else ())
    send(0)
    own, away = run(grad_context, sc, upstream, upstream_other, weights, lay)
    gc = own, lay.sibling(away)
    do_halve(0)
    send(0)
    for k in range(1, lay.z - 2):
        do_backward(k, gc, k - 1)
    do_sum(0)

    have = [[(final[side], side, (False,) * lay.bits)] for side in range(2)]

    def spread(n, side, piece):
        x, _, flips = piece
        flips = flips[:n] + (True,) + flips[n + 1 :]
        return lay.across(x, orders[side][n]), side, flips

    moments = first_moment, second_moment, tokens, lay
    near, far = [], []
    for n in range(lay.bits - 1, -1, -1):
        for side in range(2):
            have[side].append(spread(n, side, have[side][0]))
    do_backward(lay.z - 2, gc, lay.z - 3)
    for side in range(2):
        box["got", side] = have[side][1][0]
    step = run(
        adam,
        sc,
        [have[0][0], have[1][0]],
        *moments,
        before=(),
        held=[("got", 0), ("got", 1)],
    )
    for side in range(2):
        have[side][1] = (box["got", side], *have[side][1][1:])
        done = {p[2] for p in have[side]}
        near += have[side][1:]
        for n in range(lay.bits - 2, -1, -1):
            base = [have[side][m] for m in range(1, lay.bits) if m <= lay.bits - 1 - n]
            base += [p for s, p in far if s == side]
            for p in base:
                flips = p[2][:n] + (True,) + p[2][n + 1 :]
                if flips not in done:
                    done.add(flips)
                    far.append((side, spread(n, side, p)))
    do_backward(lay.z - 1, gc, lay.z - 2)
    step = run(adam, sc, near, *moments, before=step)
    step = run(adam, sc, [p for _, p in far], *moments, before=step)
    return (*grads, *step)


def solution(mesh):
    both = P(("replica", "shard"), None)
    shard = P("shard", None)
    return jax.shard_map(
        per_device,
        mesh=mesh,
        in_specs=(both, both, both, both, shard, both, shard, shard),
        out_specs=(both, both, both, shard),
        check_vma=False,
    )
```

```python
import functools

import jax
import jax.numpy as jnp
import numpy as np
from jax import lax
from jax.experimental import pallas as pl
from jax.experimental.pallas import tpu as pltpu
from jax.sharding import PartitionSpec as P

HEADS = 16
KV_HEADS = 8
DH = 128
REPEAT = HEADS // KV_HEADS

SCALE = 1.0 / 12.0
CAP = 50.0
MIB = 1024 * 1024
F32 = jnp.float32
BF16 = jnp.bfloat16

NT = (((1,), (1,)), ((), ()))
NN = (((1,), (0,)), ((), ()))


def dot(a, b, dims):
    return lax.dot_general(a, b, dims, preferred_element_type=F32)


def call(body, sc, grid, ins, outs, scratch=(), through=(), before=(), mib=20):
    n_in, n_out, n_before, n_through = len(ins), len(outs), len(before), len(through)

    def kernel(sc_ref, *refs):
        at = n_in + n_before + n_through
        body(sc_ref, *refs[:n_in], *refs[at : at + n_out], *refs[at + n_out + n_through :])

    anywhere = pl.BlockSpec(memory_space=pl.ANY)
    stay = pl.BlockSpec(memory_space=pltpu.HBM)
    aliases = {1 + n_in + n: n for n in range(n_before)}
    aliases.update({1 + n_in + n_before + n: n_out + n for n in range(n_through)})
    results = pl.pallas_call(
        kernel,
        grid_spec=pltpu.PrefetchScalarGridSpec(
            num_scalar_prefetch=1,
            grid=grid,
            in_specs=[pl.BlockSpec(block, index) for _, block, index in ins]
            + [anywhere] * n_before
            + [stay] * n_through,
            out_specs=[pl.BlockSpec(block, index) for _, _, block, index in outs]
            + [stay] * n_through,
            scratch_shapes=list(scratch),
        ),
        out_shape=[jax.ShapeDtypeStruct(shape, dtype) for shape, dtype, _, _ in outs]
        + [jax.ShapeDtypeStruct(x.shape, x.dtype) for x in through],
        input_output_aliases=aliases,
        cost_estimate=pl.CostEstimate(flops=1, transcendentals=0, bytes_accessed=1),
        compiler_params=pltpu.CompilerParams(vmem_limit_bytes=mib * MIB),
    )(sc, *[array for array, _, _ in ins], *before, *through)
    return results[:n_out], results[n_out:]


def first(*_):
    return (0, 0)


def fill_mask(mask_ref, seg_row_ref, seg_col_ref):
    length = mask_ref.shape[0]
    j = lax.broadcasted_iota(jnp.int32, (length, length), 0)
    i = lax.broadcasted_iota(jnp.int32, (length, length), 1)
    allowed = (j <= i) & (seg_col_ref[...] == seg_row_ref[...])
    mask_ref[...] = jnp.where(allowed, 1.0, 0.0).astype(F32)


def tiles_of(length):
    tile = 256
    return [(t * tile, tile, (t + 1) * tile) for t in range(length // tile)]


def softmax_tile(key, query, mask):
    cap_tanh = jnp.tanh(dot(key, query, NT) * (SCALE / CAP))
    weights = jnp.exp(cap_tanh * CAP) * mask
    inverse = 1.0 / jnp.sum(weights, axis=0, keepdims=True)
    return weights * inverse, cap_tanh


def cut_body(sc_ref, in_ref, out_ref, token_ref):
    out_ref[...] = in_ref[...]
    token_ref[...] = jnp.zeros_like(token_ref)


def cut(sc, weight, lay):
    block = (weight.shape[0], weight.shape[1] // 2)
    return call(
        cut_body,
        sc,
        (1,),
        [(weight, block, lambda n, sc: (0, sc[lay.at_bit(0)]))],
        [(block, BF16, block, first), ((8, 128), F32, (8, 128), first)],
    )


def forward_body(heads, sc_ref, q_ref, k_ref, v_ref, seg_row_ref, seg_col_ref, out_ref, mask_ref):
    @pl.when(pl.program_id(0) == 0)
    def _():
        fill_mask(mask_ref, seg_row_ref, seg_col_ref)

    value_t = v_ref[...].T
    for h in range(heads):
        for start, tile, upto in tiles_of(q_ref.shape[0]):
            probs, _ = softmax_tile(
                k_ref[:upto, :],
                q_ref[start : start + tile, h * DH : (h + 1) * DH],
                mask_ref[:upto, start : start + tile],
            )
            context = dot(value_t[:, :upto], probs.astype(BF16), NN)
            out_ref[h * DH : (h + 1) * DH, start : start + tile] = context.astype(BF16)


def forward(sc, ks, sides, block, lay, through):
    queries, keys, values, seg_row, seg_col = block
    length = queries.shape[0]
    per = lay.heads_shard
    count = len(ks)

    def shard_of(i, sc):
        k = lax.rem(ks[0] + lax.rem(i, count), lay.z)
        if len(sides) == 2:
            own = i >= count
        else:
            own = sides[0] == 1
        return 2 * sc[lay.at_z + k] + jnp.where(own, sc[0], 1 - sc[0])

    def kv_of(i, sc):
        return (0, (shard_of(i, sc) * per) // REPEAT)

    rows = per * DH
    steps = count * len(sides)
    return call(
        functools.partial(forward_body, per),
        sc,
        (steps,),
        [
            (queries, (length, rows), lambda i, sc: (0, shard_of(i, sc))),
            (keys, (length, DH), kv_of),
            (values, (length, DH), kv_of),
            (seg_row, (1, length), first),
            (seg_col, (length, 1), first),
        ],
        [((steps * rows, length), BF16, (rows, length), lambda i, sc: (i, 0))],
        scratch=[pltpu.VMEM((length, length), F32)],
        through=through,
    )


def product_body(at_bit, sc_ref, c0_ref, c1_ref, u0_ref, u1_ref, send_ref, keep_ref, acc_ref):
    half = acc_ref.shape[0] // 2
    acc = dot(c0_ref[...], u0_ref[...], NN) + dot(c1_ref[...], u1_ref[...], NN)
    acc_ref[...] = acc.astype(BF16)
    bit = sc_ref[at_bit]
    keep_ref[...] = acc_ref[pl.ds(pl.multiple_of(bit * half, half), half), :]
    send_ref[...] = acc_ref[pl.ds(pl.multiple_of((1 - bit) * half, half), half), :]


def product(sc, own, other, up0, up1, lay, through):
    length, width = up0.shape
    rows = lay.rows
    tile = width // 4
    out = ((rows // 2, width), BF16, (rows // 2, tile), lambda n, sc: (0, n))
    return call(
        functools.partial(product_body, lay.at_bit(0)),
        sc,
        (4,),
        [(x, (rows, length), lambda n, sc, at=at: (at, 0)) for x, at in (own, other)]
        + [(u, (length, tile), lambda n, sc: (0, n)) for u in (up0, up1)],
        [out, out],
        scratch=[pltpu.VMEM((rows, tile), BF16)],
        through=through,
    )


def combine_body(sc_ref, *refs):
    total = refs[0][...].astype(F32)
    for ref in refs[1:-1]:
        total = total + ref[...].astype(F32)
    refs[-1][...] = total.astype(BF16)


def combine(sc, terms, ring, away, lay, through):
    deep = len(terms) if away else lay.bits
    width = terms[0].shape[1]
    size = lay.rows >> deep
    ins = []

    def place(level):
        def index(n, sc):
            at = 0
            for m in range(level, deep):
                bit = sc[lay.at_bit(m)]
                at = 2 * at + (1 - bit if away and m == deep - 1 else bit)
            return (at, 0)

        return index

    for m, x in enumerate(terms):
        ins.append((x, (size, width), place(max(m, 1))))
    if ring is not None:
        ins.append((ring, (size, width), first))
    out = ((size, width), BF16, (size, width), first)
    return call(combine_body, sc, (1,), ins, [out], through=through)


def grad_context_body(sets, sc_ref, u0_ref, u1_ref, *refs):
    weights, (g0_ref, g1_ref, a0_ref, a1_ref) = refs[:-4], refs[-4:]
    n = pl.program_id(0)
    rows = a0_ref.shape[1] // len(sets)

    def add(weight_ref, cols):
        d0 = dot(u0_ref[...], weight_ref[...], NT)
        d1 = dot(u1_ref[...], weight_ref[...], NT)

        @pl.when(n == 0)
        def _():
            a0_ref[:, cols] = d0
            a1_ref[:, cols] = d1

        @pl.when(n > 0)
        def _():
            a0_ref[:, cols] += d0
            a1_ref[:, cols] += d1

    at = 0
    for index, count in enumerate(sets):
        cols = slice(index * rows, (index + 1) * rows)
        if count == 1:
            add(weights[at], cols)
        else:
            pl.when(n < 2)(functools.partial(add, weights[at], cols))
            pl.when(n >= 2)(functools.partial(add, weights[at + 1], cols))
        at += count

    @pl.when(n == 3)
    def _():
        g0_ref[...] = a0_ref[...].astype(BF16)
        g1_ref[...] = a1_ref[...].astype(BF16)


def grad_context(sc, up0, up1, weight_sets, lay, through):
    length, width = up0.shape
    rows, tile = lay.rows, width // 4
    total = rows * len(weight_sets)
    at = lay.at_piece
    ins = [(u, (length, tile), lambda n, sc: (0, sc[at + n])) for u in (up0, up1)]
    for weights in weight_sets:
        if len(weights) == 1:
            ins.append((weights[0], (rows, tile), lambda n, sc: (0, sc[at + n])))
        else:
            ins.append((weights[0], (rows, tile), lambda n, sc: (0, jnp.minimum(n, 1))))
            ins.append((weights[1], (rows, tile), lambda n, sc: (0, jnp.maximum(n - 2, 0))))
    return call(
        functools.partial(grad_context_body, [len(w) for w in weight_sets]),
        sc,
        (4,),
        ins,
        [((length, total), BF16, (length, total), first)] * 2,
        scratch=[pltpu.VMEM((length, total), F32)] * 2,
        through=through,
        mib=28,
    )


def backward_body(
    per, sc_ref, q_ref, k_ref, v_ref, seg_row_ref, seg_col_ref, own_ref, other_ref, *refs
):
    gq_ref, gk_ref, gv_ref, mask_ref, ak_ref, av_ref = refs[-6:]
    group = pl.program_id(0)
    parity = sc_ref[0]

    @pl.when(group == 0)
    def _():
        fill_mask(mask_ref, seg_row_ref, seg_col_ref)

    key_t = k_ref[...].T
    ak_ref[...] = jnp.zeros_like(ak_ref)
    av_ref[...] = jnp.zeros_like(av_ref)
    for h in range(REPEAT):
        side = group if per == REPEAT else h
        column = h if per == REPEAT else 0
        cols = slice(column * DH, (column + 1) * DH)
        grad = jnp.where(side == parity, own_ref[:, cols], other_ref[:, cols])
        for start, tile, upto in tiles_of(q_ref.shape[0]):
            query = q_ref[start : start + tile, h * DH : (h + 1) * DH]
            probs, cap_tanh = softmax_tile(
                k_ref[:upto, :], query, mask_ref[:upto, start : start + tile]
            )
            grad_rows = grad[start : start + tile, :]
            grad_probs = dot(v_ref[:upto, :], grad_rows, NT)
            delta = jnp.sum(probs * grad_probs, axis=0, keepdims=True)
            scores = probs * (grad_probs - delta) * (SCALE - SCALE * (cap_tanh * cap_tanh))
            scores = scores.astype(BF16)
            av_ref[:upto, :] += dot(probs.astype(BF16), grad_rows, NN)
            ak_ref[:upto, :] += dot(scores, query, NN)
            grad_query = dot(key_t[:, :upto], scores, NN).T
            gq_ref[start : start + tile, h * DH : (h + 1) * DH] = grad_query.astype(BF16)
    gk_ref[...] = ak_ref[...].astype(BF16)
    gv_ref[...] = av_ref[...].astype(BF16)


def backward(sc, k, block, own, other, column, before, lay, through):
    queries, keys, values, seg_row, seg_col = block
    length = queries.shape[0]
    per = lay.heads_shard
    groups = 2 * per // REPEAT
    at = lay.at_z + k

    def whole(i, sc):
        return (0, sc[at] * groups + i)

    heads = (length, REPEAT * DH), whole
    one = (length, DH), whole
    return call(
        functools.partial(backward_body, per),
        sc,
        (groups,),
        [
            (queries, *heads),
            (keys, *one),
            (values, *one),
            (seg_row, (1, length), first),
            (seg_col, (length, 1), first),
            (own, (length, lay.rows), lambda i, sc: (0, column)),
            (other, (length, lay.rows), lambda i, sc: (0, column)),
        ],
        [(queries.shape, BF16, *heads), (keys.shape, BF16, *one), (values.shape, BF16, *one)],
        scratch=[
            pltpu.VMEM((length, length), F32),
            pltpu.VMEM((length, DH), F32),
            pltpu.VMEM((length, DH), F32),
        ],
        before=before,
        through=through,
    )


def adam_body(pieces, tokens, sc_ref, m1_ref, m2_ref, *refs):
    out_ref = refs[-1]
    n = pl.program_id(0)

    def step(piece_ref):
        gradient = piece_ref[...].astype(F32) * (1.0 / tokens)
        moment_one = 0.9 * m1_ref[...] + 0.1 * gradient
        moment_two = 0.95 * m2_ref[...] + 0.05 * gradient * gradient
        out_ref[...] = moment_one / (jnp.sqrt(moment_two) + 1e-08)

    for p in range(pieces):
        pl.when(n == p)(functools.partial(step, refs[p]))


def adam(sc, pieces, first_moment, second_moment, tokens, lay, before, through):
    rows, width = pieces[0][0].shape
    count = len(pieces)
    columns = [lay.at_place(flips) for _, flips in pieces]

    def at(n, sc):
        row = sc[columns[0]]
        for p in range(1, count):
            row = jnp.where(n == p, sc[columns[p]], row)
        return (row, 0)

    block = (rows, width)
    return call(
        functools.partial(adam_body, count, tokens),
        sc,
        (count,),
        [(first_moment, block, at), (second_moment, block, at)]
        + [(x, block, first) for x, _ in pieces],
        [(first_moment.shape, F32, block, at)],
        before=before,
        through=through,
        mib=60,
    )


class Layout:
    def __init__(self, replicas, shards, rows):
        self.replicas, self.shards, self.rows = replicas, shards, rows
        self.z = shards // 2
        self.bits = replicas.bit_length() - 1
        self.heads_shard = HEADS // shards
        self.order = [0] + list(range(1, self.z, 2)) + list(range(self.z - 2, 0, -2))
        self.place = [self.order.index(z) for z in range(self.z)]
        self.at_z = 1
        self.at_piece = self.at_z + self.z
        table = []
        for r in range(replicas):
            for s in range(shards):
                z, core = s // 2, s % 2
                zs = [self.order[(self.place[z] - k) % self.z] for k in range(self.z)]
                bits = [(r >> self.bit_of(core, n)) & 1 for n in range(self.bits)]
                b = 2 * bits[0]
                here = sum(bit << n for n, bit in enumerate(bits[::-1]))
                places = [here ^ flips for flips in range(replicas)]
                table.append([core] + zs + [b, b + 1, 2 - b, 3 - b] + bits + places)
        self.table = np.array(table, np.int32)

    def bit_of(self, core, n):
        return self.bits - 1 - n if core else n

    def at_bit(self, n):
        return self.at_piece + 4 + n

    def at_place(self, flips):
        code = sum(int(f) << n for n, f in enumerate(flips[::-1]))
        return self.at_piece + 4 + self.bits + code

    def sibling(self, x):
        return lax.ppermute(x, "shard", [(s, s ^ 1) for s in range(self.shards)])

    def onward(self, x):
        perm = []
        for p in range(self.z):
            a, b = self.order[p], self.order[(p + 1) % self.z]
            perm += [(2 * a + core, 2 * b + core) for core in range(2)]
        return lax.ppermute(x, "shard", perm)

    def across(self, x, n):
        perm = []
        for r in range(self.replicas):
            for s in range(self.shards):
                partner = r ^ (1 << self.bit_of(s % 2, n))
                perm.append((r * self.shards + s, partner * self.shards + s))
        return lax.ppermute(x, ("replica", "shard"), perm)


def per_device(queries, keys, values, segments, out_weight, upstream, first_moment, second_moment):
    length, width = upstream.shape
    lay = Layout(lax.axis_size("replica"), lax.axis_size("shard"), out_weight.shape[0])
    tokens = length * lay.replicas * lay.shards
    device = lax.axis_index("replica") * lay.shards + lax.axis_index("shard")
    sc = lax.dynamic_index_in_dim(jnp.asarray(lay.table), device, 0, keepdims=False)
    block = (queries, keys, values, segments, segments.reshape(length, 1))

    box = {}
    terms = {}
    gc = {}
    grads = ()

    def run(function, *args, held=(), **more):
        names = ["token", *held]
        outs, handed = function(*args, through=[box[n] for n in names], **more)
        box.update(zip(names, handed))
        return outs

    def do_product(k, held=()):
        own, other = contexts[k]
        box["send", k], keep = run(
            product, sc, own, other, upstream, upstream_other, lay, held=held
        )
        terms[k] = [keep]

    def send(k):
        terms[k].append(lay.across(box["send", k], len(terms[k]) - 1))

    def do_halve(k, held=()):
        for stage in range(1, lay.bits):
            (box["send", k],) = run(combine, sc, terms[k], None, True, lay, held=held)
            held = ()
            if stage < lay.bits - 1:
                send(k)

    def do_sum(k, held=()):
        (box["sum", k],) = run(combine, sc, terms[k], box.get(("part", k)), False, lay, held=held)

    def pass_sum(k):
        box["part", (k + 1) % lay.z] = lay.onward(box["sum", k])

    def pass_weights(k):
        if k + 1 < lay.z:
            box["ring", k + 1] = lay.onward(box["ring", k])

    def cross_weights(k):
        box["cross", k] = lay.across(box["ring", k], 0)

    def do_grad_context(ks, held=()):
        sets = [[box["ring", k], box["cross", k]] if k else [out_weight] for k in ks]
        own, box["away", ks[0]] = run(
            grad_context, sc, upstream, upstream_other, sets, lay, held=held
        )
        for n, k in enumerate(ks):
            gc[k] = own, ks[0], n

    def swap_grad_context(k):
        box["gc", k] = lay.sibling(box["away", k])

    def do_backward(k, held=()):
        nonlocal grads
        own, base, column = gc[k]
        grads = run(backward, sc, k, block, own, box["gc", base], column, grads, lay, held=held)

    upstream_other = lay.sibling(upstream)
    box["ring", 1], box["token"] = cut(sc, out_weight, lay)[0]
    box["ring", 1] = lay.onward(box["ring", 1])

    late = [*range(2, lay.z), 0]
    rows = lay.rows
    contexts = {}
    (both_sides,) = run(forward, sc, [1], [0, 1], block, lay)
    contexts[1] = (both_sides, 1), (lay.sibling(both_sides[:rows]), 0)
    (away,) = run(forward, sc, late, [0], block, lay)
    away = lay.sibling(away)
    do_product(1)
    send(1)
    (stay,) = run(forward, sc, late, [1], block, lay)
    for n, k in enumerate(late):
        contexts[k] = (stay, n), (away, n)
    do_product(2)
    send(2)
    do_halve(1, held=[("ring", 1)])
    pass_weights(1)
    cross_weights(1)
    send(1)
    do_product(3)
    send(3)
    do_halve(2)
    send(2)
    do_product(0)
    do_grad_context([0, 1])
    swap_grad_context(0)
    do_sum(1, held=[("ring", 2), ("gc", 0)])
    pass_sum(1)
    pass_weights(2)
    cross_weights(2)
    do_backward(0)
    do_halve(3)
    send(3)
    do_backward(1)
    do_sum(2, held=[("send", 0)])
    pass_sum(2)
    send(0)
    for k in range(4, lay.z):
        do_product(k, held=[("ring", k - 1)])
        pass_weights(k - 1)
        cross_weights(k - 1)
        send(k)
        do_halve(k)
        send(k)
    last = lay.z - 1
    for k in range(2, last):
        do_grad_context([k])
        swap_grad_context(k)
        do_backward(k)
    do_halve(0, held=[("ring", last)])
    send(0)
    cross_weights(last)
    for k in range(3, lay.z):
        do_sum(k)
        pass_sum(k)
    do_grad_context([last])
    swap_grad_context(last)
    do_sum(0)

    have = [(box["sum", 0], (False,) * lay.bits)]

    def spread(n, piece):
        x, flips = piece
        return lay.across(x, n), flips[:n] + (True,) + flips[n + 1 :]

    moments = first_moment, second_moment, tokens, lay
    direct = [spread(n, have[0]) for n in range(lay.bits - 1, -1, -1)]
    do_backward(last)
    near = [have[0], *direct]
    have = [have[0], direct[0]]
    done = {flips for _, flips in near}
    far = []
    for n in range(lay.bits - 2, -1, -1):
        more = []
        for x, flips in have:
            flips = flips[:n] + (True,) + flips[n + 1 :]
            if flips in done:
                more += [p for p in near if p[1] == flips]
            else:
                more.append((lay.across(x, n), flips))
                far.append(more[-1])
        have += more
    step = run(adam, sc, near, *moments, before=())
    step = run(adam, sc, far, *moments, before=step)
    return (*grads, *step)


def solution(mesh):
    both = P(("replica", "shard"), None)
    shard = P("shard", None)
    return jax.shard_map(
        per_device,
        mesh=mesh,
        in_specs=(both, both, both, both, shard, both, shard, shard),
        out_specs=(both, both, both, shard),
        check_vma=False,
    )
```

```python
import functools

import jax
import jax.numpy as jnp
import numpy as np
from jax import lax
from jax.experimental import pallas as pl
from jax.experimental.pallas import tpu as pltpu
from jax.sharding import PartitionSpec as P

HEADS = 16
KV_HEADS = 8
DH = 128
REPEAT = HEADS // KV_HEADS

SCALE = 1.0 / 12.0
CAP = 50.0
MIB = 1024 * 1024
F32 = jnp.float32
BF16 = jnp.bfloat16

NT = (((1,), (1,)), ((), ()))
NN = (((1,), (0,)), ((), ()))


def dot(a, b, dims):
    return lax.dot_general(a, b, dims, preferred_element_type=F32)


def call(body, sc, grid, ins, outs, scratch=(), through=(), before=(), mib=20):
    n_in, n_out, n_before, n_through = len(ins), len(outs), len(before), len(through)

    def kernel(sc_ref, *refs):
        at = n_in + n_before + n_through
        body(sc_ref, *refs[:n_in], *refs[at : at + n_out], *refs[at + n_out + n_through :])

    anywhere = pl.BlockSpec(memory_space=pl.ANY)
    stay = pl.BlockSpec(memory_space=pltpu.HBM)
    aliases = {1 + n_in + n: n for n in range(n_before)}
    aliases.update({1 + n_in + n_before + n: n_out + n for n in range(n_through)})
    results = pl.pallas_call(
        kernel,
        grid_spec=pltpu.PrefetchScalarGridSpec(
            num_scalar_prefetch=1,
            grid=grid,
            in_specs=[pl.BlockSpec(block, index) for _, block, index in ins]
            + [anywhere] * n_before
            + [stay] * n_through,
            out_specs=[pl.BlockSpec(block, index) for _, _, block, index in outs]
            + [stay] * n_through,
            scratch_shapes=list(scratch),
        ),
        out_shape=[jax.ShapeDtypeStruct(shape, dtype) for shape, dtype, _, _ in outs]
        + [jax.ShapeDtypeStruct(x.shape, x.dtype) for x in through],
        input_output_aliases=aliases,
        cost_estimate=pl.CostEstimate(flops=1, transcendentals=0, bytes_accessed=1),
        compiler_params=pltpu.CompilerParams(vmem_limit_bytes=mib * MIB),
    )(sc, *[array for array, _, _ in ins], *before, *through)
    return results[:n_out], results[n_out:]


def first(*_):
    return (0, 0)


def fill_mask(mask_ref, seg_row_ref, seg_col_ref):
    length = mask_ref.shape[0]
    j = lax.broadcasted_iota(jnp.int32, (length, length), 0)
    i = lax.broadcasted_iota(jnp.int32, (length, length), 1)
    allowed = (j <= i) & (seg_col_ref[...] == seg_row_ref[...])
    mask_ref[...] = jnp.where(allowed, 1.0, 0.0).astype(F32)


def tiles_of(length):
    tile = 256
    return [(t * tile, tile, (t + 1) * tile) for t in range(length // tile)]


def softmax_tile(key, query, mask):
    cap_tanh = jnp.tanh(dot(key, query, NT) * (SCALE / CAP))
    weights = jnp.exp(cap_tanh * CAP) * mask
    inverse = 1.0 / jnp.sum(weights, axis=0, keepdims=True)
    return weights * inverse, cap_tanh


def cut_body(sc_ref, in_ref, out_ref, token_ref):
    out_ref[...] = in_ref[...]
    token_ref[...] = jnp.zeros_like(token_ref)


def cut(sc, weight, lay):
    block = (weight.shape[0], weight.shape[1] // 2)
    return call(
        cut_body,
        sc,
        (1,),
        [(weight, block, lambda n, sc: (0, sc[lay.at_bit(0)]))],
        [(block, BF16, block, first), ((8, 128), F32, (8, 128), first)],
    )


def relay_body(sc_ref):
    pass


def relay(sc, through):
    return call(relay_body, sc, (1,), [], [], through=through)


def forward_body(heads, sc_ref, q_ref, k_ref, v_ref, seg_row_ref, seg_col_ref, out_ref, mask_ref):
    @pl.when(pl.program_id(0) == 0)
    def _():
        fill_mask(mask_ref, seg_row_ref, seg_col_ref)

    value_t = v_ref[...].T
    for h in range(heads):
        for start, tile, upto in tiles_of(q_ref.shape[0]):
            probs, _ = softmax_tile(
                k_ref[:upto, :],
                q_ref[start : start + tile, h * DH : (h + 1) * DH],
                mask_ref[:upto, start : start + tile],
            )
            context = dot(value_t[:, :upto], probs.astype(BF16), NN)
            out_ref[h * DH : (h + 1) * DH, start : start + tile] = context.astype(BF16)


def forward(sc, ks, sides, block, lay, through):
    queries, keys, values, seg_row, seg_col = block
    length = queries.shape[0]
    per = lay.heads_shard
    count = len(ks)

    def shard_of(i, sc):
        k = lax.rem(ks[0] + lax.rem(i, count), lay.z)
        if len(sides) == 2:
            own = i >= count
        else:
            own = sides[0] == 1
        return 2 * sc[lay.at_z + k] + jnp.where(own, sc[0], 1 - sc[0])

    def kv_of(i, sc):
        return (0, (shard_of(i, sc) * per) // REPEAT)

    rows = per * DH
    steps = count * len(sides)
    return call(
        functools.partial(forward_body, per),
        sc,
        (steps,),
        [
            (queries, (length, rows), lambda i, sc: (0, shard_of(i, sc))),
            (keys, (length, DH), kv_of),
            (values, (length, DH), kv_of),
            (seg_row, (1, length), first),
            (seg_col, (length, 1), first),
        ],
        [((steps * rows, length), BF16, (rows, length), lambda i, sc: (i, 0))],
        scratch=[pltpu.VMEM((length, length), F32)],
        through=through,
    )


def product_body(at_bit, sc_ref, c0_ref, c1_ref, u0_ref, u1_ref, send_ref, keep_ref, acc_ref):
    half = acc_ref.shape[0] // 2
    acc = dot(c0_ref[...], u0_ref[...], NN) + dot(c1_ref[...], u1_ref[...], NN)
    acc_ref[...] = acc.astype(BF16)
    bit = sc_ref[at_bit]
    keep_ref[...] = acc_ref[pl.ds(pl.multiple_of(bit * half, half), half), :]
    send_ref[...] = acc_ref[pl.ds(pl.multiple_of((1 - bit) * half, half), half), :]


def product(sc, own, other, up0, up1, lay, through):
    length, width = up0.shape
    rows = lay.rows
    tile = width // 4
    out = ((rows // 2, width), BF16, (rows // 2, tile), lambda n, sc: (0, n))
    return call(
        functools.partial(product_body, lay.at_bit(0)),
        sc,
        (4,),
        [(x, (rows, length), lambda n, sc, at=at: (at, 0)) for x, at in (own, other)]
        + [(u, (length, tile), lambda n, sc: (0, n)) for u in (up0, up1)],
        [out, out],
        scratch=[pltpu.VMEM((rows, tile), BF16)],
        through=through,
    )


def combine_body(sc_ref, *refs):
    total = refs[0][...].astype(F32)
    for ref in refs[1:-1]:
        total = total + ref[...].astype(F32)
    refs[-1][...] = total.astype(BF16)


def combine(sc, terms, ring, away, lay, through):
    deep = len(terms) if away else lay.bits
    width = terms[0].shape[1]
    size = lay.rows >> deep
    ins = []

    def place(level):
        def index(n, sc):
            at = 0
            for m in range(level, deep):
                bit = sc[lay.at_bit(m)]
                at = 2 * at + (1 - bit if away and m == deep - 1 else bit)
            return (at, 0)

        return index

    for m, x in enumerate(terms):
        ins.append((x, (size, width), place(max(m, 1))))
    if ring is not None:
        ins.append((ring, (size, width), first))
    out = ((size, width), BF16, (size, width), first)
    return call(combine_body, sc, (1,), ins, [out], through=through)


def grad_context_body(sets, sc_ref, u0_ref, u1_ref, *refs):
    weights, (g0_ref, g1_ref, a0_ref, a1_ref) = refs[:-4], refs[-4:]
    n = pl.program_id(0)
    rows = a0_ref.shape[1] // len(sets)

    def add(weight_ref, cols):
        d0 = dot(u0_ref[...], weight_ref[...], NT)
        d1 = dot(u1_ref[...], weight_ref[...], NT)

        @pl.when(n == 0)
        def _():
            a0_ref[:, cols] = d0
            a1_ref[:, cols] = d1

        @pl.when(n > 0)
        def _():
            a0_ref[:, cols] += d0
            a1_ref[:, cols] += d1

    at = 0
    for index, count in enumerate(sets):
        cols = slice(index * rows, (index + 1) * rows)
        if count == 1:
            add(weights[at], cols)
        else:
            pl.when(n < 2)(functools.partial(add, weights[at], cols))
            pl.when(n >= 2)(functools.partial(add, weights[at + 1], cols))
        at += count

    @pl.when(n == 3)
    def _():
        g0_ref[...] = a0_ref[...].astype(BF16)
        g1_ref[...] = a1_ref[...].astype(BF16)


def grad_context(sc, up0, up1, weight_sets, lay, through):
    length, width = up0.shape
    rows, tile = lay.rows, width // 4
    total = rows * len(weight_sets)
    at = lay.at_piece
    ins = [(u, (length, tile), lambda n, sc: (0, sc[at + n])) for u in (up0, up1)]
    for weights in weight_sets:
        if len(weights) == 1:
            ins.append((weights[0], (rows, tile), lambda n, sc: (0, sc[at + n])))
        else:
            ins.append((weights[0], (rows, tile), lambda n, sc: (0, jnp.minimum(n, 1))))
            ins.append((weights[1], (rows, tile), lambda n, sc: (0, jnp.maximum(n - 2, 0))))
    return call(
        functools.partial(grad_context_body, [len(w) for w in weight_sets]),
        sc,
        (4,),
        ins,
        [((length, total), BF16, (length, total), first)] * 2,
        scratch=[pltpu.VMEM((length, total), F32)] * 2,
        through=through,
        mib=28,
    )


def backward_body(
    per, sc_ref, q_ref, k_ref, v_ref, seg_row_ref, seg_col_ref, own_ref, other_ref, *refs
):
    gq_ref, gk_ref, gv_ref, mask_ref, ak_ref, av_ref = refs[-6:]
    group = pl.program_id(0)
    parity = sc_ref[0]

    @pl.when(group == 0)
    def _():
        fill_mask(mask_ref, seg_row_ref, seg_col_ref)

    key_t = k_ref[...].T
    ak_ref[...] = jnp.zeros_like(ak_ref)
    av_ref[...] = jnp.zeros_like(av_ref)
    for h in range(REPEAT):
        side = group if per == REPEAT else h
        column = h if per == REPEAT else 0
        cols = slice(column * DH, (column + 1) * DH)
        grad = jnp.where(side == parity, own_ref[:, cols], other_ref[:, cols])
        for start, tile, upto in tiles_of(q_ref.shape[0]):
            query = q_ref[start : start + tile, h * DH : (h + 1) * DH]
            probs, cap_tanh = softmax_tile(
                k_ref[:upto, :], query, mask_ref[:upto, start : start + tile]
            )
            grad_rows = grad[start : start + tile, :]
            grad_probs = dot(v_ref[:upto, :], grad_rows, NT)
            delta = jnp.sum(probs * grad_probs, axis=0, keepdims=True)
            scores = probs * (grad_probs - delta) * (SCALE - SCALE * (cap_tanh * cap_tanh))
            scores = scores.astype(BF16)
            av_ref[:upto, :] += dot(probs.astype(BF16), grad_rows, NN)
            ak_ref[:upto, :] += dot(scores, query, NN)
            grad_query = dot(key_t[:, :upto], scores, NN).T
            gq_ref[start : start + tile, h * DH : (h + 1) * DH] = grad_query.astype(BF16)
    gk_ref[...] = ak_ref[...].astype(BF16)
    gv_ref[...] = av_ref[...].astype(BF16)


def backward(sc, k, block, own, other, column, before, lay, through):
    queries, keys, values, seg_row, seg_col = block
    length = queries.shape[0]
    per = lay.heads_shard
    groups = 2 * per // REPEAT
    at = lay.at_z + k

    def whole(i, sc):
        return (0, sc[at] * groups + i)

    heads = (length, REPEAT * DH), whole
    one = (length, DH), whole
    return call(
        functools.partial(backward_body, per),
        sc,
        (groups,),
        [
            (queries, *heads),
            (keys, *one),
            (values, *one),
            (seg_row, (1, length), first),
            (seg_col, (length, 1), first),
            (own, (length, lay.rows), lambda i, sc: (0, column)),
            (other, (length, lay.rows), lambda i, sc: (0, column)),
        ],
        [(queries.shape, BF16, *heads), (keys.shape, BF16, *one), (values.shape, BF16, *one)],
        scratch=[
            pltpu.VMEM((length, length), F32),
            pltpu.VMEM((length, DH), F32),
            pltpu.VMEM((length, DH), F32),
        ],
        before=before,
        through=through,
    )


def adam_body(pieces, tokens, sc_ref, m1_ref, m2_ref, *refs):
    out_ref = refs[-1]
    n = pl.program_id(0)

    def step(piece_ref):
        gradient = piece_ref[...].astype(F32) * (1.0 / tokens)
        moment_one = 0.9 * m1_ref[...] + 0.1 * gradient
        moment_two = 0.95 * m2_ref[...] + 0.05 * gradient * gradient
        out_ref[...] = moment_one / (jnp.sqrt(moment_two) + 1e-08)

    for p in range(pieces):
        pl.when(n == p)(functools.partial(step, refs[p]))


def adam(sc, pieces, first_moment, second_moment, tokens, lay, before, through):
    rows, width = pieces[0][0].shape
    count = len(pieces)
    columns = [lay.at_place(flips) for _, flips in pieces]

    def at(n, sc):
        row = sc[columns[0]]
        for p in range(1, count):
            row = jnp.where(n == p, sc[columns[p]], row)
        return (row, 0)

    block = (rows, width)
    return call(
        functools.partial(adam_body, count, tokens),
        sc,
        (count,),
        [(first_moment, block, at), (second_moment, block, at)]
        + [(x, block, first) for x, _ in pieces],
        [(first_moment.shape, F32, block, at)],
        before=before,
        through=through,
        mib=60,
    )


class Layout:
    def __init__(self, replicas, shards, rows):
        self.replicas, self.shards, self.rows = replicas, shards, rows
        self.z = shards // 2
        self.bits = replicas.bit_length() - 1
        self.heads_shard = HEADS // shards
        self.order = [0] + list(range(1, self.z, 2)) + list(range(self.z - 2, 0, -2))
        self.place = [self.order.index(z) for z in range(self.z)]
        self.at_z = 1
        self.at_piece = self.at_z + self.z
        table = []
        for r in range(replicas):
            for s in range(shards):
                z, core = s // 2, s % 2
                zs = [self.order[(self.place[z] - k) % self.z] for k in range(self.z)]
                bits = [(r >> self.bit_of(core, n)) & 1 for n in range(self.bits)]
                b = 2 * bits[0]
                here = sum(bit << n for n, bit in enumerate(bits[::-1]))
                places = [here ^ flips for flips in range(replicas)]
                table.append([core] + zs + [b, b + 1, 2 - b, 3 - b] + bits + places)
        self.table = np.array(table, np.int32)

    def bit_of(self, core, n):
        return self.bits - 1 - n if core else n

    def at_bit(self, n):
        return self.at_piece + 4 + n

    def at_place(self, flips):
        code = sum(int(f) << n for n, f in enumerate(flips[::-1]))
        return self.at_piece + 4 + self.bits + code

    def sibling(self, x):
        return lax.ppermute(x, "shard", [(s, s ^ 1) for s in range(self.shards)])

    def onward(self, x):
        perm = []
        for p in range(self.z):
            a, b = self.order[p], self.order[(p + 1) % self.z]
            perm += [(2 * a + core, 2 * b + core) for core in range(2)]
        return lax.ppermute(x, "shard", perm)

    def across(self, x, n):
        perm = []
        for r in range(self.replicas):
            for s in range(self.shards):
                partner = r ^ (1 << self.bit_of(s % 2, n))
                perm.append((r * self.shards + s, partner * self.shards + s))
        return lax.ppermute(x, ("replica", "shard"), perm)


def per_device(queries, keys, values, segments, out_weight, upstream, first_moment, second_moment):
    length, width = upstream.shape
    lay = Layout(lax.axis_size("replica"), lax.axis_size("shard"), out_weight.shape[0])
    tokens = length * lay.replicas * lay.shards
    device = lax.axis_index("replica") * lay.shards + lax.axis_index("shard")
    sc = lax.dynamic_index_in_dim(jnp.asarray(lay.table), device, 0, keepdims=False)
    block = (queries, keys, values, segments, segments.reshape(length, 1))

    box = {}
    terms = {}
    gc = {}
    grads = ()

    def run(function, *args, held=(), **more):
        names = ["token", *held]
        outs, handed = function(*args, through=[box[n] for n in names], **more)
        box.update(zip(names, handed))
        return outs

    def do_product(k, held=()):
        own, other = contexts[k]
        box["send", k], keep = run(
            product, sc, own, other, upstream, upstream_other, lay, held=held
        )
        terms[k] = [keep]

    def send(k):
        terms[k].append(lay.across(box["send", k], len(terms[k]) - 1))

    def do_halve(k, held=()):
        for stage in range(1, lay.bits):
            (box["send", k],) = run(combine, sc, terms[k], None, True, lay, held=held)
            held = ()
            if stage < lay.bits - 1:
                send(k)

    def do_sum(k, held=()):
        (box["sum", k],) = run(combine, sc, terms[k], box.get(("part", k)), False, lay, held=held)

    def pass_sum(k):
        box["part", (k + 1) % lay.z] = lay.onward(box["sum", k])

    def pass_weights(k):
        if k + 1 < lay.z:
            box["ring", k + 1] = lay.onward(box["ring", k])

    def cross_weights(k):
        box["cross", k] = lay.across(box["ring", k], 0)

    def do_grad_context(ks, held=()):
        sets = [[box["ring", k], box["cross", k]] if k else [out_weight] for k in ks]
        own, box["away", ks[0]] = run(
            grad_context, sc, upstream, upstream_other, sets, lay, held=held
        )
        for n, k in enumerate(ks):
            gc[k] = own, ks[0], n

    def swap_grad_context(k):
        box["gc", k] = lay.sibling(box["away", k])

    def do_backward(k, held=()):
        nonlocal grads
        own, base, column = gc[k]
        grads = run(backward, sc, k, block, own, box["gc", base], column, grads, lay, held=held)

    upstream_other = lay.sibling(upstream)
    box["ring", 1], box["token"] = cut(sc, out_weight, lay)[0]
    box["ring", 1] = lay.onward(box["ring", 1])

    late = [*range(2, lay.z), 0]
    rows = lay.rows
    contexts = {}
    (both_sides,) = run(forward, sc, [1], [0, 1], block, lay)
    contexts[1] = (both_sides, 1), (lay.sibling(both_sides[:rows]), 0)
    do_product(1)
    send(1)
    (both_sides,) = run(forward, sc, late, [0, 1], block, lay)
    box["context"] = lay.sibling(both_sides[: len(late) * rows])
    do_halve(1, held=[("ring", 1), "context"])
    send(1)
    pass_weights(1)
    cross_weights(1)
    for n, k in enumerate(late):
        contexts[k] = (both_sides, len(late) + n), (box["context"], n)
    do_product(2)
    do_sum(1)
    pass_sum(1)
    send(2)
    do_product(3)
    send(3)
    do_grad_context([0, 1])
    swap_grad_context(0)
    run(relay, sc, held=[("ring", 2)])
    pass_weights(2)
    cross_weights(2)
    do_halve(2)
    send(2)
    do_backward(0)
    do_product(0)
    do_halve(3)
    send(3)
    do_backward(1, held=[("send", 0)])
    send(0)
    do_sum(2)
    pass_sum(2)
    for k in range(4, lay.z):
        do_product(k, held=[("ring", k - 1)])
        pass_weights(k - 1)
        cross_weights(k - 1)
        send(k)
        do_halve(k)
        send(k)
    last = lay.z - 1
    do_grad_context([2])
    swap_grad_context(2)
    do_sum(3, held=[("ring", last)])
    pass_sum(3)
    cross_weights(last)
    do_backward(2)
    for k in range(4, lay.z):
        do_sum(k)
        pass_sum(k)
    for k in range(3, last):
        do_grad_context([k])
        swap_grad_context(k)
        do_backward(k)
    do_halve(0)
    send(0)
    do_grad_context([last])
    swap_grad_context(last)
    do_sum(0)

    have = [(box["sum", 0], (False,) * lay.bits)]

    def spread(n, piece):
        x, flips = piece
        return lay.across(x, n), flips[:n] + (True,) + flips[n + 1 :]

    moments = first_moment, second_moment, tokens, lay
    direct = [spread(n, have[0]) for n in range(lay.bits - 1, -1, -1)]
    do_backward(last)
    box["got"] = direct[0][0]
    step = run(adam, sc, have, *moments, before=(), held=["got"])
    direct[0] = (box["got"], direct[0][1])
    near = [have[0], *direct]
    have = [have[0], direct[0]]
    done = {flips for _, flips in near}
    far = []
    for n in range(lay.bits - 2, -1, -1):
        more = []
        for x, flips in have:
            flips = flips[:n] + (True,) + flips[n + 1 :]
            if flips in done:
                more += [p for p in near if p[1] == flips]
            else:
                more.append((lay.across(x, n), flips))
                far.append(more[-1])
        have += more
    step = run(adam, sc, direct, *moments, before=step)
    step = run(adam, sc, far, *moments, before=step)
    return (*grads, *step)


def solution(mesh):
    both = P(("replica", "shard"), None)
    shard = P("shard", None)
    return jax.shard_map(
        per_device,
        mesh=mesh,
        in_specs=(both, both, both, both, shard, both, shard, shard),
        out_specs=(both, both, both, shard),
        check_vma=False,
    )
```

```python
import functools

import jax
import jax.numpy as jnp
import numpy as np
from jax import lax
from jax.experimental import pallas as pl
from jax.experimental.pallas import tpu as pltpu
from jax.sharding import PartitionSpec as P

HEADS = 16
KV_HEADS = 8
DH = 128
REPEAT = HEADS // KV_HEADS

SCALE = 1.0 / 12.0
CAP = 50.0
MIB = 1024 * 1024
F32 = jnp.float32
BF16 = jnp.bfloat16

NT = (((1,), (1,)), ((), ()))
NN = (((1,), (0,)), ((), ()))


def dot(a, b, dims):
    return lax.dot_general(a, b, dims, preferred_element_type=F32)


def call(body, sc, grid, ins, outs, scratch=(), through=(), before=(), mib=20):
    n_in, n_out, n_before, n_through = len(ins), len(outs), len(before), len(through)

    def kernel(sc_ref, *refs):
        at = n_in + n_before + n_through
        body(sc_ref, *refs[:n_in], *refs[at : at + n_out], *refs[at + n_out + n_through :])

    anywhere = pl.BlockSpec(memory_space=pl.ANY)
    stay = pl.BlockSpec(memory_space=pltpu.HBM)
    aliases = {1 + n_in + n: n for n in range(n_before)}
    aliases.update({1 + n_in + n_before + n: n_out + n for n in range(n_through)})
    results = pl.pallas_call(
        kernel,
        grid_spec=pltpu.PrefetchScalarGridSpec(
            num_scalar_prefetch=1,
            grid=grid,
            in_specs=[pl.BlockSpec(block, index) for _, block, index in ins]
            + [anywhere] * n_before
            + [stay] * n_through,
            out_specs=[pl.BlockSpec(block, index) for _, _, block, index in outs]
            + [stay] * n_through,
            scratch_shapes=list(scratch),
        ),
        out_shape=[jax.ShapeDtypeStruct(shape, dtype) for shape, dtype, _, _ in outs]
        + [jax.ShapeDtypeStruct(x.shape, x.dtype) for x in through],
        input_output_aliases=aliases,
        cost_estimate=pl.CostEstimate(flops=1, transcendentals=0, bytes_accessed=1),
        compiler_params=pltpu.CompilerParams(vmem_limit_bytes=mib * MIB),
    )(sc, *[array for array, _, _ in ins], *before, *through)
    return results[:n_out], results[n_out:]


def first(*_):
    return (0, 0)


def fill_mask(mask_ref, seg_row_ref, seg_col_ref):
    length = mask_ref.shape[0]
    j = lax.broadcasted_iota(jnp.int32, (length, length), 0)
    i = lax.broadcasted_iota(jnp.int32, (length, length), 1)
    allowed = (j <= i) & (seg_col_ref[...] == seg_row_ref[...])
    mask_ref[...] = jnp.where(allowed, 1.0, 0.0).astype(F32)


def tiles_of(length):
    tile = 256
    return [(t * tile, tile, (t + 1) * tile) for t in range(length // tile)]


def softmax_tile(key, query, mask):
    cap_tanh = jnp.tanh(dot(key, query, NT) * (SCALE / CAP))
    weights = jnp.exp(cap_tanh * CAP) * mask
    inverse = 1.0 / jnp.sum(weights, axis=0, keepdims=True)
    return weights * inverse, cap_tanh


def cut_body(sc_ref, in_ref, out_ref, token_ref):
    out_ref[...] = in_ref[...]
    token_ref[...] = jnp.zeros_like(token_ref)


def cut(sc, weight, lay):
    block = (weight.shape[0], weight.shape[1] // 2)
    return call(
        cut_body,
        sc,
        (1,),
        [(weight, block, lambda n, sc: (0, sc[lay.at_bit(0)]))],
        [(block, BF16, block, first), ((8, 128), F32, (8, 128), first)],
    )


def relay_body(sc_ref):
    pass


def relay(sc, through):
    return call(relay_body, sc, (1,), [], [], through=through)


def forward_body(heads, sc_ref, q_ref, k_ref, v_ref, seg_row_ref, seg_col_ref, out_ref, mask_ref):
    @pl.when(pl.program_id(0) == 0)
    def _():
        fill_mask(mask_ref, seg_row_ref, seg_col_ref)

    value_t = v_ref[...].T
    for h in range(heads):
        for start, tile, upto in tiles_of(q_ref.shape[0]):
            probs, _ = softmax_tile(
                k_ref[:upto, :],
                q_ref[start : start + tile, h * DH : (h + 1) * DH],
                mask_ref[:upto, start : start + tile],
            )
            context = dot(value_t[:, :upto], probs.astype(BF16), NN)
            out_ref[h * DH : (h + 1) * DH, start : start + tile] = context.astype(BF16)


def forward(sc, ks, sides, block, lay, through):
    queries, keys, values, seg_row, seg_col = block
    length = queries.shape[0]
    per = lay.heads_shard
    count = len(ks)

    def shard_of(i, sc):
        k = lax.rem(ks[0] + lax.rem(i, count), lay.z)
        if len(sides) == 2:
            own = i >= count
        else:
            own = sides[0] == 1
        return 2 * sc[lay.at_z + k] + jnp.where(own, sc[0], 1 - sc[0])

    def kv_of(i, sc):
        return (0, (shard_of(i, sc) * per) // REPEAT)

    rows = per * DH
    steps = count * len(sides)
    return call(
        functools.partial(forward_body, per),
        sc,
        (steps,),
        [
            (queries, (length, rows), lambda i, sc: (0, shard_of(i, sc))),
            (keys, (length, DH), kv_of),
            (values, (length, DH), kv_of),
            (seg_row, (1, length), first),
            (seg_col, (length, 1), first),
        ],
        [((steps * rows, length), BF16, (rows, length), lambda i, sc: (i, 0))],
        scratch=[pltpu.VMEM((length, length), F32)],
        through=through,
    )


def product_body(at_bit, sc_ref, c0_ref, c1_ref, u0_ref, u1_ref, send_ref, keep_ref, acc_ref):
    half = acc_ref.shape[0] // 2
    acc = dot(c0_ref[...], u0_ref[...], NN) + dot(c1_ref[...], u1_ref[...], NN)
    acc_ref[...] = acc.astype(BF16)
    bit = sc_ref[at_bit]
    keep_ref[...] = acc_ref[pl.ds(pl.multiple_of(bit * half, half), half), :]
    send_ref[...] = acc_ref[pl.ds(pl.multiple_of((1 - bit) * half, half), half), :]


def product(sc, own, other, up0, up1, lay, through):
    length, width = up0.shape
    rows = lay.rows
    tile = width // 4
    out = ((rows // 2, width), BF16, (rows // 2, tile), lambda n, sc: (0, n))
    return call(
        functools.partial(product_body, lay.at_bit(0)),
        sc,
        (4,),
        [(x, (rows, length), lambda n, sc, at=at: (at, 0)) for x, at in (own, other)]
        + [(u, (length, tile), lambda n, sc: (0, n)) for u in (up0, up1)],
        [out, out],
        scratch=[pltpu.VMEM((rows, tile), BF16)],
        through=through,
    )


def combine_body(sc_ref, *refs):
    total = refs[0][...].astype(F32)
    for ref in refs[1:-1]:
        total = total + ref[...].astype(F32)
    refs[-1][...] = total.astype(BF16)


def combine(sc, terms, ring, away, lay, through):
    deep = len(terms) if away else lay.bits
    width = terms[0].shape[1]
    size = lay.rows >> deep
    ins = []

    def place(level):
        def index(n, sc):
            at = 0
            for m in range(level, deep):
                bit = sc[lay.at_bit(m)]
                at = 2 * at + (1 - bit if away and m == deep - 1 else bit)
            return (at, 0)

        return index

    for m, x in enumerate(terms):
        ins.append((x, (size, width), place(max(m, 1))))
    if ring is not None:
        ins.append((ring, (size, width), first))
    out = ((size, width), BF16, (size, width), first)
    return call(combine_body, sc, (1,), ins, [out], through=through)


def grad_context_body(sets, sc_ref, u0_ref, u1_ref, *refs):
    weights, (g0_ref, g1_ref, a0_ref, a1_ref) = refs[:-4], refs[-4:]
    n = pl.program_id(0)
    rows = a0_ref.shape[1] // len(sets)

    def add(weight_ref, cols):
        d0 = dot(u0_ref[...], weight_ref[...], NT)
        d1 = dot(u1_ref[...], weight_ref[...], NT)

        @pl.when(n == 0)
        def _():
            a0_ref[:, cols] = d0
            a1_ref[:, cols] = d1

        @pl.when(n > 0)
        def _():
            a0_ref[:, cols] += d0
            a1_ref[:, cols] += d1

    at = 0
    for index, count in enumerate(sets):
        cols = slice(index * rows, (index + 1) * rows)
        if count == 1:
            add(weights[at], cols)
        else:
            pl.when(n < 2)(functools.partial(add, weights[at], cols))
            pl.when(n >= 2)(functools.partial(add, weights[at + 1], cols))
        at += count

    @pl.when(n == 3)
    def _():
        g0_ref[...] = a0_ref[...].astype(BF16)
        g1_ref[...] = a1_ref[...].astype(BF16)


def grad_context(sc, up0, up1, weight_sets, lay, through):
    length, width = up0.shape
    rows, tile = lay.rows, width // 4
    total = rows * len(weight_sets)
    at = lay.at_piece
    ins = [(u, (length, tile), lambda n, sc: (0, sc[at + n])) for u in (up0, up1)]
    for weights in weight_sets:
        if len(weights) == 1:
            ins.append((weights[0], (rows, tile), lambda n, sc: (0, sc[at + n])))
        else:
            ins.append((weights[0], (rows, tile), lambda n, sc: (0, jnp.minimum(n, 1))))
            ins.append((weights[1], (rows, tile), lambda n, sc: (0, jnp.maximum(n - 2, 0))))
    return call(
        functools.partial(grad_context_body, [len(w) for w in weight_sets]),
        sc,
        (4,),
        ins,
        [((length, total), BF16, (length, total), first)] * 2,
        scratch=[pltpu.VMEM((length, total), F32)] * 2,
        through=through,
        mib=28,
    )


def backward_body(
    per, sc_ref, q_ref, k_ref, v_ref, seg_row_ref, seg_col_ref, own_ref, other_ref, *refs
):
    gq_ref, gk_ref, gv_ref, mask_ref, ak_ref, av_ref = refs[-6:]
    group = pl.program_id(0)
    parity = sc_ref[0]

    @pl.when(group == 0)
    def _():
        fill_mask(mask_ref, seg_row_ref, seg_col_ref)

    key_t = k_ref[...].T
    ak_ref[...] = jnp.zeros_like(ak_ref)
    av_ref[...] = jnp.zeros_like(av_ref)
    for h in range(REPEAT):
        side = group if per == REPEAT else h
        column = h if per == REPEAT else 0
        cols = slice(column * DH, (column + 1) * DH)
        grad = jnp.where(side == parity, own_ref[:, cols], other_ref[:, cols])
        for start, tile, upto in tiles_of(q_ref.shape[0]):
            query = q_ref[start : start + tile, h * DH : (h + 1) * DH]
            probs, cap_tanh = softmax_tile(
                k_ref[:upto, :], query, mask_ref[:upto, start : start + tile]
            )
            grad_rows = grad[start : start + tile, :]
            grad_probs = dot(v_ref[:upto, :], grad_rows, NT)
            delta = jnp.sum(probs * grad_probs, axis=0, keepdims=True)
            scores = probs * (grad_probs - delta) * (SCALE - SCALE * (cap_tanh * cap_tanh))
            scores = scores.astype(BF16)
            av_ref[:upto, :] += dot(probs.astype(BF16), grad_rows, NN)
            ak_ref[:upto, :] += dot(scores, query, NN)
            grad_query = dot(key_t[:, :upto], scores, NN).T
            gq_ref[start : start + tile, h * DH : (h + 1) * DH] = grad_query.astype(BF16)
    gk_ref[...] = ak_ref[...].astype(BF16)
    gv_ref[...] = av_ref[...].astype(BF16)


def backward(sc, k, block, own, other, column, before, lay, through):
    queries, keys, values, seg_row, seg_col = block
    length = queries.shape[0]
    per = lay.heads_shard
    groups = 2 * per // REPEAT
    at = lay.at_z + k

    def whole(i, sc):
        return (0, sc[at] * groups + i)

    heads = (length, REPEAT * DH), whole
    one = (length, DH), whole
    return call(
        functools.partial(backward_body, per),
        sc,
        (groups,),
        [
            (queries, *heads),
            (keys, *one),
            (values, *one),
            (seg_row, (1, length), first),
            (seg_col, (length, 1), first),
            (own, (length, lay.rows), lambda i, sc: (0, column)),
            (other, (length, lay.rows), lambda i, sc: (0, column)),
        ],
        [(queries.shape, BF16, *heads), (keys.shape, BF16, *one), (values.shape, BF16, *one)],
        scratch=[
            pltpu.VMEM((length, length), F32),
            pltpu.VMEM((length, DH), F32),
            pltpu.VMEM((length, DH), F32),
        ],
        before=before,
        through=through,
    )


def adam_body(pieces, tokens, sc_ref, m1_ref, m2_ref, *refs):
    out_ref = refs[-1]
    n = pl.program_id(0)

    def step(piece_ref):
        gradient = piece_ref[...].astype(F32) * (1.0 / tokens)
        moment_one = 0.9 * m1_ref[...] + 0.1 * gradient
        moment_two = 0.95 * m2_ref[...] + 0.05 * gradient * gradient
        out_ref[...] = moment_one / (jnp.sqrt(moment_two) + 1e-08)

    for p in range(pieces):
        pl.when(n == p)(functools.partial(step, refs[p]))


def adam(sc, pieces, first_moment, second_moment, tokens, lay, before, through):
    rows, width = pieces[0][0].shape
    count = len(pieces)
    columns = [lay.at_place(flips) for _, flips in pieces]

    def at(n, m, sc):
        row = sc[columns[0]]
        for p in range(1, count):
            row = jnp.where(n == p, sc[columns[p]], row)
        return (row, m)

    def of(p):
        return lambda n, m, sc: (0, jnp.where(n == p, m, jnp.where(n < p, 0, 1)))

    block = (rows, width // 2)
    return call(
        functools.partial(adam_body, count, tokens),
        sc,
        (count, 2),
        [(first_moment, block, at), (second_moment, block, at)]
        + [(x, block, of(p)) for p, (x, _) in enumerate(pieces)],
        [(first_moment.shape, F32, block, at)],
        before=before,
        through=through,
        mib=60,
    )


class Layout:
    def __init__(self, replicas, shards, rows):
        self.replicas, self.shards, self.rows = replicas, shards, rows
        self.z = shards // 2
        self.bits = replicas.bit_length() - 1
        self.heads_shard = HEADS // shards
        self.order = [0] + list(range(1, self.z, 2)) + list(range(self.z - 2, 0, -2))
        self.place = [self.order.index(z) for z in range(self.z)]
        self.at_z = 1
        self.at_piece = self.at_z + self.z
        table = []
        for r in range(replicas):
            for s in range(shards):
                z, core = s // 2, s % 2
                zs = [self.order[(self.place[z] - k) % self.z] for k in range(self.z)]
                bits = [(r >> self.bit_of(core, n)) & 1 for n in range(self.bits)]
                b = 2 * bits[0]
                here = sum(bit << n for n, bit in enumerate(bits[::-1]))
                places = [here ^ flips for flips in range(replicas)]
                table.append([core] + zs + [b, b + 1, 2 - b, 3 - b] + bits + places)
        self.table = np.array(table, np.int32)

    def bit_of(self, core, n):
        return self.bits - 1 - n if core else n

    def at_bit(self, n):
        return self.at_piece + 4 + n

    def at_place(self, flips):
        code = sum(int(f) << n for n, f in enumerate(flips[::-1]))
        return self.at_piece + 4 + self.bits + code

    def sibling(self, x):
        return lax.ppermute(x, "shard", [(s, s ^ 1) for s in range(self.shards)])

    def onward(self, x):
        perm = []
        for p in range(self.z):
            a, b = self.order[p], self.order[(p + 1) % self.z]
            perm += [(2 * a + core, 2 * b + core) for core in range(2)]
        return lax.ppermute(x, "shard", perm)

    def backward(self, x):
        perm = []
        for p in range(self.z):
            a, b = self.order[p], self.order[p - 1]
            perm += [(2 * a + core, 2 * b + core) for core in range(2)]
        return lax.ppermute(x, "shard", perm)

    def across(self, x, n):
        perm = []
        for r in range(self.replicas):
            for s in range(self.shards):
                partner = r ^ (1 << self.bit_of(s % 2, n))
                perm.append((r * self.shards + s, partner * self.shards + s))
        return lax.ppermute(x, ("replica", "shard"), perm)


def per_device(queries, keys, values, segments, out_weight, upstream, first_moment, second_moment):
    length, width = upstream.shape
    lay = Layout(lax.axis_size("replica"), lax.axis_size("shard"), out_weight.shape[0])
    tokens = length * lay.replicas * lay.shards
    device = lax.axis_index("replica") * lay.shards + lax.axis_index("shard")
    sc = lax.dynamic_index_in_dim(jnp.asarray(lay.table), device, 0, keepdims=False)
    block = (queries, keys, values, segments, segments.reshape(length, 1))

    box = {}
    terms = {}
    gc = {}
    grads = ()

    def run(function, *args, held=(), **more):
        names = ["token", *held]
        outs, handed = function(*args, through=[box[n] for n in names], **more)
        box.update(zip(names, handed))
        return outs

    def do_product(k, held=()):
        own, other = contexts[k]
        box["send", k], keep = run(
            product, sc, own, other, upstream, upstream_other, lay, held=held
        )
        terms[k] = [keep]

    def send(k):
        terms[k].append(lay.across(box["send", k], len(terms[k]) - 1))

    def do_halve(k, held=()):
        for stage in range(1, lay.bits):
            (box["send", k],) = run(combine, sc, terms[k], None, True, lay, held=held)
            held = ()
            if stage < lay.bits - 1:
                send(k)

    def do_sum(k, held=()):
        (box["sum", k],) = run(combine, sc, terms[k], box.get(("part", k)), False, lay, held=held)

    def pass_sum(k):
        box["part", (k + 1) % lay.z] = lay.onward(box["sum", k])

    def pass_weights(k):
        if k < middle:
            box["ring", k + 1] = lay.onward(box["ring", k])
        elif k > middle + 1:
            box["ring", k - 1] = lay.backward(box["ring", k])

    def cross_weights(k):
        box["cross", k] = lay.across(box["ring", k], 0)

    def do_grad_context(ks, held=()):
        sets = [[box["ring", k], box["cross", k]] if k else [out_weight] for k in ks]
        own, box["away", ks[0]] = run(
            grad_context, sc, upstream, upstream_other, sets, lay, held=held
        )
        for n, k in enumerate(ks):
            gc[k] = own, ks[0], n

    def swap_grad_context(k):
        box["gc", k] = lay.sibling(box["away", k])

    def do_backward(k, held=()):
        nonlocal grads
        own, base, column = gc[k]
        grads = run(backward, sc, k, block, own, box["gc", base], column, grads, lay, held=held)

    upstream_other = lay.sibling(upstream)
    middle, last = lay.z // 2, lay.z - 1
    half, box["token"] = cut(sc, out_weight, lay)[0]
    box["ring", 1] = lay.onward(half)
    box["ring", last] = lay.backward(half)

    late = [*range(2, lay.z), 0]
    rows = lay.rows
    contexts = {}
    (both_sides,) = run(forward, sc, [1], [0, 1], block, lay)
    contexts[1] = (both_sides, 1), (lay.sibling(both_sides[:rows]), 0)
    do_product(1)
    send(1)
    (both_sides,) = run(forward, sc, late, [0, 1], block, lay)
    box["context"] = lay.sibling(both_sides[: len(late) * rows])
    do_halve(1, held=[("ring", 1), "context"])
    send(1)
    pass_weights(1)
    cross_weights(1)
    for n, k in enumerate(late):
        contexts[k] = (both_sides, len(late) + n), (box["context"], n)
    do_product(2)
    send(2)
    do_product(3)
    send(3)
    do_sum(1)
    pass_sum(1)
    do_grad_context([0, 1])
    swap_grad_context(0)
    do_halve(2, held=[("ring", last)])
    send(2)
    pass_weights(last)
    cross_weights(last)
    do_backward(0)
    do_product(0)
    do_halve(3)
    send(3)
    do_backward(1, held=[("send", 0)])
    send(0)
    for j in range(2, middle):
        run(relay, sc, held=[("ring", j), ("ring", lay.z - j)])
        pass_weights(j)
        pass_weights(lay.z - j)
        cross_weights(j)
        cross_weights(lay.z - j)
    do_sum(2, held=[("ring", middle)])
    pass_sum(2)
    cross_weights(middle)
    for k in range(4, lay.z):
        do_product(k)
        send(k)
        do_halve(k)
        send(k)
    do_grad_context([last])
    swap_grad_context(last)
    do_sum(3)
    pass_sum(3)
    do_backward(last)
    for k in range(4, lay.z):
        do_sum(k)
        pass_sum(k)
    for k in range(2, last):
        if k != middle:
            do_grad_context([k])
            swap_grad_context(k)
            do_backward(k)
    do_halve(0)
    send(0)
    do_grad_context([middle])
    swap_grad_context(middle)
    do_sum(0)

    have = [(box["sum", 0], (False,) * lay.bits)]

    def spread(n, piece):
        x, flips = piece
        return lay.across(x, n), flips[:n] + (True,) + flips[n + 1 :]

    moments = first_moment, second_moment, tokens, lay
    direct = [spread(n, have[0]) for n in range(lay.bits - 1, -1, -1)]
    do_backward(middle)
    step = run(adam, sc, have, *moments, before=())
    box["got"] = direct[0][0]
    run(relay, sc, held=["got"])
    direct[0] = (box["got"], direct[0][1])
    near = [have[0], *direct]
    have = [have[0], direct[0]]
    done = {flips for _, flips in near}
    far = []
    for n in range(lay.bits - 2, -1, -1):
        more = []
        for x, flips in have:
            flips = flips[:n] + (True,) + flips[n + 1 :]
            if flips in done:
                more += [p for p in near if p[1] == flips]
            else:
                more.append((lay.across(x, n), flips))
                far.append(more[-1])
        have += more
    step = run(adam, sc, direct, *moments, before=step)
    step = run(adam, sc, far, *moments, before=step)
    return (*grads, *step)


def solution(mesh):
    both = P(("replica", "shard"), None)
    shard = P("shard", None)
    return jax.shard_map(
        per_device,
        mesh=mesh,
        in_specs=(both, both, both, both, shard, both, shard, shard),
        out_specs=(both, both, both, shard),
        check_vma=False,
    )
```

```python
import functools

import jax
import jax.numpy as jnp
import numpy as np
from jax import lax
from jax.experimental import pallas as pl
from jax.experimental.pallas import tpu as pltpu
from jax.sharding import PartitionSpec as P

HEADS = 16
KV_HEADS = 8
DH = 128
REPEAT = HEADS // KV_HEADS

SCALE = 1.0 / 12.0
CAP = 50.0
MIB = 1024 * 1024
F32 = jnp.float32
BF16 = jnp.bfloat16

NT = (((1,), (1,)), ((), ()))
NN = (((1,), (0,)), ((), ()))


def dot(a, b, dims):
    return lax.dot_general(a, b, dims, preferred_element_type=F32)


def call(body, sc, grid, ins, outs, scratch=(), through=(), before=(), mib=20):
    n_in, n_out, n_before, n_through = len(ins), len(outs), len(before), len(through)

    def kernel(sc_ref, *refs):
        at = n_in + n_before + n_through
        body(sc_ref, *refs[:n_in], *refs[at : at + n_out], *refs[at + n_out + n_through :])

    anywhere = pl.BlockSpec(memory_space=pl.ANY)
    stay = pl.BlockSpec(memory_space=pltpu.HBM)
    aliases = {1 + n_in + n: n for n in range(n_before)}
    aliases.update({1 + n_in + n_before + n: n_out + n for n in range(n_through)})
    results = pl.pallas_call(
        kernel,
        grid_spec=pltpu.PrefetchScalarGridSpec(
            num_scalar_prefetch=1,
            grid=grid,
            in_specs=[pl.BlockSpec(block, index) for _, block, index in ins]
            + [anywhere] * n_before
            + [stay] * n_through,
            out_specs=[pl.BlockSpec(block, index) for _, _, block, index in outs]
            + [stay] * n_through,
            scratch_shapes=list(scratch),
        ),
        out_shape=[jax.ShapeDtypeStruct(shape, dtype) for shape, dtype, _, _ in outs]
        + [jax.ShapeDtypeStruct(x.shape, x.dtype) for x in through],
        input_output_aliases=aliases,
        cost_estimate=pl.CostEstimate(flops=1, transcendentals=0, bytes_accessed=1),
        compiler_params=pltpu.CompilerParams(vmem_limit_bytes=mib * MIB),
    )(sc, *[array for array, _, _ in ins], *before, *through)
    return results[:n_out], results[n_out:]


def first(*_):
    return (0, 0)


def fill_mask(mask_ref, seg_row_ref, seg_col_ref):
    length = mask_ref.shape[0]
    j = lax.broadcasted_iota(jnp.int32, (length, length), 0)
    i = lax.broadcasted_iota(jnp.int32, (length, length), 1)
    allowed = (j <= i) & (seg_col_ref[...] == seg_row_ref[...])
    mask_ref[...] = jnp.where(allowed, 1.0, 0.0).astype(F32)


def tiles_of(length):
    tile = 256
    return [(t * tile, tile, (t + 1) * tile) for t in range(length // tile)]


def softmax_tile(key, query, mask):
    cap_tanh = jnp.tanh(dot(key, query, NT) * (SCALE / CAP))
    weights = jnp.exp(cap_tanh * CAP) * mask
    inverse = 1.0 / jnp.sum(weights, axis=0, keepdims=True)
    return weights * inverse, cap_tanh


def cut_body(sc_ref, in_ref, out_ref, token_ref):
    out_ref[...] = in_ref[...]
    token_ref[...] = jnp.zeros_like(token_ref)


def cut(sc, weight, lay):
    block = (weight.shape[0], weight.shape[1] // 2)
    return call(
        cut_body,
        sc,
        (1,),
        [(weight, block, lambda n, sc: (0, sc[lay.at_bit(0)]))],
        [(block, BF16, block, first), ((8, 128), F32, (8, 128), first)],
    )


def relay_body(sc_ref):
    pass


def relay(sc, through):
    return call(relay_body, sc, (1,), [], [], through=through)


def forward_body(heads, sc_ref, q_ref, k_ref, v_ref, seg_row_ref, seg_col_ref, out_ref, mask_ref):
    @pl.when(pl.program_id(0) == 0)
    def _():
        fill_mask(mask_ref, seg_row_ref, seg_col_ref)

    value_t = v_ref[...].T
    for h in range(heads):
        for start, tile, upto in tiles_of(q_ref.shape[0]):
            probs, _ = softmax_tile(
                k_ref[:upto, :],
                q_ref[start : start + tile, h * DH : (h + 1) * DH],
                mask_ref[:upto, start : start + tile],
            )
            context = dot(value_t[:, :upto], probs.astype(BF16), NN)
            out_ref[h * DH : (h + 1) * DH, start : start + tile] = context.astype(BF16)


def forward(sc, ks, sides, block, lay, through):
    queries, keys, values, seg_row, seg_col = block
    length = queries.shape[0]
    per = lay.heads_shard
    count = len(ks)

    def shard_of(i, sc):
        k = lax.rem(ks[0] + lax.rem(i, count), lay.z)
        if len(sides) == 2:
            own = i >= count
        else:
            own = sides[0] == 1
        return 2 * sc[lay.at_z + k] + jnp.where(own, sc[0], 1 - sc[0])

    def kv_of(i, sc):
        return (0, (shard_of(i, sc) * per) // REPEAT)

    rows = per * DH
    steps = count * len(sides)
    return call(
        functools.partial(forward_body, per),
        sc,
        (steps,),
        [
            (queries, (length, rows), lambda i, sc: (0, shard_of(i, sc))),
            (keys, (length, DH), kv_of),
            (values, (length, DH), kv_of),
            (seg_row, (1, length), first),
            (seg_col, (length, 1), first),
        ],
        [((steps * rows, length), BF16, (rows, length), lambda i, sc: (i, 0))],
        scratch=[pltpu.VMEM((length, length), F32)],
        through=through,
    )


def product_body(at_bit, sc_ref, c0_ref, c1_ref, u0_ref, u1_ref, send_ref, keep_ref, acc_ref):
    half = acc_ref.shape[0] // 2
    acc = dot(c0_ref[...], u0_ref[...], NN) + dot(c1_ref[...], u1_ref[...], NN)
    acc_ref[...] = acc.astype(BF16)
    bit = sc_ref[at_bit]
    keep_ref[...] = acc_ref[pl.ds(pl.multiple_of(bit * half, half), half), :]
    send_ref[...] = acc_ref[pl.ds(pl.multiple_of((1 - bit) * half, half), half), :]


def product(sc, own, other, up0, up1, lay, through):
    length, width = up0.shape
    rows = lay.rows
    tile = width // 4
    out = ((rows // 2, width), BF16, (rows // 2, tile), lambda n, sc: (0, n))
    return call(
        functools.partial(product_body, lay.at_bit(0)),
        sc,
        (4,),
        [(x, (rows, length), lambda n, sc, at=at: (at, 0)) for x, at in (own, other)]
        + [(u, (length, tile), lambda n, sc: (0, n)) for u in (up0, up1)],
        [out, out],
        scratch=[pltpu.VMEM((rows, tile), BF16)],
        through=through,
    )


def combine_body(sc_ref, *refs):
    total = refs[0][...].astype(F32)
    for ref in refs[1:-1]:
        total = total + ref[...].astype(F32)
    refs[-1][...] = total.astype(BF16)


def combine(sc, terms, ring, away, lay, through):
    deep = len(terms) if away else lay.bits
    width = terms[0].shape[1]
    size = lay.rows >> deep
    ins = []

    def place(level):
        def index(n, sc):
            at = 0
            for m in range(level, deep):
                bit = sc[lay.at_bit(m)]
                at = 2 * at + (1 - bit if away and m == deep - 1 else bit)
            return (at, 0)

        return index

    for m, x in enumerate(terms):
        ins.append((x, (size, width), place(max(m, 1))))
    if ring is not None:
        ins.append((ring, (size, width), first))
    out = ((size, width), BF16, (size, width), first)
    return call(combine_body, sc, (1,), ins, [out], through=through)


def grad_context_body(sets, sc_ref, u0_ref, u1_ref, *refs):
    weights, (g0_ref, g1_ref, a0_ref, a1_ref) = refs[:-4], refs[-4:]
    n = pl.program_id(0)
    rows = a0_ref.shape[1] // len(sets)

    def add(weight_ref, cols):
        d0 = dot(u0_ref[...], weight_ref[...], NT)
        d1 = dot(u1_ref[...], weight_ref[...], NT)

        @pl.when(n == 0)
        def _():
            a0_ref[:, cols] = d0
            a1_ref[:, cols] = d1

        @pl.when(n > 0)
        def _():
            a0_ref[:, cols] += d0
            a1_ref[:, cols] += d1

    at = 0
    for index, count in enumerate(sets):
        cols = slice(index * rows, (index + 1) * rows)
        if count == 1:
            add(weights[at], cols)
        else:
            pl.when(n < 2)(functools.partial(add, weights[at], cols))
            pl.when(n >= 2)(functools.partial(add, weights[at + 1], cols))
        at += count

    @pl.when(n == 3)
    def _():
        g0_ref[...] = a0_ref[...].astype(BF16)
        g1_ref[...] = a1_ref[...].astype(BF16)


def grad_context(sc, up0, up1, weight_sets, lay, through):
    length, width = up0.shape
    rows, tile = lay.rows, width // 4
    total = rows * len(weight_sets)
    at = lay.at_piece
    ins = [(u, (length, tile), lambda n, sc: (0, sc[at + n])) for u in (up0, up1)]
    for weights in weight_sets:
        if len(weights) == 1:
            ins.append((weights[0], (rows, tile), lambda n, sc: (0, sc[at + n])))
        else:
            ins.append((weights[0], (rows, tile), lambda n, sc: (0, jnp.minimum(n, 1))))
            ins.append((weights[1], (rows, tile), lambda n, sc: (0, jnp.maximum(n - 2, 0))))
    return call(
        functools.partial(grad_context_body, [len(w) for w in weight_sets]),
        sc,
        (4,),
        ins,
        [((length, total), BF16, (length, total), first)] * 2,
        scratch=[pltpu.VMEM((length, total), F32)] * 2,
        through=through,
        mib=28,
    )


def backward_body(
    per, sc_ref, q_ref, k_ref, v_ref, seg_row_ref, seg_col_ref, own_ref, other_ref, *refs
):
    gq_ref, gk_ref, gv_ref, mask_ref, ak_ref, av_ref = refs[-6:]
    group = pl.program_id(0)
    parity = sc_ref[0]

    @pl.when(group == 0)
    def _():
        fill_mask(mask_ref, seg_row_ref, seg_col_ref)

    key_t = k_ref[...].T
    ak_ref[...] = jnp.zeros_like(ak_ref)
    av_ref[...] = jnp.zeros_like(av_ref)
    for h in range(REPEAT):
        side = group if per == REPEAT else h
        column = h if per == REPEAT else 0
        cols = slice(column * DH, (column + 1) * DH)
        grad = jnp.where(side == parity, own_ref[:, cols], other_ref[:, cols])
        for start, tile, upto in tiles_of(q_ref.shape[0]):
            query = q_ref[start : start + tile, h * DH : (h + 1) * DH]
            probs, cap_tanh = softmax_tile(
                k_ref[:upto, :], query, mask_ref[:upto, start : start + tile]
            )
            grad_rows = grad[start : start + tile, :]
            grad_probs = dot(v_ref[:upto, :], grad_rows, NT)
            delta = jnp.sum(probs * grad_probs, axis=0, keepdims=True)
            scores = probs * (grad_probs - delta) * (SCALE - SCALE * (cap_tanh * cap_tanh))
            scores = scores.astype(BF16)
            av_ref[:upto, :] += dot(probs.astype(BF16), grad_rows, NN)
            ak_ref[:upto, :] += dot(scores, query, NN)
            grad_query = dot(key_t[:, :upto], scores, NN).T
            gq_ref[start : start + tile, h * DH : (h + 1) * DH] = grad_query.astype(BF16)
    gk_ref[...] = ak_ref[...].astype(BF16)
    gv_ref[...] = av_ref[...].astype(BF16)


def backward(sc, k, block, own, other, column, before, lay, through):
    queries, keys, values, seg_row, seg_col = block
    length = queries.shape[0]
    per = lay.heads_shard
    groups = 2 * per // REPEAT
    at = lay.at_z + k

    def whole(i, sc):
        return (0, sc[at] * groups + i)

    heads = (length, REPEAT * DH), whole
    one = (length, DH), whole
    return call(
        functools.partial(backward_body, per),
        sc,
        (groups,),
        [
            (queries, *heads),
            (keys, *one),
            (values, *one),
            (seg_row, (1, length), first),
            (seg_col, (length, 1), first),
            (own, (length, lay.rows), lambda i, sc: (0, column)),
            (other, (length, lay.rows), lambda i, sc: (0, column)),
        ],
        [(queries.shape, BF16, *heads), (keys.shape, BF16, *one), (values.shape, BF16, *one)],
        scratch=[
            pltpu.VMEM((length, length), F32),
            pltpu.VMEM((length, DH), F32),
            pltpu.VMEM((length, DH), F32),
        ],
        before=before,
        through=through,
    )


def adam_body(pieces, tokens, sc_ref, m1_ref, m2_ref, *refs):
    out_ref = refs[-1]
    n = pl.program_id(0)

    def step(piece_ref):
        gradient = piece_ref[...].astype(F32) * (1.0 / tokens)
        moment_one = 0.9 * m1_ref[...] + 0.1 * gradient
        moment_two = 0.95 * m2_ref[...] + 0.05 * gradient * gradient
        out_ref[...] = moment_one / (jnp.sqrt(moment_two) + 1e-08)

    for p in range(pieces):
        pl.when(n == p)(functools.partial(step, refs[p]))


def adam(sc, pieces, first_moment, second_moment, tokens, lay, before, through):
    rows, width = pieces[0][0].shape
    count = len(pieces)
    columns = [lay.at_place(flips) for _, flips in pieces]

    def at(n, m, sc):
        row = sc[columns[0]]
        for p in range(1, count):
            row = jnp.where(n == p, sc[columns[p]], row)
        return (row, m)

    def of(p):
        return lambda n, m, sc: (0, jnp.where(n == p, m, jnp.where(n < p, 0, 1)))

    block = (rows, width // 2)
    return call(
        functools.partial(adam_body, count, tokens),
        sc,
        (count, 2),
        [(first_moment, block, at), (second_moment, block, at)]
        + [(x, block, of(p)) for p, (x, _) in enumerate(pieces)],
        [(first_moment.shape, F32, block, at)],
        before=before,
        through=through,
        mib=60,
    )


class Layout:
    def __init__(self, replicas, shards, rows):
        self.replicas, self.shards, self.rows = replicas, shards, rows
        self.z = shards // 2
        self.bits = replicas.bit_length() - 1
        self.heads_shard = HEADS // shards
        self.order = [0] + list(range(1, self.z, 2)) + list(range(self.z - 2, 0, -2))
        self.place = [self.order.index(z) for z in range(self.z)]
        self.at_z = 1
        self.at_piece = self.at_z + self.z
        table = []
        for r in range(replicas):
            for s in range(shards):
                z, core = s // 2, s % 2
                zs = [self.order[(self.place[z] - k) % self.z] for k in range(self.z)]
                bits = [(r >> self.bit_of(core, n)) & 1 for n in range(self.bits)]
                b = 2 * bits[0]
                here = sum(bit << n for n, bit in enumerate(bits[::-1]))
                places = [here ^ flips for flips in range(replicas)]
                table.append([core] + zs + [b, b + 1, 2 - b, 3 - b] + bits + places)
        self.table = np.array(table, np.int32)

    def bit_of(self, core, n):
        return self.bits - 1 - n if core else n

    def at_bit(self, n):
        return self.at_piece + 4 + n

    def at_place(self, flips):
        code = sum(int(f) << n for n, f in enumerate(flips[::-1]))
        return self.at_piece + 4 + self.bits + code

    def sibling(self, x):
        return lax.ppermute(x, "shard", [(s, s ^ 1) for s in range(self.shards)])

    def onward(self, x):
        perm = []
        for p in range(self.z):
            a, b = self.order[p], self.order[(p + 1) % self.z]
            perm += [(2 * a + core, 2 * b + core) for core in range(2)]
        return lax.ppermute(x, "shard", perm)

    def across(self, x, n):
        perm = []
        for r in range(self.replicas):
            for s in range(self.shards):
                partner = r ^ (1 << self.bit_of(s % 2, n))
                perm.append((r * self.shards + s, partner * self.shards + s))
        return lax.ppermute(x, ("replica", "shard"), perm)


def per_device(queries, keys, values, segments, out_weight, upstream, first_moment, second_moment):
    length, width = upstream.shape
    lay = Layout(lax.axis_size("replica"), lax.axis_size("shard"), out_weight.shape[0])
    tokens = length * lay.replicas * lay.shards
    device = lax.axis_index("replica") * lay.shards + lax.axis_index("shard")
    sc = lax.dynamic_index_in_dim(jnp.asarray(lay.table), device, 0, keepdims=False)
    block = (queries, keys, values, segments, segments.reshape(length, 1))

    box = {}
    terms = {}
    gc = {}
    grads = ()

    def run(function, *args, held=(), **more):
        names = ["token", *held]
        outs, handed = function(*args, through=[box[n] for n in names], **more)
        box.update(zip(names, handed))
        return outs

    def do_product(k, held=()):
        own, other = contexts[k]
        box["send", k], keep = run(
            product, sc, own, other, upstream, upstream_other, lay, held=held
        )
        terms[k] = [keep]

    def send(k):
        terms[k].append(lay.across(box["send", k], len(terms[k]) - 1))

    def do_halve(k, held=()):
        for stage in range(1, lay.bits):
            (box["send", k],) = run(combine, sc, terms[k], None, True, lay, held=held)
            held = ()
            if stage < lay.bits - 1:
                send(k)

    def do_sum(k, held=()):
        (box["sum", k],) = run(combine, sc, terms[k], box.get(("part", k)), False, lay, held=held)

    def pass_sum(k):
        box["part", (k + 1) % lay.z] = lay.onward(box["sum", k])

    def pass_weights(k):
        if k + 1 < lay.z:
            box["ring", k + 1] = lay.onward(box["ring", k])

    def cross_weights(k):
        box["cross", k] = lay.across(box["ring", k], 0)

    def do_grad_context(ks, held=()):
        sets = [[box["ring", k], box["cross", k]] if k else [out_weight] for k in ks]
        own, box["away", ks[0]] = run(
            grad_context, sc, upstream, upstream_other, sets, lay, held=held
        )
        for n, k in enumerate(ks):
            gc[k] = own, ks[0], n

    def swap_grad_context(k):
        box["gc", k] = lay.sibling(box["away", k])

    def do_backward(k, held=()):
        nonlocal grads
        own, base, column = gc[k]
        grads = run(backward, sc, k, block, own, box["gc", base], column, grads, lay, held=held)

    upstream_other = lay.sibling(upstream)
    box["ring", 1], box["token"] = cut(sc, out_weight, lay)[0]
    box["ring", 1] = lay.onward(box["ring", 1])

    late = [*range(2, lay.z), 0]
    rows = lay.rows
    contexts = {}
    (both_sides,) = run(forward, sc, [1], [0, 1], block, lay)
    contexts[1] = (both_sides, 1), (lay.sibling(both_sides[:rows]), 0)
    do_product(1)
    send(1)
    (both_sides,) = run(forward, sc, late, [0, 1], block, lay)
    box["context"] = lay.sibling(both_sides[: len(late) * rows])
    do_halve(1, held=[("ring", 1), "context"])
    send(1)
    pass_weights(1)
    cross_weights(1)
    for n, k in enumerate(late):
        contexts[k] = (both_sides, len(late) + n), (box["context"], n)
    do_product(2)
    do_sum(1)
    pass_sum(1)
    send(2)
    do_product(3)
    send(3)
    do_grad_context([0, 1])
    swap_grad_context(0)
    run(relay, sc, held=[("ring", 2)])
    pass_weights(2)
    cross_weights(2)
    do_halve(2)
    send(2)
    do_backward(0)
    do_product(0)
    do_halve(3)
    send(3)
    do_backward(1, held=[("send", 0)])
    send(0)
    do_sum(2)
    pass_sum(2)
    for k in range(4, lay.z):
        do_product(k, held=[("ring", k - 1)])
        pass_weights(k - 1)
        cross_weights(k - 1)
        send(k)
        do_halve(k)
        send(k)
    last = lay.z - 1
    do_grad_context([2])
    swap_grad_context(2)
    do_sum(3, held=[("ring", last)])
    pass_sum(3)
    cross_weights(last)
    do_backward(2)
    for k in range(4, lay.z):
        do_sum(k)
        pass_sum(k)
    for k in range(3, last):
        do_grad_context([k])
        swap_grad_context(k)
        do_backward(k)
    do_halve(0)
    send(0)
    do_grad_context([last])
    swap_grad_context(last)
    do_sum(0)

    have = [(box["sum", 0], (False,) * lay.bits)]

    def spread(n, piece):
        x, flips = piece
        return lay.across(x, n), flips[:n] + (True,) + flips[n + 1 :]

    moments = first_moment, second_moment, tokens, lay
    direct = [spread(n, have[0]) for n in range(lay.bits - 1, -1, -1)]
    do_backward(last)
    step = run(adam, sc, have, *moments, before=())
    box["got"] = direct[0][0]
    run(relay, sc, held=["got"])
    direct[0] = (box["got"], direct[0][1])
    near = [have[0], *direct]
    have = [have[0], direct[0]]
    done = {flips for _, flips in near}
    far = []
    for n in range(lay.bits - 2, -1, -1):
        more = []
        for x, flips in have:
            flips = flips[:n] + (True,) + flips[n + 1 :]
            if flips in done:
                more += [p for p in near if p[1] == flips]
            else:
                more.append((lay.across(x, n), flips))
                far.append(more[-1])
        have += more
    step = run(adam, sc, direct, *moments, before=step)
    step = run(adam, sc, far, *moments, before=step)
    return (*grads, *step)


def solution(mesh):
    both = P(("replica", "shard"), None)
    shard = P("shard", None)
    return jax.shard_map(
        per_device,
        mesh=mesh,
        in_specs=(both, both, both, both, shard, both, shard, shard),
        out_specs=(both, both, both, shard),
        check_vma=False,
    )
```

```python
import functools

import jax
import jax.numpy as jnp
import numpy as np
from jax import lax
from jax.experimental import pallas as pl
from jax.experimental.pallas import tpu as pltpu
from jax.sharding import PartitionSpec as P

HEADS = 16
KV_HEADS = 8
DH = 128
REPEAT = HEADS // KV_HEADS

SCALE = 1.0 / 12.0
CAP = 50.0
MIB = 1024 * 1024
F32 = jnp.float32
BF16 = jnp.bfloat16

NT = (((1,), (1,)), ((), ()))
NN = (((1,), (0,)), ((), ()))


def dot(a, b, dims):
    return lax.dot_general(a, b, dims, preferred_element_type=F32)


def call(body, sc, grid, ins, outs, scratch=(), through=(), before=(), mib=20):
    n_in, n_out, n_before, n_through = len(ins), len(outs), len(before), len(through)

    def kernel(sc_ref, *refs):
        at = n_in + n_before + n_through
        body(sc_ref, *refs[:n_in], *refs[at : at + n_out], *refs[at + n_out + n_through :])

    anywhere = pl.BlockSpec(memory_space=pl.ANY)
    stay = pl.BlockSpec(memory_space=pltpu.HBM)
    aliases = {1 + n_in + n: n for n in range(n_before)}
    aliases.update({1 + n_in + n_before + n: n_out + n for n in range(n_through)})
    results = pl.pallas_call(
        kernel,
        grid_spec=pltpu.PrefetchScalarGridSpec(
            num_scalar_prefetch=1,
            grid=grid,
            in_specs=[pl.BlockSpec(block, index) for _, block, index in ins]
            + [anywhere] * n_before
            + [stay] * n_through,
            out_specs=[pl.BlockSpec(block, index) for _, _, block, index in outs]
            + [stay] * n_through,
            scratch_shapes=list(scratch),
        ),
        out_shape=[jax.ShapeDtypeStruct(shape, dtype) for shape, dtype, _, _ in outs]
        + [jax.ShapeDtypeStruct(x.shape, x.dtype) for x in through],
        input_output_aliases=aliases,
        cost_estimate=pl.CostEstimate(flops=1, transcendentals=0, bytes_accessed=1),
        compiler_params=pltpu.CompilerParams(vmem_limit_bytes=mib * MIB),
    )(sc, *[array for array, _, _ in ins], *before, *through)
    return results[:n_out], results[n_out:]


def first(*_):
    return (0, 0)


def fill_mask(mask_ref, seg_row_ref, seg_col_ref):
    length = mask_ref.shape[0]
    j = lax.broadcasted_iota(jnp.int32, (length, length), 0)
    i = lax.broadcasted_iota(jnp.int32, (length, length), 1)
    allowed = (j <= i) & (seg_col_ref[...] == seg_row_ref[...])
    mask_ref[...] = jnp.where(allowed, 1.0, 0.0).astype(F32)


def tiles_of(length):
    tile = 256
    return [(t * tile, tile, (t + 1) * tile) for t in range(length // tile)]


def softmax_tile(key, query, mask):
    cap_tanh = jnp.tanh(dot(key, query, NT) * (SCALE / CAP))
    weights = jnp.exp(cap_tanh * CAP) * mask
    inverse = 1.0 / jnp.sum(weights, axis=0, keepdims=True)
    return weights * inverse, cap_tanh


def cut_body(sc_ref, in_ref, out_ref, token_ref):
    out_ref[...] = in_ref[...]
    token_ref[...] = jnp.zeros_like(token_ref)


def cut(sc, weight, lay):
    block = (weight.shape[0], weight.shape[1] // 2)
    return call(
        cut_body,
        sc,
        (1,),
        [(weight, block, lambda n, sc: (0, sc[lay.at_bit(0)]))],
        [(block, BF16, block, first), ((8, 128), F32, (8, 128), first)],
    )


def relay_body(sc_ref):
    pass


def relay(sc, through):
    return call(relay_body, sc, (1,), [], [], through=through)


def forward_body(heads, sc_ref, q_ref, k_ref, v_ref, seg_row_ref, seg_col_ref, out_ref, mask_ref):
    @pl.when(pl.program_id(0) == 0)
    def _():
        fill_mask(mask_ref, seg_row_ref, seg_col_ref)

    value_t = v_ref[...].T
    for h in range(heads):
        for start, tile, upto in tiles_of(q_ref.shape[0]):
            probs, _ = softmax_tile(
                k_ref[:upto, :],
                q_ref[start : start + tile, h * DH : (h + 1) * DH],
                mask_ref[:upto, start : start + tile],
            )
            context = dot(value_t[:, :upto], probs.astype(BF16), NN)
            out_ref[h * DH : (h + 1) * DH, start : start + tile] = context.astype(BF16)


def forward(sc, ks, sides, block, lay, through):
    queries, keys, values, seg_row, seg_col = block
    length = queries.shape[0]
    per = lay.heads_shard
    count = len(ks)

    def shard_of(i, sc):
        k = lax.rem(ks[0] + lax.rem(i, count), lay.z)
        if len(sides) == 2:
            own = i >= count
        else:
            own = sides[0] == 1
        return 2 * sc[lay.at_z + k] + jnp.where(own, sc[0], 1 - sc[0])

    def kv_of(i, sc):
        return (0, (shard_of(i, sc) * per) // REPEAT)

    rows = per * DH
    steps = count * len(sides)
    return call(
        functools.partial(forward_body, per),
        sc,
        (steps,),
        [
            (queries, (length, rows), lambda i, sc: (0, shard_of(i, sc))),
            (keys, (length, DH), kv_of),
            (values, (length, DH), kv_of),
            (seg_row, (1, length), first),
            (seg_col, (length, 1), first),
        ],
        [((steps * rows, length), BF16, (rows, length), lambda i, sc: (i, 0))],
        scratch=[pltpu.VMEM((length, length), F32)],
        through=through,
    )


def product_body(at_bit, sc_ref, c0_ref, c1_ref, u0_ref, u1_ref, send_ref, keep_ref, acc_ref):
    half = acc_ref.shape[0] // 2
    acc = dot(c0_ref[...], u0_ref[...], NN) + dot(c1_ref[...], u1_ref[...], NN)
    acc_ref[...] = acc.astype(BF16)
    bit = sc_ref[at_bit]
    keep_ref[...] = acc_ref[pl.ds(pl.multiple_of(bit * half, half), half), :]
    send_ref[...] = acc_ref[pl.ds(pl.multiple_of((1 - bit) * half, half), half), :]


def product(sc, own, other, up0, up1, lay, through):
    length, width = up0.shape
    rows = lay.rows
    tile = width // 4
    out = ((rows // 2, width), BF16, (rows // 2, tile), lambda n, sc: (0, n))
    return call(
        functools.partial(product_body, lay.at_bit(0)),
        sc,
        (4,),
        [(x, (rows, length), lambda n, sc, at=at: (at, 0)) for x, at in (own, other)]
        + [(u, (length, tile), lambda n, sc: (0, n)) for u in (up0, up1)],
        [out, out],
        scratch=[pltpu.VMEM((rows, tile), BF16)],
        through=through,
    )


def combine_body(sc_ref, *refs):
    total = refs[0][...].astype(F32)
    for ref in refs[1:-1]:
        total = total + ref[...].astype(F32)
    refs[-1][...] = total.astype(BF16)


def combine(sc, terms, ring, away, lay, through):
    deep = len(terms) if away else lay.bits
    width = terms[0].shape[1]
    size = lay.rows >> deep
    ins = []

    def place(level):
        def index(n, sc):
            at = 0
            for m in range(level, deep):
                bit = sc[lay.at_bit(m)]
                at = 2 * at + (1 - bit if away and m == deep - 1 else bit)
            return (at, 0)

        return index

    for m, x in enumerate(terms):
        ins.append((x, (size, width), place(max(m, 1))))
    if ring is not None:
        ins.append((ring, (size, width), first))
    out = ((size, width), BF16, (size, width), first)
    return call(combine_body, sc, (1,), ins, [out], through=through)


def grad_context_body(sets, sc_ref, u0_ref, u1_ref, *refs):
    weights, (g0_ref, g1_ref, a0_ref, a1_ref) = refs[:-4], refs[-4:]
    n = pl.program_id(0)
    rows = a0_ref.shape[1] // len(sets)

    def add(weight_ref, cols):
        d0 = dot(u0_ref[...], weight_ref[...], NT)
        d1 = dot(u1_ref[...], weight_ref[...], NT)

        @pl.when(n == 0)
        def _():
            a0_ref[:, cols] = d0
            a1_ref[:, cols] = d1

        @pl.when(n > 0)
        def _():
            a0_ref[:, cols] += d0
            a1_ref[:, cols] += d1

    at = 0
    for index, count in enumerate(sets):
        cols = slice(index * rows, (index + 1) * rows)
        if count == 1:
            add(weights[at], cols)
        else:
            pl.when(n < 2)(functools.partial(add, weights[at], cols))
            pl.when(n >= 2)(functools.partial(add, weights[at + 1], cols))
        at += count

    @pl.when(n == 3)
    def _():
        g0_ref[...] = a0_ref[...].astype(BF16)
        g1_ref[...] = a1_ref[...].astype(BF16)


def grad_context(sc, up0, up1, weight_sets, lay, through):
    length, width = up0.shape
    rows, tile = lay.rows, width // 4
    total = rows * len(weight_sets)
    at = lay.at_piece
    ins = [(u, (length, tile), lambda n, sc: (0, sc[at + n])) for u in (up0, up1)]
    for weights in weight_sets:
        if len(weights) == 1:
            ins.append((weights[0], (rows, tile), lambda n, sc: (0, sc[at + n])))
        else:
            ins.append((weights[0], (rows, tile), lambda n, sc: (0, jnp.minimum(n, 1))))
            ins.append((weights[1], (rows, tile), lambda n, sc: (0, jnp.maximum(n - 2, 0))))
    return call(
        functools.partial(grad_context_body, [len(w) for w in weight_sets]),
        sc,
        (4,),
        ins,
        [((length, total), BF16, (length, total), first)] * 2,
        scratch=[pltpu.VMEM((length, total), F32)] * 2,
        through=through,
        mib=28,
    )


def backward_body(
    per, sc_ref, q_ref, k_ref, v_ref, seg_row_ref, seg_col_ref, own_ref, other_ref, *refs
):
    gq_ref, gk_ref, gv_ref, mask_ref, ak_ref, av_ref = refs[-6:]
    group = pl.program_id(0)
    parity = sc_ref[0]

    @pl.when(group == 0)
    def _():
        fill_mask(mask_ref, seg_row_ref, seg_col_ref)

    key_t = k_ref[...].T
    ak_ref[...] = jnp.zeros_like(ak_ref)
    av_ref[...] = jnp.zeros_like(av_ref)
    for h in range(REPEAT):
        side = group if per == REPEAT else h
        column = h if per == REPEAT else 0
        cols = slice(column * DH, (column + 1) * DH)
        grad = jnp.where(side == parity, own_ref[:, cols], other_ref[:, cols])
        for start, tile, upto in tiles_of(q_ref.shape[0]):
            query = q_ref[start : start + tile, h * DH : (h + 1) * DH]
            probs, cap_tanh = softmax_tile(
                k_ref[:upto, :], query, mask_ref[:upto, start : start + tile]
            )
            grad_rows = grad[start : start + tile, :]
            grad_probs = dot(v_ref[:upto, :], grad_rows, NT)
            delta = jnp.sum(probs * grad_probs, axis=0, keepdims=True)
            scores = probs * (grad_probs - delta) * (SCALE - SCALE * (cap_tanh * cap_tanh))
            scores = scores.astype(BF16)
            av_ref[:upto, :] += dot(probs.astype(BF16), grad_rows, NN)
            ak_ref[:upto, :] += dot(scores, query, NN)
            grad_query = dot(key_t[:, :upto], scores, NN).T
            gq_ref[start : start + tile, h * DH : (h + 1) * DH] = grad_query.astype(BF16)
    gk_ref[...] = ak_ref[...].astype(BF16)
    gv_ref[...] = av_ref[...].astype(BF16)


def backward(sc, k, block, own, other, column, before, lay, through):
    queries, keys, values, seg_row, seg_col = block
    length = queries.shape[0]
    per = lay.heads_shard
    groups = 2 * per // REPEAT
    at = lay.at_z + k

    def whole(i, sc):
        return (0, sc[at] * groups + i)

    heads = (length, REPEAT * DH), whole
    one = (length, DH), whole
    return call(
        functools.partial(backward_body, per),
        sc,
        (groups,),
        [
            (queries, *heads),
            (keys, *one),
            (values, *one),
            (seg_row, (1, length), first),
            (seg_col, (length, 1), first),
            (own, (length, lay.rows), lambda i, sc: (0, column)),
            (other, (length, lay.rows), lambda i, sc: (0, column)),
        ],
        [(queries.shape, BF16, *heads), (keys.shape, BF16, *one), (values.shape, BF16, *one)],
        scratch=[
            pltpu.VMEM((length, length), F32),
            pltpu.VMEM((length, DH), F32),
            pltpu.VMEM((length, DH), F32),
        ],
        before=before,
        through=through,
    )


def adam_body(pieces, tokens, sc_ref, m1_ref, m2_ref, *refs):
    out_ref = refs[-1]
    n = pl.program_id(0)

    def step(piece_ref):
        gradient = piece_ref[...].astype(F32) * (1.0 / tokens)
        moment_one = 0.9 * m1_ref[...] + 0.1 * gradient
        moment_two = 0.95 * m2_ref[...] + 0.05 * gradient * gradient
        out_ref[...] = moment_one / (jnp.sqrt(moment_two) + 1e-08)

    for p in range(pieces):
        pl.when(n == p)(functools.partial(step, refs[p]))


def adam(sc, pieces, first_moment, second_moment, tokens, lay, before, through):
    rows, width = pieces[0][0].shape
    count = len(pieces)
    columns = [lay.at_place(flips) for _, flips in pieces]

    def at(n, m, sc):
        row = sc[columns[0]]
        for p in range(1, count):
            row = jnp.where(n == p, sc[columns[p]], row)
        return (row, m)

    def of(p):
        return lambda n, m, sc: (0, jnp.where(n == p, m, jnp.where(n < p, 0, 1)))

    block = (rows, width // 2)
    return call(
        functools.partial(adam_body, count, tokens),
        sc,
        (count, 2),
        [(first_moment, block, at), (second_moment, block, at)]
        + [(x, block, of(p)) for p, (x, _) in enumerate(pieces)],
        [(first_moment.shape, F32, block, at)],
        before=before,
        through=through,
        mib=60,
    )


class Layout:
    def __init__(self, replicas, shards, rows):
        self.replicas, self.shards, self.rows = replicas, shards, rows
        self.z = shards // 2
        self.bits = replicas.bit_length() - 1
        self.heads_shard = HEADS // shards
        self.order = [0] + list(range(1, self.z, 2)) + list(range(self.z - 2, 0, -2))
        self.place = [self.order.index(z) for z in range(self.z)]
        self.at_z = 1
        self.at_piece = self.at_z + self.z
        table = []
        for r in range(replicas):
            for s in range(shards):
                z, core = s // 2, s % 2
                zs = [self.order[(self.place[z] - k) % self.z] for k in range(self.z)]
                bits = [(r >> self.bit_of(core, n)) & 1 for n in range(self.bits)]
                b = 2 * bits[0]
                here = sum(bit << n for n, bit in enumerate(bits[::-1]))
                places = [here ^ flips for flips in range(replicas)]
                table.append([core] + zs + [b, b + 1, 2 - b, 3 - b] + bits + places)
        self.table = np.array(table, np.int32)

    def bit_of(self, core, n):
        return self.bits - 1 - n if core else n

    def at_bit(self, n):
        return self.at_piece + 4 + n

    def at_place(self, flips):
        code = sum(int(f) << n for n, f in enumerate(flips[::-1]))
        return self.at_piece + 4 + self.bits + code

    def sibling(self, x):
        return lax.ppermute(x, "shard", [(s, s ^ 1) for s in range(self.shards)])

    def onward(self, x):
        perm = []
        for p in range(self.z):
            a, b = self.order[p], self.order[(p + 1) % self.z]
            perm += [(2 * a + core, 2 * b + core) for core in range(2)]
        return lax.ppermute(x, "shard", perm)

    def across(self, x, n):
        perm = []
        for r in range(self.replicas):
            for s in range(self.shards):
                partner = r ^ (1 << self.bit_of(s % 2, n))
                perm.append((r * self.shards + s, partner * self.shards + s))
        return lax.ppermute(x, ("replica", "shard"), perm)


def per_device(queries, keys, values, segments, out_weight, upstream, first_moment, second_moment):
    length, width = upstream.shape
    lay = Layout(lax.axis_size("replica"), lax.axis_size("shard"), out_weight.shape[0])
    tokens = length * lay.replicas * lay.shards
    device = lax.axis_index("replica") * lay.shards + lax.axis_index("shard")
    sc = lax.dynamic_index_in_dim(jnp.asarray(lay.table), device, 0, keepdims=False)
    block = (queries, keys, values, segments, segments.reshape(length, 1))

    box = {}
    terms = {}
    gc = {}
    grads = ()

    def run(function, *args, held=(), **more):
        names = ["token", *held]
        outs, handed = function(*args, through=[box[n] for n in names], **more)
        box.update(zip(names, handed))
        return outs

    def do_product(k, held=()):
        own, other = contexts[k]
        box["send", k], keep = run(
            product, sc, own, other, upstream, upstream_other, lay, held=held
        )
        terms[k] = [keep]

    def send(k):
        terms[k].append(lay.across(box["send", k], len(terms[k]) - 1))

    def do_halve(k, held=()):
        for stage in range(1, lay.bits):
            (box["send", k],) = run(combine, sc, terms[k], None, True, lay, held=held)
            held = ()
            if stage < lay.bits - 1:
                send(k)

    def do_sum(k, held=()):
        (box["sum", k],) = run(combine, sc, terms[k], box.get(("part", k)), False, lay, held=held)

    def pass_sum(k):
        box["part", (k + 1) % lay.z] = lay.onward(box["sum", k])

    def pass_weights(k):
        if k + 1 < lay.z:
            box["ring", k + 1] = lay.onward(box["ring", k])

    def cross_weights(k):
        box["cross", k] = lay.across(box["ring", k], 0)

    def do_grad_context(ks, held=()):
        sets = [[box["ring", k], box["cross", k]] if k else [out_weight] for k in ks]
        own, box["away", ks[0]] = run(
            grad_context, sc, upstream, upstream_other, sets, lay, held=held
        )
        for n, k in enumerate(ks):
            gc[k] = own, ks[0], n

    def swap_grad_context(k):
        box["gc", k] = lay.sibling(box["away", k])

    def do_backward(k, held=()):
        nonlocal grads
        own, base, column = gc[k]
        grads = run(backward, sc, k, block, own, box["gc", base], column, grads, lay, held=held)

    upstream_other = lay.sibling(upstream)
    box["ring", 1], box["token"] = cut(sc, out_weight, lay)[0]
    box["ring", 1] = lay.onward(box["ring", 1])

    late = [*range(2, lay.z), 0]
    rows = lay.rows
    contexts = {}
    (both_sides,) = run(forward, sc, [1], [0, 1], block, lay)
    contexts[1] = (both_sides, 1), (lay.sibling(both_sides[:rows]), 0)
    do_product(1)
    send(1)
    (both_sides,) = run(forward, sc, late, [0, 1], block, lay)
    box["context"] = lay.sibling(both_sides[: len(late) * rows])
    do_halve(1, held=[("ring", 1), "context"])
    send(1)
    pass_weights(1)
    cross_weights(1)
    for n, k in enumerate(late):
        contexts[k] = (both_sides, len(late) + n), (box["context"], n)
    do_product(2)
    do_sum(1)
    pass_sum(1)
    send(2)
    do_product(3)
    send(3)
    do_grad_context([0, 1])
    swap_grad_context(0)
    run(relay, sc, held=[("ring", 2)])
    pass_weights(2)
    cross_weights(2)
    do_halve(2)
    send(2)
    do_backward(0)
    do_product(0)
    do_halve(3)
    send(3)
    do_backward(1, held=[("send", 0)])
    send(0)
    do_sum(2)
    pass_sum(2)
    for k in range(4, lay.z):
        do_product(k, held=[("ring", k - 1)])
        pass_weights(k - 1)
        cross_weights(k - 1)
        send(k)
        do_halve(k)
        send(k)
    last = lay.z - 1
    do_grad_context([2])
    swap_grad_context(2)
    run(relay, sc, held=[("ring", last)])
    cross_weights(last)
    do_backward(2)
    do_halve(0)
    send(0)
    do_sum(3)
    pass_sum(3)
    for k in range(4, lay.z):
        do_sum(k)
        pass_sum(k)
    for k in range(3, last):
        do_grad_context([k])
        swap_grad_context(k)
        do_backward(k)
    do_grad_context([last])
    swap_grad_context(last)
    do_sum(0)

    have = [(box["sum", 0], (False,) * lay.bits)]

    def spread(n, piece):
        x, flips = piece
        return lay.across(x, n), flips[:n] + (True,) + flips[n + 1 :]

    moments = first_moment, second_moment, tokens, lay
    direct = [spread(n, have[0]) for n in range(lay.bits - 1, -1, -1)]
    do_backward(last)
    step = run(adam, sc, have, *moments, before=())
    box["got"] = direct[0][0]
    run(relay, sc, held=["got"])
    direct[0] = (box["got"], direct[0][1])
    near = [have[0], *direct]
    have = [have[0], direct[0]]
    done = {flips for _, flips in near}
    far = []
    for n in range(lay.bits - 2, -1, -1):
        more = []
        for x, flips in have:
            flips = flips[:n] + (True,) + flips[n + 1 :]
            if flips in done:
                more += [p for p in near if p[1] == flips]
            else:
                more.append((lay.across(x, n), flips))
                far.append(more[-1])
        have += more
    step = run(adam, sc, direct, *moments, before=step)
    step = run(adam, sc, far, *moments, before=step)
    return (*grads, *step)


def solution(mesh):
    both = P(("replica", "shard"), None)
    shard = P("shard", None)
    return jax.shard_map(
        per_device,
        mesh=mesh,
        in_specs=(both, both, both, both, shard, both, shard, shard),
        out_specs=(both, both, both, shard),
        check_vma=False,
    )
```

```python
import functools

import jax
import jax.numpy as jnp
import numpy as np
from jax import lax
from jax.experimental import pallas as pl
from jax.experimental.pallas import tpu as pltpu
from jax.sharding import PartitionSpec as P

HEADS = 16
KV_HEADS = 8
DH = 128
REPEAT = HEADS // KV_HEADS

SCALE = 1.0 / 12.0
CAP = 50.0
MIB = 1024 * 1024
F32 = jnp.float32
BF16 = jnp.bfloat16

NT = (((1,), (1,)), ((), ()))
NN = (((1,), (0,)), ((), ()))


def dot(a, b, dims):
    return lax.dot_general(a, b, dims, preferred_element_type=F32)


def call(body, sc, grid, ins, outs, scratch=(), through=(), before=(), mib=20):
    n_in, n_out, n_before, n_through = len(ins), len(outs), len(before), len(through)

    def kernel(sc_ref, *refs):
        at = n_in + n_before + n_through
        body(sc_ref, *refs[:n_in], *refs[at : at + n_out], *refs[at + n_out + n_through :])

    anywhere = pl.BlockSpec(memory_space=pl.ANY)
    stay = pl.BlockSpec(memory_space=pltpu.HBM)
    aliases = {1 + n_in + n: n for n in range(n_before)}
    aliases.update({1 + n_in + n_before + n: n_out + n for n in range(n_through)})
    results = pl.pallas_call(
        kernel,
        grid_spec=pltpu.PrefetchScalarGridSpec(
            num_scalar_prefetch=1,
            grid=grid,
            in_specs=[pl.BlockSpec(block, index) for _, block, index in ins]
            + [anywhere] * n_before
            + [stay] * n_through,
            out_specs=[pl.BlockSpec(block, index) for _, _, block, index in outs]
            + [stay] * n_through,
            scratch_shapes=list(scratch),
        ),
        out_shape=[jax.ShapeDtypeStruct(shape, dtype) for shape, dtype, _, _ in outs]
        + [jax.ShapeDtypeStruct(x.shape, x.dtype) for x in through],
        input_output_aliases=aliases,
        cost_estimate=pl.CostEstimate(flops=1, transcendentals=0, bytes_accessed=1),
        compiler_params=pltpu.CompilerParams(vmem_limit_bytes=mib * MIB),
    )(sc, *[array for array, _, _ in ins], *before, *through)
    return results[:n_out], results[n_out:]


def first(*_):
    return (0, 0)


def fill_mask(mask_ref, seg_row_ref, seg_col_ref):
    length = mask_ref.shape[0]
    j = lax.broadcasted_iota(jnp.int32, (length, length), 0)
    i = lax.broadcasted_iota(jnp.int32, (length, length), 1)
    allowed = (j <= i) & (seg_col_ref[...] == seg_row_ref[...])
    mask_ref[...] = jnp.where(allowed, 1.0, 0.0).astype(F32)


def tiles_of(length):
    tile = 256
    return [(t * tile, tile, (t + 1) * tile) for t in range(length // tile)]


def softmax_tile(key, query, mask):
    cap_tanh = jnp.tanh(dot(key, query, NT) * (SCALE / CAP))
    weights = jnp.exp(cap_tanh * CAP) * mask
    inverse = 1.0 / jnp.sum(weights, axis=0, keepdims=True)
    return weights * inverse, cap_tanh


def cut_body(sc_ref, in_ref, out_ref, token_ref):
    out_ref[...] = in_ref[...]
    token_ref[...] = jnp.zeros_like(token_ref)


def cut(sc, weight, lay):
    block = (weight.shape[0], weight.shape[1] // 2)
    return call(
        cut_body,
        sc,
        (1,),
        [(weight, block, lambda n, sc: (0, sc[lay.at_bit(0)]))],
        [(block, BF16, block, first), ((8, 128), F32, (8, 128), first)],
    )


def relay_body(sc_ref):
    pass


def relay(sc, through):
    return call(relay_body, sc, (1,), [], [], through=through)


def forward_body(heads, sc_ref, q_ref, k_ref, v_ref, seg_row_ref, seg_col_ref, out_ref, mask_ref):
    @pl.when(pl.program_id(0) == 0)
    def _():
        fill_mask(mask_ref, seg_row_ref, seg_col_ref)

    value_t = v_ref[...].T
    for h in range(heads):
        for start, tile, upto in tiles_of(q_ref.shape[0]):
            probs, _ = softmax_tile(
                k_ref[:upto, :],
                q_ref[start : start + tile, h * DH : (h + 1) * DH],
                mask_ref[:upto, start : start + tile],
            )
            context = dot(value_t[:, :upto], probs.astype(BF16), NN)
            out_ref[h * DH : (h + 1) * DH, start : start + tile] = context.astype(BF16)


def forward(sc, ks, sides, block, lay, through):
    queries, keys, values, seg_row, seg_col = block
    length = queries.shape[0]
    per = lay.heads_shard
    count = len(ks)

    def shard_of(i, sc):
        k = lax.rem(ks[0] + lax.rem(i, count), lay.z)
        if len(sides) == 2:
            own = i >= count
        else:
            own = sides[0] == 1
        return 2 * sc[lay.at_z + k] + jnp.where(own, sc[0], 1 - sc[0])

    def kv_of(i, sc):
        return (0, (shard_of(i, sc) * per) // REPEAT)

    rows = per * DH
    steps = count * len(sides)
    return call(
        functools.partial(forward_body, per),
        sc,
        (steps,),
        [
            (queries, (length, rows), lambda i, sc: (0, shard_of(i, sc))),
            (keys, (length, DH), kv_of),
            (values, (length, DH), kv_of),
            (seg_row, (1, length), first),
            (seg_col, (length, 1), first),
        ],
        [((steps * rows, length), BF16, (rows, length), lambda i, sc: (i, 0))],
        scratch=[pltpu.VMEM((length, length), F32)],
        through=through,
    )


def product_body(at_bit, sc_ref, c0_ref, c1_ref, u0_ref, u1_ref, send_ref, keep_ref, acc_ref):
    half = acc_ref.shape[0] // 2
    acc = dot(c0_ref[...], u0_ref[...], NN) + dot(c1_ref[...], u1_ref[...], NN)
    acc_ref[...] = acc.astype(BF16)
    bit = sc_ref[at_bit]
    keep_ref[...] = acc_ref[pl.ds(pl.multiple_of(bit * half, half), half), :]
    send_ref[...] = acc_ref[pl.ds(pl.multiple_of((1 - bit) * half, half), half), :]


def product(sc, own, other, up0, up1, lay, through):
    length, width = up0.shape
    rows = lay.rows
    tile = width // 4
    out = ((rows // 2, width), BF16, (rows // 2, tile), lambda n, sc: (0, n))
    return call(
        functools.partial(product_body, lay.at_bit(0)),
        sc,
        (4,),
        [(x, (rows, length), lambda n, sc, at=at: (at, 0)) for x, at in (own, other)]
        + [(u, (length, tile), lambda n, sc: (0, n)) for u in (up0, up1)],
        [out, out],
        scratch=[pltpu.VMEM((rows, tile), BF16)],
        through=through,
    )


def combine_body(sc_ref, *refs):
    total = refs[0][...].astype(F32)
    for ref in refs[1:-1]:
        total = total + ref[...].astype(F32)
    refs[-1][...] = total.astype(BF16)


def combine(sc, terms, ring, away, lay, through):
    deep = len(terms) if away else lay.bits
    width = terms[0].shape[1]
    size = lay.rows >> deep
    ins = []

    def place(level):
        def index(n, sc):
            at = 0
            for m in range(level, deep):
                bit = sc[lay.at_bit(m)]
                at = 2 * at + (1 - bit if away and m == deep - 1 else bit)
            return (at, 0)

        return index

    for m, x in enumerate(terms):
        ins.append((x, (size, width), place(max(m, 1))))
    if ring is not None:
        ins.append((ring, (size, width), first))
    out = ((size, width), BF16, (size, width), first)
    return call(combine_body, sc, (1,), ins, [out], through=through)


def grad_context_body(sets, sc_ref, u0_ref, u1_ref, *refs):
    weights, (g0_ref, g1_ref, a0_ref, a1_ref) = refs[:-4], refs[-4:]
    n = pl.program_id(0)
    rows = a0_ref.shape[1] // len(sets)

    def add(weight_ref, cols):
        d0 = dot(u0_ref[...], weight_ref[...], NT)
        d1 = dot(u1_ref[...], weight_ref[...], NT)

        @pl.when(n == 0)
        def _():
            a0_ref[:, cols] = d0
            a1_ref[:, cols] = d1

        @pl.when(n > 0)
        def _():
            a0_ref[:, cols] += d0
            a1_ref[:, cols] += d1

    at = 0
    for index, count in enumerate(sets):
        cols = slice(index * rows, (index + 1) * rows)
        if count == 1:
            add(weights[at], cols)
        else:
            pl.when(n < 2)(functools.partial(add, weights[at], cols))
            pl.when(n >= 2)(functools.partial(add, weights[at + 1], cols))
        at += count

    @pl.when(n == 3)
    def _():
        g0_ref[...] = a0_ref[...].astype(BF16)
        g1_ref[...] = a1_ref[...].astype(BF16)


def grad_context(sc, up0, up1, weight_sets, lay, through):
    length, width = up0.shape
    rows, tile = lay.rows, width // 4
    total = rows * len(weight_sets)
    at = lay.at_piece
    ins = [(u, (length, tile), lambda n, sc: (0, sc[at + n])) for u in (up0, up1)]
    for weights in weight_sets:
        if len(weights) == 1:
            ins.append((weights[0], (rows, tile), lambda n, sc: (0, sc[at + n])))
        else:
            ins.append((weights[0], (rows, tile), lambda n, sc: (0, jnp.minimum(n, 1))))
            ins.append((weights[1], (rows, tile), lambda n, sc: (0, jnp.maximum(n - 2, 0))))
    return call(
        functools.partial(grad_context_body, [len(w) for w in weight_sets]),
        sc,
        (4,),
        ins,
        [((length, total), BF16, (length, total), first)] * 2,
        scratch=[pltpu.VMEM((length, total), F32)] * 2,
        through=through,
        mib=28,
    )


def backward_body(
    per, sc_ref, q_ref, k_ref, v_ref, seg_row_ref, seg_col_ref, own_ref, other_ref, *refs
):
    gq_ref, gk_ref, gv_ref, mask_ref, ak_ref, av_ref = refs[-6:]
    group = pl.program_id(0)
    parity = sc_ref[0]

    @pl.when(group == 0)
    def _():
        fill_mask(mask_ref, seg_row_ref, seg_col_ref)

    key_t = k_ref[...].T
    ak_ref[...] = jnp.zeros_like(ak_ref)
    av_ref[...] = jnp.zeros_like(av_ref)
    for h in range(REPEAT):
        side = group if per == REPEAT else h
        column = h if per == REPEAT else 0
        cols = slice(column * DH, (column + 1) * DH)
        grad = jnp.where(side == parity, own_ref[:, cols], other_ref[:, cols])
        for start, tile, upto in tiles_of(q_ref.shape[0]):
            query = q_ref[start : start + tile, h * DH : (h + 1) * DH]
            probs, cap_tanh = softmax_tile(
                k_ref[:upto, :], query, mask_ref[:upto, start : start + tile]
            )
            grad_rows = grad[start : start + tile, :]
            grad_probs = dot(v_ref[:upto, :], grad_rows, NT)
            delta = jnp.sum(probs * grad_probs, axis=0, keepdims=True)
            scores = probs * (grad_probs - delta) * (SCALE - SCALE * (cap_tanh * cap_tanh))
            scores = scores.astype(BF16)
            av_ref[:upto, :] += dot(probs.astype(BF16), grad_rows, NN)
            ak_ref[:upto, :] += dot(scores, query, NN)
            grad_query = dot(key_t[:, :upto], scores, NN).T
            gq_ref[start : start + tile, h * DH : (h + 1) * DH] = grad_query.astype(BF16)
    gk_ref[...] = ak_ref[...].astype(BF16)
    gv_ref[...] = av_ref[...].astype(BF16)


def backward(sc, k, block, own, other, column, before, lay, through):
    queries, keys, values, seg_row, seg_col = block
    length = queries.shape[0]
    per = lay.heads_shard
    groups = 2 * per // REPEAT
    at = lay.at_z + k

    def whole(i, sc):
        return (0, sc[at] * groups + i)

    heads = (length, REPEAT * DH), whole
    one = (length, DH), whole
    return call(
        functools.partial(backward_body, per),
        sc,
        (groups,),
        [
            (queries, *heads),
            (keys, *one),
            (values, *one),
            (seg_row, (1, length), first),
            (seg_col, (length, 1), first),
            (own, (length, lay.rows), lambda i, sc: (0, column)),
            (other, (length, lay.rows), lambda i, sc: (0, column)),
        ],
        [(queries.shape, BF16, *heads), (keys.shape, BF16, *one), (values.shape, BF16, *one)],
        scratch=[
            pltpu.VMEM((length, length), F32),
            pltpu.VMEM((length, DH), F32),
            pltpu.VMEM((length, DH), F32),
        ],
        before=before,
        through=through,
    )


def adam_body(pieces, tokens, sc_ref, m1_ref, m2_ref, *refs):
    out_ref = refs[-1]
    n = pl.program_id(0)

    def step(piece_ref):
        gradient = piece_ref[...].astype(F32) * (1.0 / tokens)
        moment_one = 0.9 * m1_ref[...] + 0.1 * gradient
        moment_two = 0.95 * m2_ref[...] + 0.05 * gradient * gradient
        out_ref[...] = moment_one / (jnp.sqrt(moment_two) + 1e-08)

    for p in range(pieces):
        pl.when(n == p)(functools.partial(step, refs[p]))


def adam(sc, pieces, first_moment, second_moment, tokens, lay, before, through):
    rows, width = pieces[0][0].shape
    count = len(pieces)
    columns = [lay.at_place(flips) for _, flips in pieces]

    def at(n, m, sc):
        row = sc[columns[0]]
        for p in range(1, count):
            row = jnp.where(n == p, sc[columns[p]], row)
        return (row, m)

    def of(p):
        return lambda n, m, sc: (0, jnp.where(n == p, m, jnp.where(n < p, 0, 1)))

    block = (rows, width // 2)
    return call(
        functools.partial(adam_body, count, tokens),
        sc,
        (count, 2),
        [(first_moment, block, at), (second_moment, block, at)]
        + [(x, block, of(p)) for p, (x, _) in enumerate(pieces)],
        [(first_moment.shape, F32, block, at)],
        before=before,
        through=through,
        mib=60,
    )


class Layout:
    def __init__(self, replicas, shards, rows):
        self.replicas, self.shards, self.rows = replicas, shards, rows
        self.z = shards // 2
        self.bits = replicas.bit_length() - 1
        self.heads_shard = HEADS // shards
        self.order = [0] + list(range(1, self.z, 2)) + list(range(self.z - 2, 0, -2))
        self.place = [self.order.index(z) for z in range(self.z)]
        self.at_z = 1
        self.at_piece = self.at_z + self.z
        table = []
        for r in range(replicas):
            for s in range(shards):
                z, core = s // 2, s % 2
                zs = [self.order[(self.place[z] - k) % self.z] for k in range(self.z)]
                bits = [(r >> self.bit_of(core, n)) & 1 for n in range(self.bits)]
                b = 2 * bits[0]
                here = sum(bit << n for n, bit in enumerate(bits[::-1]))
                places = [here ^ flips for flips in range(replicas)]
                table.append([core] + zs + [b, b + 1, 2 - b, 3 - b] + bits + places)
        self.table = np.array(table, np.int32)

    def bit_of(self, core, n):
        return self.bits - 1 - n if core else n

    def at_bit(self, n):
        return self.at_piece + 4 + n

    def at_place(self, flips):
        code = sum(int(f) << n for n, f in enumerate(flips[::-1]))
        return self.at_piece + 4 + self.bits + code

    def sibling(self, x):
        return lax.ppermute(x, "shard", [(s, s ^ 1) for s in range(self.shards)])

    def onward(self, x):
        perm = []
        for p in range(self.z):
            a, b = self.order[p], self.order[(p + 1) % self.z]
            perm += [(2 * a + core, 2 * b + core) for core in range(2)]
        return lax.ppermute(x, "shard", perm)

    def across(self, x, n):
        perm = []
        for r in range(self.replicas):
            for s in range(self.shards):
                partner = r ^ (1 << self.bit_of(s % 2, n))
                perm.append((r * self.shards + s, partner * self.shards + s))
        return lax.ppermute(x, ("replica", "shard"), perm)


def per_device(queries, keys, values, segments, out_weight, upstream, first_moment, second_moment):
    length, width = upstream.shape
    lay = Layout(lax.axis_size("replica"), lax.axis_size("shard"), out_weight.shape[0])
    tokens = length * lay.replicas * lay.shards
    device = lax.axis_index("replica") * lay.shards + lax.axis_index("shard")
    sc = lax.dynamic_index_in_dim(jnp.asarray(lay.table), device, 0, keepdims=False)
    block = (queries, keys, values, segments, segments.reshape(length, 1))

    box = {}
    terms = {}
    gc = {}
    grads = ()

    def run(function, *args, held=(), **more):
        names = ["token", *held]
        outs, handed = function(*args, through=[box[n] for n in names], **more)
        box.update(zip(names, handed))
        return outs

    def do_product(k, held=()):
        own, other = contexts[k]
        box["send", k], keep = run(
            product, sc, own, other, upstream, upstream_other, lay, held=held
        )
        terms[k] = [keep]

    def send(k):
        terms[k].append(lay.across(box["send", k], len(terms[k]) - 1))

    def do_halve(k, held=()):
        for stage in range(1, lay.bits):
            (box["send", k],) = run(combine, sc, terms[k], None, True, lay, held=held)
            held = ()
            if stage < lay.bits - 1:
                send(k)

    def do_sum(k, held=()):
        (box["sum", k],) = run(combine, sc, terms[k], box.get(("part", k)), False, lay, held=held)

    def pass_sum(k):
        box["part", (k + 1) % lay.z] = lay.onward(box["sum", k])

    def pass_weights(k):
        if k + 1 < lay.z:
            box["ring", k + 1] = lay.onward(box["ring", k])

    def cross_weights(k):
        box["cross", k] = lay.across(box["ring", k], 0)

    def do_grad_context(ks, held=()):
        sets = [[box["ring", k], box["cross", k]] if k else [out_weight] for k in ks]
        own, box["away", ks[0]] = run(
            grad_context, sc, upstream, upstream_other, sets, lay, held=held
        )
        for n, k in enumerate(ks):
            gc[k] = own, ks[0], n

    def swap_grad_context(k):
        box["gc", k] = lay.sibling(box["away", k])

    def do_backward(k, held=()):
        nonlocal grads
        own, base, column = gc[k]
        grads = run(backward, sc, k, block, own, box["gc", base], column, grads, lay, held=held)

    upstream_other = lay.sibling(upstream)
    box["ring", 1], box["token"] = cut(sc, out_weight, lay)[0]
    box["ring", 1] = lay.onward(box["ring", 1])

    late = [*range(2, lay.z), 0]
    rows = lay.rows
    contexts = {}
    (both_sides,) = run(forward, sc, [1], [0, 1], block, lay)
    contexts[1] = (both_sides, 1), (lay.sibling(both_sides[:rows]), 0)
    do_product(1)
    send(1)
    (both_sides,) = run(forward, sc, late, [0, 1], block, lay)
    box["context"] = lay.sibling(both_sides[: len(late) * rows])
    do_halve(1, held=[("ring", 1), "context"])
    send(1)
    pass_weights(1)
    cross_weights(1)
    for n, k in enumerate(late):
        contexts[k] = (both_sides, len(late) + n), (box["context"], n)
    do_product(2)
    do_sum(1)
    pass_sum(1)
    send(2)
    do_product(3)
    send(3)
    do_grad_context([0, 1])
    swap_grad_context(0)
    run(relay, sc, held=[("ring", 2)])
    pass_weights(2)
    cross_weights(2)
    do_halve(2)
    send(2)
    do_backward(0)
    do_product(0)
    do_halve(3)
    send(3)
    do_backward(1, held=[("send", 0)])
    send(0)
    for k in range(4, lay.z):
        do_product(k, held=[("ring", k - 1)])
        pass_weights(k - 1)
        cross_weights(k - 1)
        send(k)
        do_halve(k)
        send(k)
    last = lay.z - 1
    do_grad_context([2])
    swap_grad_context(2)
    do_sum(2, held=[("ring", last)])
    pass_sum(2)
    cross_weights(last)
    do_backward(2)
    do_halve(0)
    send(0)
    do_sum(3)
    pass_sum(3)
    for k in range(4, lay.z):
        do_sum(k)
        pass_sum(k)
    for k in range(3, last):
        do_grad_context([k])
        swap_grad_context(k)
        do_backward(k)
    do_grad_context([last])
    swap_grad_context(last)
    do_sum(0)

    have = [(box["sum", 0], (False,) * lay.bits)]

    def spread(n, piece):
        x, flips = piece
        return lay.across(x, n), flips[:n] + (True,) + flips[n + 1 :]

    moments = first_moment, second_moment, tokens, lay
    direct = [spread(n, have[0]) for n in range(lay.bits - 1, -1, -1)]
    do_backward(last)
    step = run(adam, sc, have, *moments, before=())
    box["got"] = direct[0][0]
    run(relay, sc, held=["got"])
    direct[0] = (box["got"], direct[0][1])
    near = [have[0], *direct]
    have = [have[0], direct[0]]
    done = {flips for _, flips in near}
    far = []
    for n in range(lay.bits - 2, -1, -1):
        more = []
        for x, flips in have:
            flips = flips[:n] + (True,) + flips[n + 1 :]
            if flips in done:
                more += [p for p in near if p[1] == flips]
            else:
                more.append((lay.across(x, n), flips))
                far.append(more[-1])
        have += more
    step = run(adam, sc, direct, *moments, before=step)
    step = run(adam, sc, far, *moments, before=step)
    return (*grads, *step)


def solution(mesh):
    both = P(("replica", "shard"), None)
    shard = P("shard", None)
    return jax.shard_map(
        per_device,
        mesh=mesh,
        in_specs=(both, both, both, both, shard, both, shard, shard),
        out_specs=(both, both, both, shard),
        check_vma=False,
    )
```
